256 devices in a mesh: grp: 4 (over z_hi), tp: 64 (over x, z_lo, y, core).
Axes of the slice: x: 4, y: 4, z: 8 (z_hi: 4, z_lo: 2; z = z_hi * 2 + z_lo), core: 2. Of those that a mesh axis runs over, the one named last changes fastest.
Arguments:
- hidden: bfloat16 [4, 256, 8192], P('grp', None, 'tp'), may hold values from -6 to 6
- lengths: int32 [4], P('grp'), may hold values from 64 to 256, as said below
- norm_gain: float32 [2, 8192], P(None, 'tp'), may hold values from 0.1 to 1.9
- q_weight: bfloat16 [2, 64, 128, 8192], P(None, None, 'grp', 'tp'), may hold values from -0.0625 to 0.0625
- q_bias: bfloat16 [2, 8192], P(None, 'tp'), may hold values from -3 to 3
- kv_weight: bfloat16 [2, 64, 128, 2048], P(None, None, 'grp', 'tp'), may hold values from -0.0625 to 0.0625
- kv_bias: bfloat16 [2, 2048], P(None, 'tp'), may hold values from -111 to 111
- out_weight: bfloat16 [2, 64, 128, 8192], P(None, None, 'grp', 'tp'), may hold values from -0.0625 to 0.0625
Outputs:
- final_hidden: bfloat16 [4, 256, 8192], P('grp', None, 'tp')
The draws below stay inside these ranges and needn't reach their ends.
Inputs may be any that keep to these rules, and one draw needn't show every extreme that they name: `lengths`: at least one prompt has exactly 256 live tokens.
All inputs are finite; a program needn't handle non-finite values.
Results may differ from the reference program's by a relative error of at most 0.017.
The reference program's roundings to bfloat16 on the way count: a program that leaves them out, or rounds other values in their place, can miss the bound.
Values may be sent and summed in bfloat16 or wider, within the bound.
No kernel may reach another device: no remote copies, remote signals or barrier semaphores. Data moves between devices by JAX's collectives and lax.ppermute only.
A program may use at most 64 MiB of HBM per device.

```python
import jax
import jax.numpy as jnp
from jax import lax

D = 8192
HD = 128
KVH = 8
LAYERS = 2
TOK = 256
PROMPTS = 4
NBLOCK = 64
BLOCK_FEAT = 128


def draw_lengths(key, part):
    key = jax.random.fold_in(key, 7)
    first, second = jax.random.split(key)
    base = jax.random.randint(first, (PROMPTS,), TOK // 4, TOK + 1)
    chosen = jax.random.randint(second, (), 0, PROMPTS)
    return jnp.where(jnp.arange(PROMPTS) == chosen, TOK, base).astype(jnp.int32)


def draw_kv_bias(key, part):
    key = jax.random.fold_in(key, 11)
    base_key = jax.random.fold_in(key, 0)
    columns = 2 * KVH * HD
    values = 0.5 * jnp.clip(jax.random.normal(base_key, (LAYERS, columns), jnp.float32), -6.0, 6.0)
    return values.astype(jnp.bfloat16)


def level_of(own_key, shape, shards, smallest, largest):
    loudness, own = 1.0, jax.random.fold_in(own_key, 6)
    for position, parts in shards:
        heights = jnp.exp(jax.random.uniform(jax.random.fold_in(own, position), (parts,), jnp.float32, smallest / len(shards), largest / len(shards)))
        loudness = loudness * jnp.repeat(heights, shape[position] // parts).reshape([-1 if axis == position else 1 for axis in range(len(shape))])
    return loudness


def centred(own_key, dims, scale, bound, shards=(), held_as=jnp.bfloat16):
    values = scale * jax.random.normal(own_key, dims, jnp.float32)
    if shards:
        values = values * level_of(own_key, dims, shards, -0.22, 0.18)
    return jnp.clip(values, -bound, bound).astype(held_as)


def setup_inputs(seed: int = 0) -> dict:
    seeds = jax.random.split(jax.random.key(seed), 9)
    hidden = centred(seeds[0], (PROMPTS, TOK, D), 1.0, 6.0, ((0, 4), (2, 64)))
    lengths = draw_lengths(jax.random.fold_in(seeds[8], 71), 0)
    norm_gain = jnp.clip(1.0 + 0.18 * jax.random.normal(seeds[2], (LAYERS, D), jnp.float32), 0.1, 1.9)
    q_weight = centred(seeds[3], (LAYERS, NBLOCK, BLOCK_FEAT, D), D ** -0.5, 0.0625, ((2, 4), (3, 64)))
    q_bias = centred(seeds[4], (LAYERS, D), 0.5, 3.0, ((1, 64),))
    kv_weight = centred(seeds[5], (LAYERS, NBLOCK, BLOCK_FEAT, 2 * KVH * HD), D ** -0.5, 0.0625, ((2, 4), (3, 64)))
    kv_bias = draw_kv_bias(jax.random.fold_in(seeds[8], 71), 0)
    out_weight = centred(seeds[7], (LAYERS, NBLOCK, BLOCK_FEAT, D), D ** -0.5, 0.0625, ((2, 4), (3, 64)))
    return {"hidden": hidden, "lengths": lengths, "norm_gain": norm_gain, "q_weight": q_weight, "q_bias": q_bias, "kv_weight": kv_weight, "kv_bias": kv_bias, "out_weight": out_weight}


def rotate(heads, positions):
    half = heads.shape[-1] // 2
    inv = 1.0 / 1000000.0 ** (jnp.arange(half, dtype=jnp.float32) * 2.0 / heads.shape[-1])
    angle = positions.astype(jnp.float32)[:, None] * inv[None, :]
    cosine = jnp.cos(angle)[:, None, :]
    sine = jnp.sin(angle)[:, None, :]
    first = heads[..., :half]
    second = heads[..., half:]
    return jnp.concatenate([first * cosine - second * sine, second * cosine + first * sine], axis=-1)

def one_prompt(x, length, norm_gain, q_weight, q_bias, kv_weight, kv_bias, out_weight):
    tokens = x.shape[0]
    heads = D // HD
    group = heads // KVH
    positions = jnp.arange(tokens, dtype=jnp.int32)
    allowed = (positions[None, :] <= positions[:, None]) & (positions[None, :] < length)
    for layer in range(LAYERS):
        query_matrix = q_weight[layer].reshape(D, D)
        pair_matrix = kv_weight[layer].reshape(D, 2 * KVH * HD)
        output_matrix = out_weight[layer].reshape(D, D)
        xf = x.astype(jnp.float32)
        ss = lax.optimization_barrier(jnp.sum(xf * xf, axis=1))
        xn = (xf * lax.rsqrt(ss / D + 1e-06)[:, None] * norm_gain[layer][None, :]).astype(jnp.bfloat16)
        query = jnp.dot(xn, query_matrix, preferred_element_type=jnp.float32) + q_bias[layer].astype(jnp.float32)[None, :]
        query = rotate(query.reshape(tokens, heads, HD), positions).astype(jnp.bfloat16)
        kv = jnp.dot(xn, pair_matrix, preferred_element_type=jnp.float32)
        kv = (kv + kv_bias[layer].astype(jnp.float32)[None, :]).astype(jnp.bfloat16)
        keys = rotate(kv[:, :KVH * HD].reshape(tokens, KVH, HD).astype(jnp.float32), positions).astype(jnp.bfloat16)
        values = kv[:, KVH * HD:].reshape(tokens, KVH, HD)
        grouped = query.reshape(tokens, KVH, group, HD).astype(jnp.float32)
        scores = jnp.einsum('tkgd,skd->kgts', grouped, keys.astype(jnp.float32)) / jnp.sqrt(jnp.float32(HD))
        scores = jnp.where(allowed[None, None], scores, jnp.float32(-1e+30))
        top = lax.optimization_barrier(jnp.max(scores, axis=-1, keepdims=True))
        weights = jnp.exp(scores - top)
        probs = (weights / lax.optimization_barrier(jnp.sum(weights, axis=-1, keepdims=True))).astype(jnp.bfloat16)
        attended = jnp.einsum('kgts,skd->tkgd', probs.astype(jnp.float32), values.astype(jnp.float32))
        attended = attended.reshape(tokens, D).astype(jnp.bfloat16)
        mixed = jnp.dot(attended, output_matrix, preferred_element_type=jnp.float32)
        x = (xf + mixed).astype(jnp.bfloat16)
    return x

def reference(hidden, lengths, norm_gain, q_weight, q_bias, kv_weight, kv_bias, out_weight):
    outputs = []
    for prompt in range(hidden.shape[0]):
        outputs.append(one_prompt(hidden[prompt], lengths[prompt], norm_gain, q_weight, q_bias, kv_weight, kv_bias, out_weight))
    return jnp.stack(outputs, axis=0)
```

```python
import functools

import jax
import jax.numpy as jnp
from jax import lax
from jax.experimental import pallas as pl
from jax.experimental.pallas import tpu as pltpu
from jax.sharding import PartitionSpec as P

D = 8192
HD = 128
LAYERS = 2
TOK = 256
GRP = 4
QUARTER = HD // GRP
ALL = GRP * TOK
HALF = ALL // 2
KCORE = 32 * QUARTER
BF = jnp.bfloat16
F32 = jnp.float32

VM = pl.BlockSpec(memory_space=pltpu.VMEM)
SM = pl.BlockSpec(memory_space=pltpu.SMEM)
PARAMS = pltpu.CompilerParams(vmem_limit_bytes=24 * 1024 * 1024)


def tp_index(x, z, y, c):
    return ((x * 2 + z) * 4 + y) * 2 + c


COORDS = [
    (x, z, y, c) for x in range(4) for z in range(2) for y in range(4) for c in range(2)
]


def tp_perm(move):
    return [(tp_index(*at), tp_index(*move(*at))) for at in COORDS]


CORE_SWAP = tp_perm(lambda x, z, y, c: (x, z, y, 1 - c))
Z_SWAP = tp_perm(lambda x, z, y, c: (x, 1 - z, y, c))
X_SLOT = [tp_perm(lambda x, z, y, c, s=s: ((x - s) % 4, z, y, c)) for s in range(4)]
Y_SLOT = [tp_perm(lambda x, z, y, c, s=s: (x, z, (y - s) % 4, c)) for s in range(4)]
G_UP = [[(g, (g + k) % GRP) for g in range(GRP)] for k in range(GRP)]
G_DOWN = [[(g, (g - k) % GRP) for g in range(GRP)] for k in range(GRP)]


def kv_perm(own):
    pairs = []
    for m in range(64):
        kind, head, part = m // 32, (m % 32) // 4, m % 4
        pairs.append((m, 8 * head + 2 * part + (kind if own else 1 - kind)))
    return pairs


KV_OWN = kv_perm(True)
KV_OTHER = kv_perm(False)


def split3(value):
    high = value.astype(BF)
    rest = value - high.astype(F32)
    middle = rest.astype(BF)
    low = (rest - middle.astype(F32)).astype(BF)
    return high, middle, low


def call(body, outs, *args, specs=None, scratch=(), flops=0, nbytes=1 << 20):
    return pl.pallas_call(
        body,
        grid=(1,),
        out_shape=outs,
        in_specs=specs or [VM] * len(args),
        out_specs=jax.tree.map(lambda _: VM, outs),
        scratch_shapes=list(scratch),
        compiler_params=PARAMS,
        cost_estimate=pl.CostEstimate(flops=flops, bytes_accessed=nbytes, transcendentals=0),
    )(*args)


def shape(dims, dtype=BF):
    return jax.ShapeDtypeStruct(dims, dtype)


def block_order(where):
    x, z, y = where[0], where[1], where[2]
    for slot in range(32):
        dy, dx, dz = slot // 8, (slot // 2) % 4, slot % 2
        yield slot, (((x + dx) & 3) * 2 + (z ^ dz)) * 4 + ((y + dy) & 3)


def prep_in_body(where, own, other, kv_own, kv_other, out, wide, narrow):
    c = where[3]
    for base, ref, kv in ((0, own, kv_own), (160, other, kv_other)):
        for slot, pair in block_order(where):
            at = pl.ds(slot * QUARTER, QUARTER)
            wide[at, :] = ref[0, 2 * pair + c] if base == 0 else ref[0, pair]
            narrow[at, :] = kv[0, pair]
        out[base : base + 128, :] = wide[...].T
        out[base + 128 : base + 160, :] = narrow[...].T


def prep_out_body(rolled, where, own, other, out, wide, tall):
    c, g = where[3], where[4]
    for base, ref in ((0, own), (4, other)):
        for slot, pair in block_order(where):
            wide[pl.ds(slot * QUARTER, QUARTER), :] = (
                ref[0, 2 * pair + c] if base == 0 else ref[0, pair]
            )
        tall[...] = wide[...].T.reshape(4, QUARTER, KCORE)
        for k in range(4):
            out[base + k] = tall[(g + k) & 3] if rolled else tall[k]


def layer_spec(dims, layer):
    return pl.BlockSpec((1,) + dims, lambda i: (layer,) + (0,) * len(dims))


def prep_in(layer, where, q_weight, q_other, kv_own, kv_other):
    return call(
        prep_in_body,
        shape((320, KCORE)),
        where,
        q_weight,
        q_other,
        kv_own,
        kv_other,
        specs=[
            SM,
            layer_spec((64, QUARTER, 128), layer),
            layer_spec((32, QUARTER, 128), layer),
            layer_spec((32, QUARTER, 32), layer),
            layer_spec((32, QUARTER, 32), layer),
        ],
        scratch=[pltpu.VMEM((KCORE, 128), BF), pltpu.VMEM((KCORE, 32), BF)],
    )


def prep_out(layer, where, out_weight, o_other):
    out = call(
        functools.partial(prep_out_body, layer == 0),
        shape((8, QUARTER, KCORE)),
        where,
        out_weight,
        o_other,
        specs=[
            SM,
            layer_spec((64, QUARTER, 128), layer),
            layer_spec((32, QUARTER, 128), layer),
        ],
        scratch=[pltpu.VMEM((KCORE, 128), BF), pltpu.VMEM((4, QUARTER, KCORE), BF)],
    )
    return out.reshape(256, KCORE)


def init_body(where, hidden, gain, first, second, third, fourth, gains, tall):
    g = where[4]
    tall[...] = hidden[0].astype(F32).T.astype(BF).reshape(4, QUARTER, TOK)
    for k, out in enumerate((first, second, third, fourth)):
        out[...] = tall[(g + k) & 3]
    gains[...] = jnp.zeros_like(gains)
    for layer in range(LAYERS):
        for i, part in enumerate(split3(gain[:, layer : layer + 1])):
            gains[:, 3 * layer + i : 3 * layer + i + 1] = part


def gather(block, cut):
    other = lax.ppermute(block, "tp", Z_SWAP)
    both = jnp.stack([block, other])
    left, right = both[:, :, :cut], both[:, :, cut:]
    lefts = [left] + [lax.ppermute(left, "tp", X_SLOT[s]) for s in (1, 3, 2)]
    rights = [right] + [lax.ppermute(right, "tp", Y_SLOT[s]) for s in (1, 3, 2)]
    left = jnp.stack([lefts[0], lefts[1], lefts[3], lefts[2]])
    right = jnp.stack([rights[0], rights[1], rights[3], rights[2]])
    lefts = [left] + [lax.ppermute(left, "tp", Y_SLOT[s]) for s in (1, 3, 2)]
    rights = [right] + [lax.ppermute(right, "tp", X_SLOT[s]) for s in (1, 3, 2)]
    return (
        [lefts[0], lefts[1], lefts[3], lefts[2]],
        [rights[0], rights[1], rights[3], rights[2]],
    )


def project_in_body(layer, *refs):
    lefts, rights, gains = refs[0:4], refs[4:8], refs[8:12]
    weight, mine, total, theirs, scaled = refs[12:]
    squares_l = jnp.zeros((QUARTER, HALF), F32)
    squares_r = jnp.zeros((QUARTER, HALF), F32)
    for slot in range(32):
        dy, dx, dz = slot // 8, (slot // 2) % 4, slot % 2
        rows = slice(slot * QUARTER, (slot + 1) * QUARTER)
        parts = gains[dy][dx, dz, :, 3 * layer : 3 * layer + 3].astype(F32)
        gain = parts[:, 0:1] + parts[:, 1:2] + parts[:, 2:3]
        left = lefts[dy][dx, dz].astype(F32)
        right = rights[dx][dy, dz].astype(F32)
        scaled[rows, :HALF] = (left * gain).astype(BF)
        scaled[rows, HALF:] = (right * gain).astype(BF)
        squares_l += left * left
        squares_r += right * right
    ss_l = jnp.sum(squares_l, axis=0, keepdims=True)
    ss_r = jnp.sum(squares_r, axis=0, keepdims=True)
    ss = jnp.concatenate([ss_l, ss_r], axis=1)
    total[...] = jnp.broadcast_to(ss, total.shape)
    out = jnp.dot(weight[...], scaled[...], preferred_element_type=F32)
    mine[...] = out[:160]
    high, middle, low = split3(jnp.broadcast_to(ss, (16, ALL)))
    row = lax.broadcasted_iota(jnp.int32, (16, ALL), 0)
    zero = jnp.zeros((16, ALL), F32)
    packed = jnp.where(
        row == 0,
        high.astype(F32),
        jnp.where(row == 1, middle.astype(F32), jnp.where(row == 2, low.astype(F32), zero)),
    )
    theirs[0:160, :] = out[160:].astype(BF)
    theirs[160:176, :] = packed.astype(BF)


def project_in(layer, lefts, rights, gains, weight):
    half = pl.BlockSpec((4, 2, QUARTER, HALF), lambda i: (0, 0, 0, 0))
    lane = pl.BlockSpec((4, 2, QUARTER, 128), lambda i: (0, 0, 0, HALF // 128))
    return call(
        functools.partial(project_in_body, layer),
        [shape((160, ALL), F32), shape((8, ALL), F32), shape((176, ALL))],
        *lefts,
        *rights,
        *gains,
        weight,
        specs=[half] * 8 + [lane] * 4 + [VM],
        scratch=[pltpu.VMEM((KCORE, ALL), BF)],
        flops=2 * 320 * KCORE * ALL,
        nbytes=5 << 20,
    )


def unpack_ss(ref):
    rows = ref[160:176, :].astype(F32)
    return rows[0:1] + rows[1:2] + rows[2:3]


def reduce_in_body(mine, total, theirs, keep, *sends):
    values = mine[...] + theirs[0:160, :].astype(F32)
    ss = total[0:1, :] + unpack_ss(theirs)
    keep[0:160, :] = values[:, :TOK]
    keep[160:168, :] = jnp.broadcast_to(ss[:, :TOK], (8, TOK))
    for k, send in enumerate(sends, start=1):
        at = slice(k * TOK, (k + 1) * TOK)
        send[0:160, :] = values[:, at].astype(BF)
        parts = [p.astype(F32) for p in split3(jnp.broadcast_to(ss[:, at], (16, TOK)))]
        row = lax.broadcasted_iota(jnp.int32, (16, TOK), 0)
        packed = jnp.where(
            row == 0, parts[0], jnp.where(row == 1, parts[1], jnp.where(row == 2, parts[2], 0.0))
        )
        send[160:176, :] = packed.astype(BF)


def norm_scale(keep, arrived):
    ss = keep[160:161, :]
    for ref in arrived:
        ss = ss + unpack_ss(ref)
    return lax.rsqrt(ss / D + 1e-06)


def total_rows(keep, arrived, rows):
    out = keep[rows, :]
    for ref in arrived:
        out = out + ref[rows, :].astype(F32)
    return out


def kv_body(keep, a, b, c, bias, out):
    arrived = (a, b, c)
    scale = norm_scale(keep, arrived)
    out[...] = (total_rows(keep, arrived, slice(128, 160)) * scale + bias[...]).astype(BF)


def rotated(first, second, cosine, sine):
    return (
        (first * cosine - second * sine).astype(BF),
        (second * cosine + first * sine).astype(BF),
    )


def attend_body(
    where, length, keep, a, b, c, bias, kv0, kv1, kv2, kv3, cosine, sine, *rest
):
    outs, pairs, query, keys, vals, tall = rest[0:4], rest[4], rest[5], rest[6], rest[7], rest[8]
    arrived = (a, b, c)
    y, core, g = where[2], where[3], where[4]
    scale = norm_scale(keep, arrived)
    q = total_rows(keep, arrived, slice(0, 128)) * scale + bias[...]
    cos, sin = cosine[...], sine[...]
    query[0:64, :], query[64:128, :] = rotated(q[:64], q[64:], cos, sin)
    for s, ref in enumerate((kv0, kv1, kv2, kv3)):
        pairs[s] = ref[...]
    k = [pairs[(i - y) & 3, core].astype(F32) for i in range(4)]
    for i in range(4):
        vals[i * QUARTER : (i + 1) * QUARTER, :] = pairs[(i - y) & 3, 1 - core]
    keys[0:64, :], keys[64:128, :] = rotated(
        jnp.concatenate(k[0:2], axis=0), jnp.concatenate(k[2:4], axis=0), cos, sin
    )
    scores = lax.dot_general(
        keys[...], query[...], (((0,), (0,)), ((), ())), preferred_element_type=F32
    ) / jnp.sqrt(jnp.float32(HD))
    s_at = lax.broadcasted_iota(jnp.int32, (TOK, TOK), 0)
    t_at = lax.broadcasted_iota(jnp.int32, (TOK, TOK), 1)
    allowed = (s_at <= t_at) & (s_at < length[0])
    scores = jnp.where(allowed, scores, -1e30)
    weights = jnp.exp(scores - jnp.max(scores, axis=0, keepdims=True))
    probs = (weights / jnp.sum(weights, axis=0, keepdims=True)).astype(BF)
    attended = jnp.dot(vals[...], probs, preferred_element_type=F32).astype(BF)
    tall[...] = attended.reshape(4, QUARTER, TOK)
    for i, out in enumerate(outs):
        out[...] = tall[(g + i) & 3]


def project_out_body(*refs):
    lefts, rights = refs[0:4], refs[4:8]
    weight, mine, theirs, scaled = refs[8:]
    for slot in range(32):
        dy, dx, dz = slot // 8, (slot // 2) % 4, slot % 2
        rows = slice(slot * QUARTER, (slot + 1) * QUARTER)
        scaled[rows, :HALF] = lefts[dy][dx, dz]
        scaled[rows, HALF:] = rights[dx][dy, dz]
    out = jnp.dot(weight[...], scaled[...], preferred_element_type=F32)
    mine[...] = out[:128]
    theirs[...] = out[128:].astype(BF)


def project_out(lefts, rights, weight):
    return call(
        project_out_body,
        [shape((128, ALL), F32), shape((128, ALL))],
        *lefts,
        *rights,
        weight,
        scratch=[pltpu.VMEM((KCORE, ALL), BF)],
        flops=2 * 256 * KCORE * ALL,
        nbytes=5 << 20,
    )


def by_rows_body(mine, theirs, keep, *sends):
    values = mine[...] + theirs[...].astype(F32)
    keep[...] = values[:QUARTER]
    for k, send in enumerate(sends, start=1):
        send[...] = values[k * QUARTER : (k + 1) * QUARTER].astype(BF)


def by_slots_body(mine, theirs, keep, *sends):
    values = mine[...] + theirs[...].astype(F32)
    keep[...] = values[:, :TOK]
    for k, send in enumerate(sends, start=1):
        send[...] = values[:, k * TOK : (k + 1) * TOK].astype(BF)


def residual_body(x, keep, a, b, c, out):
    for slot in range(4):
        at = slice(slot * TOK, (slot + 1) * TOK)
        value = x[:, at].astype(F32)
        mixed = keep[:, at]
        for k, ref in enumerate((a, b, c), start=1):
            there = (slot - k) % 4
            mixed = mixed + ref[:, there * TOK : (there + 1) * TOK].astype(F32)
        out[:, at] = (value + mixed).astype(BF)


def final_body(where, x0, x1, x2, x3, keep, a, b, c, out, tall):
    g = where[4]
    for k, ref in enumerate((x0, x1, x2, x3)):
        tall[(g + k) & 3] = ref[...]
    mixed = keep[...]
    for ref in (a, b, c):
        mixed = mixed + ref[...].astype(F32)
    value = tall[...].reshape(HD, TOK).astype(F32) + mixed
    out[0] = value.astype(BF).astype(F32).T.astype(BF)


def local(hidden, lengths, norm_gain, q_weight, q_bias, kv_weight, kv_bias, out_weight):
    tp = lax.axis_index("tp").astype(jnp.int32)
    g = lax.axis_index("grp").astype(jnp.int32)
    core, y, z, x_at = tp % 2, (tp // 2) % 4, (tp // 8) % 2, tp // 16
    where = jnp.stack([x_at, z, y, core, g, g, g, g])
    kind = tp // 32

    def halves(weight, which):
        parts = weight.reshape(LAYERS, 32, 2, QUARTER, weight.shape[3])
        return lax.dynamic_index_in_dim(parts, which, axis=2, keepdims=False)

    own_gain = lax.dynamic_slice(norm_gain, (0, g * QUARTER), (LAYERS, QUARTER)).T
    piece = shape((QUARTER, TOK))
    *pieces, gains = call(
        init_body,
        [piece, piece, piece, piece, shape((QUARTER, 128))],
        where,
        hidden,
        own_gain,
        specs=[SM, VM, VM],
        scratch=[pltpu.VMEM((4, QUARTER, TOK), BF)],
    )
    slots = [pieces[0]] + [lax.ppermute(pieces[k], "grp", G_UP[k]) for k in (1, 2, 3)]
    x = jnp.concatenate(slots, axis=1)

    kv_own = lax.ppermute(halves(kv_weight, kind), "tp", KV_OWN)
    kv_other = lax.ppermute(halves(kv_weight, 1 - kind), "tp", KV_OTHER)
    kv_bias = lax.ppermute(kv_bias, "tp", KV_OWN).astype(F32).T
    q_other = lax.ppermute(halves(q_weight, 1 - core), "tp", CORE_SWAP)
    o_other = lax.ppermute(halves(out_weight, 1 - core), "tp", CORE_SWAP)
    q_bias = q_bias.astype(F32).T

    inv = 1.0 / 1000000.0 ** (jnp.arange(HD // 2, dtype=F32) * 2.0 / HD)
    angle = inv[:, None] * jnp.arange(TOK, dtype=F32)[None, :]
    cosine, sine = jnp.cos(angle), jnp.sin(angle)

    source = jnp.concatenate(slots[0:2] + [gains] + slots[2:4], axis=1)
    gain_lanes = None
    for layer in range(LAYERS):
        w_in = prep_in(layer, where, q_weight, q_other, kv_own, kv_other)
        w_out = prep_out(layer, where, out_weight, o_other)
        if layer == 0:
            lefts, rights = gather(source, HALF + 128)
            gain_lanes = lefts
        else:
            lefts, rights = gather(x, HALF)
        mine, total, theirs = project_in(layer, lefts, rights, gain_lanes, w_in)
        theirs = lax.ppermute(theirs, "tp", CORE_SWAP)
        send = shape((176, TOK))
        keep, *sends = call(
            reduce_in_body, [shape((168, TOK), F32), send, send, send], mine, total, theirs
        )
        arrived = [lax.ppermute(sends[k - 1], "grp", G_DOWN[k]) for k in (1, 2, 3)]
        kv = call(
            kv_body,
            shape((QUARTER, TOK)),
            keep,
            *arrived,
            kv_bias[:, layer : layer + 1],
        )
        pair = jnp.stack([kv, lax.ppermute(kv, "tp", CORE_SWAP)])
        pairs = [pair] + [lax.ppermute(pair, "tp", Y_SLOT[s]) for s in (1, 2, 3)]
        pieces = call(
            attend_body,
            [piece, piece, piece, piece],
            where,
            lengths,
            keep,
            *arrived,
            q_bias[:, layer : layer + 1],
            *pairs,
            cosine,
            sine,
            specs=[SM, SM] + [VM] * 11,
            scratch=[
                pltpu.VMEM((4, 2, QUARTER, TOK), BF),
                pltpu.VMEM((HD, TOK), BF),
                pltpu.VMEM((HD, TOK), BF),
                pltpu.VMEM((HD, TOK), BF),
                pltpu.VMEM((4, QUARTER, TOK), BF),
            ],
            flops=4 * TOK * TOK * HD,
        )
        slots = [pieces[0]] + [lax.ppermute(pieces[k], "grp", G_UP[k]) for k in (1, 2, 3)]
        lefts, rights = gather(jnp.concatenate(slots, axis=1), HALF)
        mine, theirs = project_out(lefts, rights, w_out)
        theirs = lax.ppermute(theirs, "tp", CORE_SWAP)
        if layer < LAYERS - 1:
            send = shape((QUARTER, ALL))
            keep, *sends = call(
                by_rows_body, [shape((QUARTER, ALL), F32), send, send, send], mine, theirs
            )
            arrived = [lax.ppermute(sends[k - 1], "grp", G_UP[k]) for k in (1, 2, 3)]
            x = call(residual_body, shape((QUARTER, ALL)), x, keep, *arrived)
        else:
            backs = [x[:, :TOK]] + [
                lax.ppermute(x[:, k * TOK : (k + 1) * TOK], "grp", G_DOWN[k]) for k in (1, 2, 3)
            ]
            send = shape((HD, TOK))
            keep, *sends = call(
                by_slots_body, [shape((HD, TOK), F32), send, send, send], mine, theirs
            )
            arrived = [lax.ppermute(sends[k - 1], "grp", G_DOWN[k]) for k in (1, 2, 3)]
            out = call(
                final_body,
                shape((1, TOK, HD)),
                where,
                *backs,
                keep,
                *arrived,
                specs=[SM] + [VM] * 8,
                scratch=[pltpu.VMEM((4, QUARTER, TOK), BF)],
            )
    return out


def solution(mesh):
    placed = (
        P("grp", None, "tp"),
        P("grp"),
        P(None, "tp"),
        P(None, None, "grp", "tp"),
        P(None, "tp"),
        P(None, None, "grp", "tp"),
        P(None, "tp"),
        P(None, None, "grp", "tp"),
    )
    return jax.shard_map(
        local, mesh=mesh, in_specs=placed, out_specs=P("grp", None, "tp"), check_vma=False
    )
```

```python
import functools

import jax
import jax.numpy as jnp
from jax import lax
from jax.experimental import pallas as pl
from jax.experimental.pallas import tpu as pltpu
from jax.sharding import PartitionSpec as P

D = 8192
HD = 128
LAYERS = 2
TOK = 256
GRP = 4
QUARTER = HD // GRP
PART = TOK // 2
WIDE = GRP * PART
DEPTH = 64 * QUARTER
BF = jnp.bfloat16
F32 = jnp.float32

VM = pl.BlockSpec(memory_space=pltpu.VMEM)
SM = pl.BlockSpec(memory_space=pltpu.SMEM)
PARAMS = pltpu.CompilerParams(vmem_limit_bytes=24 * 1024 * 1024)


def tp_index(x, z, y, c):
    return ((x * 2 + z) * 4 + y) * 2 + c


COORDS = [
    (x, z, y, c) for x in range(4) for z in range(2) for y in range(4) for c in range(2)
]


def tp_perm(move):
    return [(tp_index(*at), tp_index(*move(*at))) for at in COORDS]


def along(x_first, s):
    def move(x, z, y, c):
        if (c == 0) == x_first:
            return ((x - s) % 4, z, y, c)
        return (x, z, (y - s) % 4, c)

    return tp_perm(move)


CORE_SWAP = tp_perm(lambda x, z, y, c: (x, z, y, 1 - c))
Z_SWAP = tp_perm(lambda x, z, y, c: (x, 1 - z, y, c))
FIRST = [along(True, s) for s in range(4)]
SECOND = [along(False, s) for s in range(4)]
Y_SLOT = [tp_perm(lambda x, z, y, c, s=s: (x, z, (y - s) % 4, c)) for s in range(4)]
G_UP = [[(g, (g + k) % GRP) for g in range(GRP)] for k in range(GRP)]
G_DOWN = [[(g, (g - k) % GRP) for g in range(GRP)] for k in range(GRP)]
KV_MOVE = [(m, 8 * ((m % 32) // 4) + 2 * (m % 4) + m // 32) for m in range(64)]


def split3(value):
    high = value.astype(BF)
    rest = value - high.astype(F32)
    middle = rest.astype(BF)
    low = (rest - middle.astype(F32)).astype(BF)
    return high, middle, low


def call(body, outs, *args, specs=None, scratch=(), flops=0, nbytes=1 << 20):
    return pl.pallas_call(
        body,
        grid=(1,),
        out_shape=outs,
        in_specs=specs or [VM] * len(args),
        out_specs=jax.tree.map(lambda _: VM, outs),
        scratch_shapes=list(scratch),
        compiler_params=PARAMS,
        cost_estimate=pl.CostEstimate(flops=flops, bytes_accessed=nbytes, transcendentals=0),
    )(*args)


def shape(dims, dtype=BF):
    return jax.ShapeDtypeStruct(dims, dtype)


def half_lanes(index):
    return pl.ds(pl.multiple_of(index * PART, PART), PART)


def turn_body(weight, out):
    for layer in range(LAYERS):
        out[layer] = weight[layer].reshape(DEPTH, HD).T


def turn_kv_body(weight, bias, out):
    for layer in range(LAYERS):
        out[layer, :, :DEPTH] = weight[layer].reshape(DEPTH, QUARTER).T
        out[layer, :, DEPTH:] = jnp.broadcast_to(bias[:, layer : layer + 1], (QUARTER, HD))


def init_body(where, hidden, gain, first, second, third, fourth, gains, tall):
    c, g = where[3], where[4]
    for i in range(2):
        half = c if i == 0 else 1 - c
        tokens = hidden[0, half_lanes(half), :]
        tall[:, i] = tokens.astype(F32).T.astype(BF).reshape(4, QUARTER, PART)
    for k, out in enumerate((first, second, third, fourth)):
        out[...] = tall[(g + k) & 3]
    gains[...] = jnp.zeros_like(gains)
    for layer in range(LAYERS):
        for i, part in enumerate(split3(gain[:, layer : layer + 1])):
            gains[0, :, 3 * layer + i : 3 * layer + i + 1] = part


def gather(block):
    other = lax.ppermute(block, "tp", Z_SWAP)
    both = jnp.stack([block, other])
    across = lax.ppermute(both, "tp", FIRST[2])
    up = lax.ppermute(both, "tp", FIRST[1])
    down = lax.ppermute(both, "tp", FIRST[3])
    line = jnp.stack([both, up, across, down])
    up = lax.ppermute(line, "tp", SECOND[1])
    down = lax.ppermute(line, "tp", SECOND[3])
    across_a = lax.ppermute(up[:2], "tp", SECOND[1])
    across_b = lax.ppermute(down[2:], "tp", SECOND[3])
    return line, up, across_a, across_b, down


def arrivals(where, refs):
    x, z, y, c = where[0], where[1], where[2], where[3]
    line, up, across_a, across_b, down = refs
    for second in range(4):
        for first in range(4):
            if second == 2:
                ref, at = (across_a, first) if first < 2 else (across_b, first - 2)
            else:
                ref, at = (line, up, None, down)[second], first
            col = (x + jnp.where(c == 0, first, second)) & 3
            row = (y + jnp.where(c == 0, second, first)) & 3
            for dz in range(2):
                pair = (col * 2 + (z ^ dz)) * 4 + row
                for dc in range(2):
                    start = pl.multiple_of((2 * pair + (c ^ dc)) * QUARTER, QUARTER)
                    yield pl.ds(start, QUARTER), dc, ref, at, dz


def project_in_body(layer, where, *refs):
    blocks, gains = refs[0:5], refs[5:10]
    own, own_kv, other, other_kv = refs[10:14]
    mine, total, theirs, weight, scaled = refs[14:]
    for base, wide, narrow in ((0, own, own_kv), (160, other, other_kv)):
        weight[base : base + 128, :] = wide[0]
        weight[base + 128 : base + 160, :] = narrow[0, :, :DEPTH]
    squares = [jnp.zeros((QUARTER, PART), F32) for _ in range(GRP)]
    places = zip(arrivals(where, blocks), arrivals(where, gains))
    for (rows, dc, ref, at, dz), (_, _, gain_ref, _, _) in places:
        lane = 6 * dc + 3 * layer
        parts = gain_ref[at, dz, 0, :, lane : lane + 3].astype(F32)
        gain = parts[:, 0:1] + parts[:, 1:2] + parts[:, 2:3]
        for slot in range(GRP):
            value = ref[at, dz, 4 * dc + slot].astype(F32)
            scaled[rows, slot * PART : (slot + 1) * PART] = (value * gain).astype(BF)
            squares[slot] += value * value
    ss = jnp.concatenate([jnp.sum(s, axis=0, keepdims=True) for s in squares], axis=1)
    total[...] = jnp.broadcast_to(ss, total.shape)
    out = jnp.dot(weight[...], scaled[...], preferred_element_type=F32)
    mine[...] = out[:160]
    theirs[0:160, :] = out[160:].astype(BF)
    theirs[160:176, :] = pack_ss(ss)


def pack_ss(ss):
    high, middle, low = [
        p.astype(F32) for p in split3(jnp.broadcast_to(ss, (16, ss.shape[1])))
    ]
    row = lax.broadcasted_iota(jnp.int32, high.shape, 0)
    return jnp.where(
        row == 0, high, jnp.where(row == 1, middle, jnp.where(row == 2, low, 0.0))
    ).astype(BF)


def unpack_ss(ref, at=slice(None)):
    rows = ref[160:176, at].astype(F32)
    return rows[0:1] + rows[1:2] + rows[2:3]


def project_in(layer, where, blocks, gains, own, own_kv, other, other_kv):
    def tiles(length, first, count):
        return pl.BlockSpec(
            (length, 2, count, QUARTER, PART), lambda i: (0, 0, first, 0, 0)
        )

    def of_layer(rows, depth):
        return pl.BlockSpec((1, rows, depth), lambda i: (layer, 0, 0))

    lengths = (4, 4, 2, 2, 4)
    weights = [of_layer(HD, DEPTH), of_layer(QUARTER, DEPTH + HD)]
    return call(
        functools.partial(project_in_body, layer),
        [shape((160, WIDE), F32), shape((8, WIDE), F32), shape((176, WIDE))],
        where,
        *blocks,
        *gains,
        own,
        own_kv,
        other,
        other_kv,
        specs=[SM]
        + [tiles(n, 0, 8) for n in lengths]
        + [tiles(n, 8, 1) for n in lengths]
        + weights
        + weights,
        scratch=[pltpu.VMEM((320, DEPTH), BF), pltpu.VMEM((DEPTH, WIDE), BF)],
        flops=2 * 320 * DEPTH * WIDE,
        nbytes=5 << 20,
    )


def share_in_body(where, mine, total, theirs, keep, *sends):
    c = where[3]
    own, other = half_lanes(c), half_lanes(1 - c)
    keep[0:160, own] = mine[:, :PART]
    keep[0:160, other] = theirs[0:160, :PART].astype(F32)
    keep[160:168, own] = total[:, :PART]
    keep[160:168, other] = jnp.broadcast_to(unpack_ss(theirs, slice(0, PART)), (8, PART))
    for k, send in enumerate(sends, start=1):
        at = slice(k * PART, (k + 1) * PART)
        send[0:160, own] = mine[:, at].astype(BF)
        send[160:176, own] = pack_ss(total[0:1, at])
        send[:, other] = theirs[:, at]


def norm_scale(keep, arrived):
    ss = keep[160:161, :]
    for ref in arrived:
        ss = ss + unpack_ss(ref)
    return lax.rsqrt(ss / D + 1e-06)


def total_rows(keep, arrived, rows):
    out = keep[rows, :]
    for ref in arrived:
        out = out + ref[rows, :].astype(F32)
    return out


def kv_body(keep, a, b, c, bias, out):
    arrived = (a, b, c)
    scale = norm_scale(keep, arrived)
    column = bias[0, :, 0:1].astype(F32)
    out[...] = (total_rows(keep, arrived, slice(128, 160)) * scale + column).astype(BF)


def rotated(first, second, cosine, sine):
    return (
        (first * cosine - second * sine).astype(BF),
        (second * cosine + first * sine).astype(BF),
    )


def attend_body(
    where, length, keep, a, b, c, bias, kv0, kv1, kv2, kv3, cosine, sine, *rest
):
    outs, pairs, query, keys, vals, tall = rest[0:4], rest[4], rest[5], rest[6], rest[7], rest[8]
    arrived = (a, b, c)
    y, core, g = where[2], where[3], where[4]
    scale = norm_scale(keep, arrived)
    q = total_rows(keep, arrived, slice(0, 128)) * scale + bias[...]
    cos, sin = cosine[...], sine[...]
    query[0:64, :], query[64:128, :] = rotated(q[:64], q[64:], cos, sin)
    for s, ref in enumerate((kv0, kv1, kv2, kv3)):
        pairs[s] = ref[...]
    k = [pairs[(i - y) & 3, core].astype(F32) for i in range(4)]
    for i in range(4):
        vals[i * QUARTER : (i + 1) * QUARTER, :] = pairs[(i - y) & 3, 1 - core]
    keys[0:64, :], keys[64:128, :] = rotated(
        jnp.concatenate(k[0:2], axis=0), jnp.concatenate(k[2:4], axis=0), cos, sin
    )
    scores = lax.dot_general(
        keys[...], query[...], (((0,), (0,)), ((), ())), preferred_element_type=F32
    ) / jnp.sqrt(jnp.float32(HD))
    s_at = lax.broadcasted_iota(jnp.int32, (TOK, TOK), 0)
    t_at = lax.broadcasted_iota(jnp.int32, (TOK, TOK), 1)
    allowed = (s_at <= t_at) & (s_at < length[0])
    scores = jnp.where(allowed, scores, -1e30)
    weights = jnp.exp(scores - jnp.max(scores, axis=0, keepdims=True))
    probs = (weights / jnp.sum(weights, axis=0, keepdims=True)).astype(BF)
    attended = jnp.dot(vals[...], probs, preferred_element_type=F32).astype(BF)
    tall[...] = attended.reshape(4, QUARTER, TOK)
    for i, out in enumerate(outs):
        out[0] = tall[(g + i) & 3, :, half_lanes(core)]
        out[1] = tall[(g + i) & 3, :, half_lanes(1 - core)]


def project_out_body(where, *refs):
    blocks, own, other = refs[0:5], refs[5], refs[6]
    mine, theirs, weight, stacked = refs[7:]
    weight[0:HD, :] = own[0]
    weight[HD:, :] = other[0]
    for rows, dc, ref, at, dz in arrivals(where, blocks):
        for slot in range(GRP):
            stacked[rows, slot * PART : (slot + 1) * PART] = ref[at, dz, 4 * dc + slot]
    out = jnp.dot(weight[...], stacked[...], preferred_element_type=F32)
    mine[...] = out[:HD]
    theirs[...] = out[HD:].astype(BF)


def project_out(layer, where, blocks, own, other):
    of_layer = pl.BlockSpec((1, HD, DEPTH), lambda i: (layer, 0, 0))
    return call(
        project_out_body,
        [shape((HD, WIDE), F32), shape((HD, WIDE))],
        where,
        *blocks,
        own,
        other,
        specs=[SM] + [VM] * 5 + [of_layer] * 2,
        scratch=[pltpu.VMEM((2 * HD, DEPTH), BF), pltpu.VMEM((DEPTH, WIDE), BF)],
        flops=2 * 256 * DEPTH * WIDE,
        nbytes=5 << 20,
    )


def by_rows_body(where, mine, theirs, keep, *sends):
    g = where[4]
    for k in range(4):
        rows = pl.ds(pl.multiple_of(((g + k) & 3) * QUARTER, QUARTER), QUARTER)
        for slot in range(GRP):
            at = slice(slot * PART, (slot + 1) * PART)
            if k == 0:
                keep[slot] = mine[rows, at]
                keep[4 + slot] = theirs[rows, at].astype(F32)
            else:
                sends[k - 1][slot] = mine[rows, at].astype(BF)
                sends[k - 1][4 + slot] = theirs[rows, at]


def by_slots_body(mine, theirs, keep, *sends):
    for k in range(4):
        at = slice(k * PART, (k + 1) * PART)
        if k == 0:
            keep[0] = mine[:, at]
            keep[1] = theirs[:, at].astype(F32)
        else:
            sends[k - 1][0] = mine[:, at].astype(BF)
            sends[k - 1][1] = theirs[:, at]


def residual_body(x, keep, a, b, c, out):
    for half in range(2):
        for slot in range(4):
            mixed = keep[4 * half + slot]
            for k, ref in enumerate((a, b, c), start=1):
                mixed = mixed + ref[4 * half + (slot - k) % 4].astype(F32)
            out[4 * half + slot] = (x[4 * half + slot].astype(F32) + mixed).astype(BF)


def final_body(where, x0, x1, x2, x3, keep, a, b, c, out, tall):
    core, g = where[3], where[4]
    for k, ref in enumerate((x0, x1, x2, x3)):
        for half in range(2):
            tall[half, (g + k) & 3] = ref[half]
    for half in range(2):
        mixed = keep[half]
        for ref in (a, b, c):
            mixed = mixed + ref[half].astype(F32)
        value = (tall[half].reshape(HD, PART).astype(F32) + mixed).astype(BF)
        at = half_lanes(core if half == 0 else 1 - core)
        out[0, at, :] = value.astype(F32).T.astype(BF)


def both_cores(x, extra=()):
    sent = lax.ppermute(jnp.concatenate([x[4:], *extra]), "tp", CORE_SWAP)
    if not extra:
        return jnp.concatenate([x[:4], sent])
    lanes = jnp.concatenate(
        [extra[0][:, :, :6], sent[4:, :, :6], extra[0][:, :, 12:]], axis=2
    )
    return jnp.concatenate([x[:4], sent[:4], lanes])


def tiles_of(pieces):
    slots = [pieces[0]] + [lax.ppermute(pieces[k], "grp", G_UP[k]) for k in (1, 2, 3)]
    return jnp.stack(slots, axis=1).reshape(8, QUARTER, PART)


def local(hidden, lengths, norm_gain, q_weight, q_bias, kv_weight, kv_bias, out_weight):
    tp = lax.axis_index("tp").astype(jnp.int32)
    g = lax.axis_index("grp").astype(jnp.int32)
    where = jnp.stack([tp // 16, (tp // 8) % 2, (tp // 2) % 4, tp % 2, g, g, g, g])

    own_gain = lax.dynamic_slice(norm_gain, (0, g * QUARTER), (LAYERS, QUARTER)).T
    piece = shape((2, QUARTER, PART))
    *pieces, gains = call(
        init_body,
        [piece, piece, piece, piece, shape((1, QUARTER, PART))],
        where,
        hidden,
        own_gain,
        specs=[SM, VM, VM],
        scratch=[pltpu.VMEM((4, 2, QUARTER, PART), BF)],
    )
    x = tiles_of(pieces)

    kv_turned = call(
        turn_kv_body, shape((LAYERS, QUARTER, DEPTH + HD)), kv_weight, kv_bias.T
    )
    kv_own = lax.ppermute(kv_turned, "tp", KV_MOVE)
    kv_other = lax.ppermute(kv_own, "tp", CORE_SWAP)
    turned = shape((LAYERS, HD, DEPTH))
    q_own = call(turn_body, turned, q_weight)
    q_other = lax.ppermute(q_own, "tp", CORE_SWAP)
    o_own = call(turn_body, turned, out_weight)
    o_other = lax.ppermute(o_own, "tp", CORE_SWAP)
    q_bias = q_bias.astype(F32).T

    inv = 1.0 / 1000000.0 ** (jnp.arange(HD // 2, dtype=F32) * 2.0 / HD)
    angle = inv[:, None] * jnp.arange(TOK, dtype=F32)[None, :]
    cosine, sine = jnp.cos(angle), jnp.sin(angle)

    gain_blocks = None
    for layer in range(LAYERS):
        if layer == 0:
            blocks = gather(both_cores(x, (gains,)))
            gain_blocks = blocks
        else:
            blocks = gather(both_cores(x))
        mine, total, theirs = project_in(
            layer, where, blocks, gain_blocks, q_own, kv_own, q_other, kv_other
        )
        theirs = lax.ppermute(theirs, "tp", CORE_SWAP)
        send = shape((176, TOK))
        keep, *sends = call(
            share_in_body,
            [shape((168, TOK), F32), send, send, send],
            where,
            mine,
            total,
            theirs,
            specs=[SM] + [VM] * 3,
        )
        arrived = [lax.ppermute(sends[k - 1], "grp", G_DOWN[k]) for k in (1, 2, 3)]
        kv = call(
            kv_body,
            shape((QUARTER, TOK)),
            keep,
            *arrived,
            kv_own,
            specs=[VM] * 4
            + [pl.BlockSpec((1, QUARTER, HD), lambda i: (layer, 0, DEPTH // HD))],
        )
        pair = jnp.stack([kv, lax.ppermute(kv, "tp", CORE_SWAP)])
        pairs = [pair] + [lax.ppermute(pair, "tp", Y_SLOT[s]) for s in (1, 2, 3)]
        pieces = call(
            attend_body,
            [piece, piece, piece, piece],
            where,
            lengths,
            keep,
            *arrived,
            q_bias[:, layer : layer + 1],
            *pairs,
            cosine,
            sine,
            specs=[SM, SM] + [VM] * 11,
            scratch=[
                pltpu.VMEM((4, 2, QUARTER, TOK), BF),
                pltpu.VMEM((HD, TOK), BF),
                pltpu.VMEM((HD, TOK), BF),
                pltpu.VMEM((HD, TOK), BF),
                pltpu.VMEM((4, QUARTER, TOK), BF),
            ],
            flops=4 * TOK * TOK * HD,
        )
        blocks = gather(both_cores(tiles_of(pieces)))
        mine, theirs = project_out(layer, where, blocks, o_own, o_other)
        theirs = lax.ppermute(theirs, "tp", CORE_SWAP)
        if layer < LAYERS - 1:
            send = shape((8, QUARTER, PART))
            keep, *sends = call(
                by_rows_body,
                [shape((8, QUARTER, PART), F32), send, send, send],
                where,
                mine,
                theirs,
                specs=[SM, VM, VM],
            )
            arrived = [lax.ppermute(sends[k - 1], "grp", G_UP[k]) for k in (1, 2, 3)]
            x = call(residual_body, shape((8, QUARTER, PART)), x, keep, *arrived)
        else:
            slots = x.reshape(2, 4, QUARTER, PART)
            backs = [slots[:, 0]] + [
                lax.ppermute(slots[:, k], "grp", G_DOWN[k]) for k in (1, 2, 3)
            ]
            send = shape((2, HD, PART))
            keep, *sends = call(
                by_slots_body, [shape((2, HD, PART), F32), send, send, send], mine, theirs
            )
            arrived = [lax.ppermute(sends[k - 1], "grp", G_DOWN[k]) for k in (1, 2, 3)]
            out = call(
                final_body,
                shape((1, TOK, HD)),
                where,
                *backs,
                keep,
                *arrived,
                specs=[SM] + [VM] * 8,
                scratch=[pltpu.VMEM((2, 4, QUARTER, PART), BF)],
            )
    return out


def solution(mesh):
    placed = (
        P("grp", None, "tp"),
        P("grp"),
        P(None, "tp"),
        P(None, None, "grp", "tp"),
        P(None, "tp"),
        P(None, None, "grp", "tp"),
        P(None, "tp"),
        P(None, None, "grp", "tp"),
    )
    return jax.shard_map(
        local, mesh=mesh, in_specs=placed, out_specs=P("grp", None, "tp"), check_vma=False
    )
```

```python
import functools

import jax
import jax.numpy as jnp
from jax import lax
from jax.experimental import pallas as pl
from jax.experimental.pallas import tpu as pltpu
from jax.sharding import PartitionSpec as P

D = 8192
HD = 128
LAYERS = 2
TOK = 256
GRP = 4
QUARTER = HD // GRP
PART = TOK // 2
WIDE = GRP * PART
DEPTH = 64 * QUARTER
IN = HD + QUARTER
ROWS = 2 * HD
BF = jnp.bfloat16
F32 = jnp.float32

VM = pl.BlockSpec(memory_space=pltpu.VMEM)
SM = pl.BlockSpec(memory_space=pltpu.SMEM)
ANY = pl.BlockSpec(memory_space=pl.ANY)
PARAMS = pltpu.CompilerParams(vmem_limit_bytes=40 * 1024 * 1024)


def tp_index(x, z, y, c):
    return ((x * 2 + z) * 4 + y) * 2 + c


COORDS = [
    (x, z, y, c) for x in range(4) for z in range(2) for y in range(4) for c in range(2)
]


def tp_perm(move):
    return [(tp_index(*at), tp_index(*move(*at))) for at in COORDS]


def along(x_first, s):
    def move(x, z, y, c):
        if (c == 0) == x_first:
            return ((x - s) % 4, z, y, c)
        return (x, z, (y - s) % 4, c)

    return tp_perm(move)


CORE_SWAP = tp_perm(lambda x, z, y, c: (x, z, y, 1 - c))
Z_SWAP = tp_perm(lambda x, z, y, c: (x, 1 - z, y, c))
FIRST = [along(True, s) for s in range(4)]
SECOND = [along(False, s) for s in range(4)]
Y_SLOT = [tp_perm(lambda x, z, y, c, s=s: (x, z, (y - s) % 4, c)) for s in range(4)]
G_UP = [[(g, (g + k) % GRP) for g in range(GRP)] for k in range(GRP)]
G_DOWN = [[(g, (g - k) % GRP) for g in range(GRP)] for k in range(GRP)]
KV_MOVE = [(m, 8 * ((m % 32) // 4) + 2 * (m % 4) + m // 32) for m in range(64)]


def split3(value):
    high = value.astype(BF)
    rest = value - high.astype(F32)
    middle = rest.astype(BF)
    low = (rest - middle.astype(F32)).astype(BF)
    return high, middle, low


def call(body, outs, *args, specs=None, scratch=(), flops=0, nbytes=1 << 20):
    return pl.pallas_call(
        body,
        grid=(1,),
        out_shape=outs,
        in_specs=specs or [VM] * len(args),
        out_specs=jax.tree.map(lambda _: VM, outs),
        scratch_shapes=list(scratch),
        compiler_params=PARAMS,
        cost_estimate=pl.CostEstimate(flops=flops, bytes_accessed=nbytes, transcendentals=0),
    )(*args)


def shape(dims, dtype=BF):
    return jax.ShapeDtypeStruct(dims, dtype)


def half_lanes(index):
    return pl.ds(pl.multiple_of(index * PART, PART), PART)


def pack_ss(ss):
    parts = [p.astype(F32) for p in split3(jnp.broadcast_to(ss, (16, ss.shape[1])))]
    row = lax.broadcasted_iota(jnp.int32, parts[0].shape, 0)
    out = jnp.zeros(parts[0].shape, F32)
    for i, part in enumerate(parts):
        out = jnp.where(row == i, part, out)
    return out.astype(BF)


def unpack_ss(rows):
    rows = rows.astype(F32)
    return rows[0:1] + rows[1:2] + rows[2:3]


def rotated(value, cosine, sine):
    first, second = value[:64], value[64:]
    return jnp.concatenate(
        [first * cosine - second * sine, second * cosine + first * sine], axis=0
    ).astype(BF)


def turn_body(weight, out):
    for layer in range(LAYERS):
        out[layer] = weight[layer].reshape(DEPTH, HD).T


def turn_one_body(weight, after, out):
    out[...] = weight[0].reshape(DEPTH, HD).T


def turn_one(layer, weight, after):
    return call(
        turn_one_body,
        shape((HD, DEPTH)),
        weight,
        after,
        specs=[pl.BlockSpec((1, 64, QUARTER, HD), lambda i: (layer, 0, 0, 0)), ANY],
    )


def turn_kv_body(weight, bias, out):
    for layer in range(LAYERS):
        out[layer, :, :DEPTH] = weight[layer].reshape(DEPTH, QUARTER).T
        out[layer, :, DEPTH:] = jnp.broadcast_to(bias[:, layer : layer + 1], (QUARTER, HD))


def bundle_body(wide, narrow, after, out):
    out[:HD, :] = wide[0]
    out[HD:, :] = narrow[0, :, :DEPTH]


def bundle(layer, wide, narrow, after):
    return call(
        bundle_body,
        shape((IN, DEPTH)),
        wide,
        narrow,
        after,
        specs=[of_layer(layer, HD, DEPTH), of_layer(layer, QUARTER, DEPTH + HD), ANY],
    )


def of_layer(layer, rows, depth, at=0):
    return pl.BlockSpec((1, rows, depth), lambda i: (layer, 0, at))


def from_groups(own):
    mine = [own] + [lax.ppermute(own, "grp", G_DOWN[k]) for k in (1, 2, 3)]
    return mine, [lax.ppermute(w, "tp", CORE_SWAP) for w in mine]


def init_body(where, hidden, mine, theirs):
    c = where[3]
    mine[...] = hidden[0, half_lanes(c), :].astype(F32).T.astype(BF)
    theirs[...] = hidden[0, half_lanes(1 - c), :].astype(F32).T.astype(BF)


def spread_body(where, own, other, columns, first, second, third, fourth, tall, sums):
    g = where[4]
    values = [own[...].astype(F32), other[...].astype(F32)]
    for dc in range(2):
        scaled = (values[dc] * columns[:, 4 * dc : 4 * dc + 1]).astype(BF)
        tall[:, dc] = scaled.reshape(4, QUARTER, PART)
    for i in range(4):
        rows = slice(i * QUARTER, (i + 1) * QUARTER)
        squares = values[0][rows] * values[0][rows] + values[1][rows] * values[1][rows]
        sums[i] = pack_ss(jnp.sum(squares, axis=0, keepdims=True))
    for k, out in enumerate((first, second, third, fourth)):
        at = (g + k) & 3
        out[0:QUARTER, :] = tall[at, 0]
        out[QUARTER : 2 * QUARTER, :] = tall[at, 1]
        out[2 * QUARTER :, :] = sums[at]


def join_body(first, second, third, fourth, out):
    sums = []
    for slot, ref in enumerate((first, second, third, fourth)):
        out[slot * 64 : slot * 64 + 64, :] = ref[0:64, :]
        sums.append(ref[64:80, :].astype(F32)[0:3])
    sums.append(jnp.zeros((4, PART), F32))
    out[ROWS:, :] = jnp.concatenate(sums, axis=0).astype(BF)


def gather(block):
    other = lax.ppermute(block, "tp", Z_SWAP)
    both = jnp.stack([block, other])
    across = lax.ppermute(both, "tp", FIRST[2])
    up = lax.ppermute(both, "tp", FIRST[1])
    down = lax.ppermute(both, "tp", FIRST[3])
    line = jnp.stack([both, up, across, down])
    up = lax.ppermute(line, "tp", SECOND[1])
    down = lax.ppermute(line, "tp", SECOND[3])
    across_a = lax.ppermute(up[:2], "tp", SECOND[1])
    across_b = lax.ppermute(down[2:], "tp", SECOND[3])
    return line, up, across_a, across_b, down


def arrivals(where, refs):
    x, z, y, c = where[0], where[1], where[2], where[3]
    line, up, across_a, across_b, down = refs
    for second in range(4):
        for first in range(4):
            if second == 2:
                ref, at = (across_a, first) if first < 2 else (across_b, first - 2)
            else:
                ref, at = (line, up, None, down)[second], first
            col = (x + jnp.where(c == 0, first, second)) & 3
            row = (y + jnp.where(c == 0, second, first)) & 3
            for dz in range(2):
                yield (col * 2 + (z ^ dz)) * 4 + row, ref, at, dz


def block_rows(where, pair, dc):
    start = (2 * pair + (where[3] ^ dc)) * QUARTER
    return pl.ds(pl.multiple_of(start, QUARTER), QUARTER)


def place_quarters(where, blocks, placed):
    g = where[4]
    ss = jnp.zeros((1, PART), F32)
    for pair, ref, at, dz in arrivals(where, blocks):
        for dc in range(2):
            rows = block_rows(where, pair, dc)
            for k in range(GRP):
                start = pl.multiple_of(dc * HD + ((g + k) & 3) * QUARTER, QUARTER)
                placed[k, rows, :] = ref[at, dz, pl.ds(start, QUARTER), :]
        if ref.shape[2] > ROWS:
            ss = ss + unpack_ss(ref[at, dz, ROWS : ROWS + 16, :])
    return ss


def multiply_quarters(own, other, weight, placed, rows):
    out = jnp.zeros((2 * rows, PART), F32)
    for k in range(GRP):
        weight[k, :rows, :] = own[k][...]
        weight[k, rows:, :] = other[k][...]
        out = out + jnp.dot(weight[k], placed[k], preferred_element_type=F32)
    return out


def partial_in_body(where, *refs):
    blocks = refs[0:5]
    own, own_kv, other, other_kv = refs[5:9]
    keep, sends, (weight, placed) = refs[9], refs[10:13], refs[13:]
    for base, wide, narrow in ((0, own, own_kv), (IN, other, other_kv)):
        weight[base : base + HD, :] = wide[0]
        weight[base + HD : base + IN, :] = narrow[0, :, :DEPTH]
    ss = [jnp.zeros((1, PART), F32) for _ in range(GRP)]
    for pair, ref, at, dz in arrivals(where, blocks):
        sums = ref[at, dz, ROWS : ROWS + 16, :].astype(F32)
        for slot in range(GRP):
            lanes = slice(slot * PART, (slot + 1) * PART)
            for dc in range(2):
                start = slot * 64 + dc * QUARTER
                placed[block_rows(where, pair, dc), lanes] = ref[
                    at, dz, start : start + QUARTER, :
                ]
            for i in range(3):
                ss[slot] = ss[slot] + sums[3 * slot + i : 3 * slot + i + 1]
    out = jnp.dot(weight[...], placed[...], preferred_element_type=F32)
    keep[0 : 2 * IN, :] = out[:, :PART]
    keep[2 * IN :, :] = jnp.broadcast_to(ss[0], (8, PART))
    for k, send in enumerate(sends, start=1):
        send[0 : 2 * IN, :] = out[:, k * PART : (k + 1) * PART].astype(BF)
        send[2 * IN :, :] = pack_ss(ss[k])


def finish(where, rows, scale, columns, layer, bias, cosine, sine, q, kv):
    c = where[3]
    half = half_lanes(c)
    cos, sin = cosine[:, half], sine[:, half]
    for dc in range(2):
        base = dc * IN
        lane = 4 * dc + 2 + layer
        value = rows[base : base + HD] * scale + columns[:, lane : lane + 1]
        q[:, dc * PART : (dc + 1) * PART] = rotated(value, cos, sin)
        column = bias[dc][0, :, 0:1].astype(F32)
        value = rows[base + HD : base + IN] * scale + column
        kv[c if dc == 0 else 1 - c] = value.astype(BF)


def reduced_in_body(where, keep, a, b, c, columns, bias, other_bias, cosine, sine, q, kv):
    rows = keep[...]
    sums, ss = rows[: 2 * IN], rows[2 * IN : 2 * IN + 1]
    for ref in (a, b, c):
        sums = sums + ref[0 : 2 * IN, :].astype(F32)
        ss = ss + unpack_ss(ref[2 * IN :, :])
    scale = lax.rsqrt(ss / D + 1e-06)
    finish(where, sums, scale, columns, 0, (bias, other_bias), cosine, sine, q, kv)


def whole_in_body(layer, where, *refs):
    blocks, own, other = refs[0:5], refs[5:9], refs[9:13]
    columns, bias, other_bias, cosine, sine, q, kv, weight, placed = refs[13:]
    ss = place_quarters(where, blocks, placed)
    out = multiply_quarters(own, other, weight, placed, IN)
    scale = lax.rsqrt(ss / D + 1e-06)
    finish(where, out, scale, columns, layer, (bias, other_bias), cosine, sine, q, kv)


def in_specs_after(layer):
    bias = of_layer(layer, QUARTER, HD, DEPTH // HD)
    return [VM, bias, bias, VM, VM]


IN_OUTS = [shape((HD, 2 * PART)), shape((2, QUARTER, PART))]


def attend_body(where, length, q, own, other, cosine, sine, out, raw, keys, vals):
    y, c = where[2], where[3]
    for ref, half in ((own, half_lanes(c)), (other, half_lanes(1 - c))):
        for i in range(4):
            rows = slice(i * QUARTER, (i + 1) * QUARTER)
            slot = (i - y) & 3
            raw[rows, half] = ref[slot, 0]
            vals[rows, half] = ref[slot, 1]
    keys[...] = rotated(raw[...].astype(F32), cosine[...], sine[...])
    scores = lax.dot_general(
        keys[...], q[...], (((0,), (0,)), ((), ())), preferred_element_type=F32
    ) / jnp.sqrt(jnp.float32(HD))
    s_at = lax.broadcasted_iota(jnp.int32, (TOK, TOK), 0)
    t_at = (lax.broadcasted_iota(jnp.int32, (TOK, TOK), 1) & (PART - 1)) + c * PART
    allowed = (s_at <= t_at) & (s_at < length[0])
    scores = jnp.where(allowed, scores, -1e30)
    weights = jnp.exp(scores - jnp.max(scores, axis=0, keepdims=True))
    probs = (weights / jnp.sum(weights, axis=0, keepdims=True)).astype(BF)
    attended = jnp.dot(vals[...], probs, preferred_element_type=F32).astype(BF)
    out[0:HD, :] = attended[:, :PART]
    out[HD:, :] = attended[:, PART:]


def whole_out_body(layer, where, *refs):
    blocks, own, other = refs[0:5], refs[5:9], refs[9:13]
    x_own, x_other, columns = refs[13:16]
    outs, (weight, placed) = refs[16:-2], refs[-2:]
    place_quarters(where, blocks, placed)
    mixed = multiply_quarters(own, other, weight, placed, HD)
    new = []
    for dc, x in enumerate((x_own, x_other)):
        value = (x[...].astype(F32) + mixed[dc * HD : (dc + 1) * HD]).astype(BF)
        outs[dc][...] = value
        new.append(value.astype(F32))
    if layer < LAYERS - 1:
        squares = jnp.zeros((HD, PART), F32)
        for dc in range(2):
            lane = 4 * dc + layer + 1
            scaled = new[dc] * columns[:, lane : lane + 1]
            outs[2][dc * HD : (dc + 1) * HD, :] = scaled.astype(BF)
            squares = squares + new[dc] * new[dc]
        outs[2][ROWS:, :] = pack_ss(jnp.sum(squares, axis=0, keepdims=True))


def final_body(where, mine, theirs, out):
    c = where[3]
    out[0, half_lanes(c), :] = mine[...].astype(F32).T.astype(BF)
    out[0, half_lanes(1 - c), :] = theirs[...].astype(F32).T.astype(BF)


def local(hidden, lengths, norm_gain, q_weight, q_bias, kv_weight, kv_bias, out_weight):
    tp = lax.axis_index("tp").astype(jnp.int32)
    g = lax.axis_index("grp").astype(jnp.int32)
    where = jnp.stack([tp // 16, (tp // 8) % 2, (tp // 2) % 4, tp % 2, g, g, g, g])

    tile = shape((HD, PART))
    x_own, theirs = call(init_body, [tile, tile], where, hidden, specs=[SM, VM])
    x_other = lax.ppermute(theirs, "tp", CORE_SWAP)
    lines = jnp.concatenate([norm_gain, q_bias.astype(F32)])
    columns = jnp.concatenate([lines, lax.ppermute(lines, "tp", CORE_SWAP)]).T
    piece = shape((80, PART))
    pieces = call(
        spread_body,
        [piece] * 4,
        where,
        x_own,
        x_other,
        columns,
        specs=[SM, VM, VM, VM],
        scratch=[pltpu.VMEM((4, 2, QUARTER, PART), BF), pltpu.VMEM((4, 16, PART), BF)],
    )
    slots = [pieces[0]] + [lax.ppermute(pieces[k], "grp", G_UP[k]) for k in (1, 2, 3)]
    block = call(join_body, shape((ROWS + 16, PART)), *slots)

    kv_turned = call(
        turn_kv_body, shape((LAYERS, QUARTER, DEPTH + HD)), kv_weight, kv_bias.T
    )
    kv_own = lax.ppermute(kv_turned, "tp", KV_MOVE)
    kv_other = lax.ppermute(kv_own, "tp", CORE_SWAP)
    q_own = call(turn_body, shape((LAYERS, HD, DEPTH)), q_weight)
    q_other = lax.ppermute(q_own, "tp", CORE_SWAP)

    inv = 1.0 / 1000000.0 ** (jnp.arange(HD // 2, dtype=F32) * 2.0 / HD)
    angle = inv[:, None] * jnp.arange(TOK, dtype=F32)[None, :]
    cosine, sine = jnp.cos(angle), jnp.sin(angle)

    out_own, out_other = from_groups(turn_one(0, out_weight, block))
    in_own, in_other = None, None

    for layer in range(LAYERS):
        blocks = gather(block)
        if layer == 0:
            send = shape((2 * IN + 16, PART))
            keep, *sends = call(
                partial_in_body,
                [shape((2 * IN + 8, PART), F32), send, send, send],
                where,
                *blocks,
                q_own,
                kv_own,
                q_other,
                kv_other,
                specs=[SM] + [VM] * 5
                + [of_layer(0, HD, DEPTH), of_layer(0, QUARTER, DEPTH + HD)] * 2,
                scratch=[pltpu.VMEM((2 * IN, DEPTH), BF), pltpu.VMEM((DEPTH, WIDE), BF)],
                flops=4 * IN * DEPTH * WIDE,
                nbytes=5 << 20,
            )
            arrived = [lax.ppermute(sends[k - 1], "grp", G_DOWN[k]) for k in (1, 2, 3)]
            q, kv = call(
                reduced_in_body,
                IN_OUTS,
                where,
                keep,
                *arrived,
                columns,
                kv_own,
                kv_other,
                cosine,
                sine,
                specs=[SM] + [VM] * 4 + in_specs_after(0),
            )
            in_own, in_other = from_groups(bundle(1, q_own, kv_own, q))
            next_own, next_other = from_groups(turn_one(1, out_weight, in_own[2]))
        else:
            q, kv = call(
                functools.partial(whole_in_body, layer),
                IN_OUTS,
                where,
                *blocks,
                *in_own,
                *in_other,
                columns,
                kv_own,
                kv_other,
                cosine,
                sine,
                specs=[SM] + [VM] * 13 + in_specs_after(layer),
                scratch=[
                    pltpu.VMEM((GRP, 2 * IN, DEPTH), BF),
                    pltpu.VMEM((GRP, DEPTH, PART), BF),
                ],
                flops=4 * IN * DEPTH * WIDE,
                nbytes=10 << 20,
            )
        kvs = jnp.stack([kv] + [lax.ppermute(kv, "tp", Y_SLOT[s]) for s in (1, 2, 3)])
        block = call(
            attend_body,
            shape((ROWS, PART)),
            where,
            lengths,
            q,
            kvs,
            lax.ppermute(kvs, "tp", CORE_SWAP),
            cosine,
            sine,
            specs=[SM, SM] + [VM] * 5,
            scratch=[pltpu.VMEM((HD, TOK), BF)] * 3,
            flops=4 * TOK * TOK * HD,
        )
        blocks = gather(block)
        last = layer == LAYERS - 1
        outs = call(
            functools.partial(whole_out_body, layer),
            [tile, tile] + ([] if last else [shape((ROWS + 16, PART))]),
            where,
            *blocks,
            *out_own,
            *out_other,
            x_own,
            x_other,
            columns,
            specs=[SM] + [VM] * 16,
            scratch=[
                pltpu.VMEM((GRP, ROWS, DEPTH), BF),
                pltpu.VMEM((GRP, DEPTH, PART), BF),
            ],
            flops=4 * HD * DEPTH * WIDE,
            nbytes=8 << 20,
        )
        if not last:
            x_own, x_other, block = outs
            out_own, out_other = next_own, next_other
    mine, theirs = outs
    theirs = lax.ppermute(theirs, "tp", CORE_SWAP)
    return call(final_body, shape((1, TOK, HD)), where, mine, theirs, specs=[SM, VM, VM])


def solution(mesh):
    placed = (
        P("grp", None, "tp"),
        P("grp"),
        P(None, "tp"),
        P(None, None, "grp", "tp"),
        P(None, "tp"),
        P(None, None, "grp", "tp"),
        P(None, "tp"),
        P(None, None, "grp", "tp"),
    )
    return jax.shard_map(
        local, mesh=mesh, in_specs=placed, out_specs=P("grp", None, "tp"), check_vma=False
    )
```

```python
import functools

import jax
import jax.numpy as jnp
from jax import lax
from jax.experimental import pallas as pl
from jax.experimental.pallas import tpu as pltpu
from jax.sharding import PartitionSpec as P

D = 8192
HD = 128
LAYERS = 2
TOK = 256
GRP = 4
QUARTER = HD // GRP
PART = TOK // 2
WIDE = GRP * PART
DEPTH = 64 * QUARTER
IN = HD + QUARTER
SOON = HD // 2
ROWS = 2 * HD
BF = jnp.bfloat16
F32 = jnp.float32

VM = pl.BlockSpec(memory_space=pltpu.VMEM)
SM = pl.BlockSpec(memory_space=pltpu.SMEM)
ANY = pl.BlockSpec(memory_space=pl.ANY)
PARAMS = pltpu.CompilerParams(vmem_limit_bytes=40 * 1024 * 1024)


def tp_index(x, z, y, c):
    return ((x * 2 + z) * 4 + y) * 2 + c


COORDS = [
    (x, z, y, c) for x in range(4) for z in range(2) for y in range(4) for c in range(2)
]


def tp_perm(move):
    return [(tp_index(*at), tp_index(*move(*at))) for at in COORDS]


def along(x_first, s):
    def move(x, z, y, c):
        if (c == 0) == x_first:
            return ((x - s) % 4, z, y, c)
        return (x, z, (y - s) % 4, c)

    return tp_perm(move)


CORE_SWAP = tp_perm(lambda x, z, y, c: (x, z, y, 1 - c))
Z_SWAP = tp_perm(lambda x, z, y, c: (x, 1 - z, y, c))
FIRST = [along(True, s) for s in range(4)]
SECOND = [along(False, s) for s in range(4)]
Y_SLOT = [tp_perm(lambda x, z, y, c, s=s: (x, z, (y - s) % 4, c)) for s in range(4)]
G_UP = [[(g, (g + k) % GRP) for g in range(GRP)] for k in range(GRP)]
G_DOWN = [[(g, (g - k) % GRP) for g in range(GRP)] for k in range(GRP)]
KV_MOVE = [(m, 8 * ((m % 32) // 4) + 2 * (m % 4) + m // 32) for m in range(64)]


def split3(value):
    high = value.astype(BF)
    rest = value - high.astype(F32)
    middle = rest.astype(BF)
    low = (rest - middle.astype(F32)).astype(BF)
    return high, middle, low


def call(body, outs, *args, specs=None, scratch=()):
    return pl.pallas_call(
        body,
        grid=(1,),
        out_shape=outs,
        in_specs=specs or [VM] * len(args),
        out_specs=jax.tree.map(lambda _: VM, outs),
        scratch_shapes=list(scratch),
        compiler_params=PARAMS,
        cost_estimate=pl.CostEstimate(flops=0, bytes_accessed=1 << 10, transcendentals=0),
    )(*args)


def shape(dims, dtype=BF):
    return jax.ShapeDtypeStruct(dims, dtype)


def half_lanes(index):
    return pl.ds(pl.multiple_of(index * PART, PART), PART)


def pack_ss(ss):
    parts = [p.astype(F32) for p in split3(jnp.broadcast_to(ss, (16, ss.shape[1])))]
    row = lax.broadcasted_iota(jnp.int32, parts[0].shape, 0)
    out = jnp.zeros(parts[0].shape, F32)
    for i, part in enumerate(parts):
        out = jnp.where(row == i, part, out)
    return out.astype(BF)


def unpack_ss(rows):
    rows = rows.astype(F32)
    return rows[0:1] + rows[1:2] + rows[2:3]


def rotated(value, cosine, sine):
    first, second = value[:64], value[64:]
    return jnp.concatenate(
        [first * cosine - second * sine, second * cosine + first * sine], axis=0
    ).astype(BF)


def turn_body(weight, out):
    for layer in range(LAYERS):
        out[layer] = weight[layer].reshape(DEPTH, HD).T


def turn_one_body(weight, after, out):
    out[...] = weight[0].reshape(DEPTH, HD).T


def turn_one(layer, weight, after):
    return call(
        turn_one_body,
        shape((HD, DEPTH)),
        weight,
        after,
        specs=[pl.BlockSpec((1, 64, QUARTER, HD), lambda i: (layer, 0, 0, 0)), ANY],
    )


def turn_kv_body(weight, bias, out):
    for layer in range(LAYERS):
        out[layer, :, :DEPTH] = weight[layer].reshape(DEPTH, QUARTER).T
        out[layer, :, DEPTH:] = jnp.broadcast_to(bias[:, layer : layer + 1], (QUARTER, HD))


def soon_body(wide, query, after, out):
    out[:HD, :] = wide[0].reshape(DEPTH, HD).T
    out[HD:, :] = query[0, :SOON, :]


def soon(wide, query, after):
    return call(
        soon_body,
        shape((HD + SOON, DEPTH)),
        wide,
        query,
        after,
        specs=[
            pl.BlockSpec((1, 64, QUARTER, HD), lambda i: (0, 0, 0, 0)),
            of_layer(1, HD, DEPTH),
            ANY,
        ],
    )


def rest_body(query, narrow, after, out):
    out[: HD - SOON, :] = query[0, SOON:, :]
    out[HD - SOON :, :] = narrow[0, :, :DEPTH]


def rest(query, narrow, after):
    return call(
        rest_body,
        shape((IN - SOON, DEPTH)),
        query,
        narrow,
        after,
        specs=[of_layer(1, HD, DEPTH), of_layer(1, QUARTER, DEPTH + HD), ANY],
    )


def of_layer(layer, rows, depth, at=0):
    return pl.BlockSpec((1, rows, depth), lambda i: (layer, 0, at))


def with_other(mine, after):
    mine, _ = lax.optimization_barrier((mine, after))
    return mine, lax.ppermute(mine, "tp", CORE_SWAP)


def init_body(where, hidden, mine, theirs):
    c = where[3]
    mine[...] = hidden[0, half_lanes(c), :].astype(F32).T.astype(BF)
    theirs[...] = hidden[0, half_lanes(1 - c), :].astype(F32).T.astype(BF)


def spread_body(where, own, other, columns, first, second, third, fourth, tall, sums):
    g = where[4]
    values = [own[...].astype(F32), other[...].astype(F32)]
    for dc in range(2):
        scaled = (values[dc] * columns[:, 4 * dc : 4 * dc + 1]).astype(BF)
        tall[:, dc] = scaled.reshape(4, QUARTER, PART)
    for i in range(4):
        rows = slice(i * QUARTER, (i + 1) * QUARTER)
        squares = values[0][rows] * values[0][rows] + values[1][rows] * values[1][rows]
        sums[i] = pack_ss(jnp.sum(squares, axis=0, keepdims=True))
    for k, out in enumerate((first, second, third, fourth)):
        at = (g + k) & 3
        out[0:QUARTER, :] = tall[at, 0]
        out[QUARTER : 2 * QUARTER, :] = tall[at, 1]
        out[2 * QUARTER :, :] = sums[at]


def join_body(first, second, third, fourth, out):
    sums = []
    for slot, ref in enumerate((first, second, third, fourth)):
        out[slot * 64 : slot * 64 + 64, :] = ref[0:64, :]
        sums.append(ref[64:80, :].astype(F32)[0:3])
    sums.append(jnp.zeros((4, PART), F32))
    out[ROWS:, :] = jnp.concatenate(sums, axis=0).astype(BF)


def gather(block):
    other = lax.ppermute(block, "tp", Z_SWAP)
    both = jnp.stack([block, other])
    across = lax.ppermute(both, "tp", FIRST[2])
    up = lax.ppermute(both, "tp", FIRST[1])
    down = lax.ppermute(both, "tp", FIRST[3])
    line = jnp.stack([both, up, across, down])
    up = lax.ppermute(line, "tp", SECOND[1])
    down = lax.ppermute(line, "tp", SECOND[3])
    across_a = lax.ppermute(up[:2], "tp", SECOND[1])
    across_b = lax.ppermute(down[2:], "tp", SECOND[3])
    return (line, up, across_a, across_b, down), both, up


def arrivals(where, refs):
    x, z, y, c = where[0], where[1], where[2], where[3]
    line, up, across_a, across_b, down = refs
    for second in range(4):
        for first in range(4):
            if second == 2:
                ref, at = (across_a, first) if first < 2 else (across_b, first - 2)
            else:
                ref, at = (line, up, None, down)[second], first
            col = (x + jnp.where(c == 0, first, second)) & 3
            row = (y + jnp.where(c == 0, second, first)) & 3
            for dz in range(2):
                yield (col * 2 + (z ^ dz)) * 4 + row, ref, at, dz


def block_rows(where, pair, dc):
    start = (2 * pair + (where[3] ^ dc)) * QUARTER
    return pl.ds(pl.multiple_of(start, QUARTER), QUARTER)


def place_quarters(where, blocks, placed):
    ss = jnp.zeros((1, PART), F32)
    for pair, ref, at, dz in arrivals(where, blocks):
        for dc in range(2):
            rows = block_rows(where, pair, dc)
            for k in range(GRP):
                start = dc * HD + k * QUARTER
                placed[k, rows, :] = ref[at, dz, start : start + QUARTER, :]
        if ref.shape[2] > ROWS:
            ss = ss + unpack_ss(ref[at, dz, ROWS : ROWS + 16, :])
    return ss


def multiply_quarters(parts, weight, placed):
    out = jnp.zeros((weight.shape[1], PART), F32)
    for k in range(GRP):
        base = 0
        for ref in parts:
            weight[k, base : base + ref.shape[1], :] = ref[k]
            base += ref.shape[1]
        out = out + jnp.dot(weight[k], placed[k], preferred_element_type=F32)
    return out


def partial_in_body(where, *refs):
    blocks = refs[0:5]
    own, own_kv, other, other_kv = refs[5:9]
    keep, sends, (weight, placed) = refs[9], refs[10:13], refs[13:]
    for base, wide, narrow in ((0, own, own_kv), (IN, other, other_kv)):
        weight[base : base + HD, :] = wide[0]
        weight[base + HD : base + IN, :] = narrow[0, :, :DEPTH]
    ss = [jnp.zeros((1, PART), F32) for _ in range(GRP)]
    for pair, ref, at, dz in arrivals(where, blocks):
        sums = ref[at, dz, ROWS : ROWS + 16, :].astype(F32)
        for slot in range(GRP):
            lanes = slice(slot * PART, (slot + 1) * PART)
            for dc in range(2):
                start = slot * 64 + dc * QUARTER
                placed[block_rows(where, pair, dc), lanes] = ref[
                    at, dz, start : start + QUARTER, :
                ]
            for i in range(3):
                ss[slot] = ss[slot] + sums[3 * slot + i : 3 * slot + i + 1]
    out = jnp.dot(weight[...], placed[...], preferred_element_type=F32)
    keep[0 : 2 * IN, :] = out[:, :PART]
    keep[2 * IN :, :] = jnp.broadcast_to(ss[0], (8, PART))
    for k, send in enumerate(sends, start=1):
        send[0 : 2 * IN, :] = out[:, k * PART : (k + 1) * PART].astype(BF)
        send[2 * IN :, :] = pack_ss(ss[k])


def finish(where, rows, scale, columns, layer, bias, cosine, sine, q, kv):
    c = where[3]
    half = half_lanes(c)
    cos, sin = cosine[:, half], sine[:, half]
    for dc in range(2):
        base = dc * IN
        lane = 4 * dc + 2 + layer
        value = rows[base : base + HD] * scale + columns[:, lane : lane + 1]
        q[:, dc * PART : (dc + 1) * PART] = rotated(value, cos, sin)
        column = bias[dc][0, :, 0:1].astype(F32)
        value = rows[base + HD : base + IN] * scale + column
        kv[c if dc == 0 else 1 - c] = value.astype(BF)


def reduced_in_body(where, keep, a, b, c, columns, bias, other_bias, cosine, sine, q, kv):
    rows = keep[...]
    sums, ss = rows[: 2 * IN], rows[2 * IN : 2 * IN + 1]
    for ref in (a, b, c):
        sums = sums + ref[0 : 2 * IN, :].astype(F32)
        ss = ss + unpack_ss(ref[2 * IN :, :])
    scale = lax.rsqrt(ss / D + 1e-06)
    finish(where, sums, scale, columns, 0, (bias, other_bias), cosine, sine, q, kv)


def whole_in_body(layer, where, *refs):
    blocks, parts = refs[0:5], refs[5:9]
    columns, bias, other_bias, cosine, sine, q, kv, weight, placed = refs[9:]
    ss = place_quarters(where, blocks, placed)
    out = multiply_quarters(parts, weight, placed)
    scale = lax.rsqrt(ss / D + 1e-06)
    finish(where, out, scale, columns, layer, (bias, other_bias), cosine, sine, q, kv)


SOON_SPEC = pl.BlockSpec((GRP, SOON, DEPTH), lambda i: (0, HD // SOON, 0))
OUT_SPEC = pl.BlockSpec((GRP, HD, DEPTH), lambda i: (0, 0, 0))


def in_specs_after(layer):
    bias = of_layer(layer, QUARTER, HD, DEPTH // HD)
    return [VM, bias, bias, VM, VM]


IN_OUTS = [shape((HD, 2 * PART)), shape((2, QUARTER, PART))]


def attend_body(where, length, q, own, other, cosine, sine, out, raw, keys, vals):
    y, c = where[2], where[3]
    for ref, half in ((own, half_lanes(c)), (other, half_lanes(1 - c))):
        for i in range(4):
            rows = slice(i * QUARTER, (i + 1) * QUARTER)
            slot = (i - y) & 3
            raw[rows, half] = ref[slot, 0]
            vals[rows, half] = ref[slot, 1]
    keys[...] = rotated(raw[...].astype(F32), cosine[...], sine[...])
    scores = lax.dot_general(
        keys[...], q[...], (((0,), (0,)), ((), ())), preferred_element_type=F32
    ) / jnp.sqrt(jnp.float32(HD))
    s_at = lax.broadcasted_iota(jnp.int32, (TOK, TOK), 0)
    t_at = (lax.broadcasted_iota(jnp.int32, (TOK, TOK), 1) & (PART - 1)) + c * PART
    allowed = (s_at <= t_at) & (s_at < length[0])
    scores = jnp.where(allowed, scores, -1e30)
    weights = jnp.exp(scores - jnp.max(scores, axis=0, keepdims=True))
    probs = (weights / jnp.sum(weights, axis=0, keepdims=True)).astype(BF)
    attended = jnp.dot(vals[...], probs, preferred_element_type=F32).astype(BF)
    out[0:HD, :] = attended[:, :PART]
    out[HD:, :] = attended[:, PART:]


def whole_out_body(layer, where, *refs):
    blocks, parts = refs[0:5], refs[5:7]
    x_own, x_other, columns = refs[7:10]
    outs, (weight, placed) = refs[10:-2], refs[-2:]
    place_quarters(where, blocks, placed)
    mixed = multiply_quarters(parts, weight, placed)
    new = []
    for dc, x in enumerate((x_own, x_other)):
        value = (x[...].astype(F32) + mixed[dc * HD : (dc + 1) * HD]).astype(BF)
        outs[dc][...] = value
        new.append(value.astype(F32))
    if layer < LAYERS - 1:
        squares = jnp.zeros((HD, PART), F32)
        for dc in range(2):
            lane = 4 * dc + layer + 1
            scaled = new[dc] * columns[:, lane : lane + 1]
            outs[2][dc * HD : (dc + 1) * HD, :] = scaled.astype(BF)
            squares = squares + new[dc] * new[dc]
        outs[2][ROWS:, :] = pack_ss(jnp.sum(squares, axis=0, keepdims=True))


def final_body(where, mine, theirs, out):
    c = where[3]
    out[0, half_lanes(c), :] = mine[...].astype(F32).T.astype(BF)
    out[0, half_lanes(1 - c), :] = theirs[...].astype(F32).T.astype(BF)


def local(hidden, lengths, norm_gain, q_weight, q_bias, kv_weight, kv_bias, out_weight):
    tp = lax.axis_index("tp").astype(jnp.int32)
    g = lax.axis_index("grp").astype(jnp.int32)
    where = jnp.stack([tp // 16, (tp // 8) % 2, (tp // 2) % 4, tp % 2, g, g, g, g])

    tile = shape((HD, PART))
    x_own, theirs = call(init_body, [tile, tile], where, hidden, specs=[SM, VM])
    x_other = lax.ppermute(theirs, "tp", CORE_SWAP)
    lines = jnp.concatenate([norm_gain, q_bias.astype(F32)])
    columns = jnp.concatenate([lines, lax.ppermute(lines, "tp", CORE_SWAP)]).T
    piece = shape((80, PART))
    pieces = call(
        spread_body,
        [piece] * 4,
        where,
        x_own,
        x_other,
        columns,
        specs=[SM, VM, VM, VM],
        scratch=[pltpu.VMEM((4, 2, QUARTER, PART), BF), pltpu.VMEM((4, 16, PART), BF)],
    )
    slots = [pieces[0]] + [lax.ppermute(pieces[k], "grp", G_UP[k]) for k in (1, 2, 3)]
    kv_turned = call(
        turn_kv_body, shape((LAYERS, QUARTER, DEPTH + HD)), kv_weight, kv_bias.T
    )
    kv_own = lax.ppermute(kv_turned, "tp", KV_MOVE)
    q_own = call(turn_body, shape((LAYERS, HD, DEPTH)), q_weight)
    soon_all = lax.all_gather(soon(out_weight, q_own, slots[1]), "grp")
    *slots, kv_own = lax.optimization_barrier((*slots, kv_own))
    kv_other = lax.ppermute(kv_own, "tp", CORE_SWAP)
    block = call(join_body, shape((ROWS + 16, PART)), *slots)
    q_other = lax.ppermute(q_own, "tp", CORE_SWAP)

    inv = 1.0 / 1000000.0 ** (jnp.arange(HD // 2, dtype=F32) * 2.0 / HD)
    angle = inv[:, None] * jnp.arange(TOK, dtype=F32)[None, :]
    cosine, sine = jnp.cos(angle), jnp.sin(angle)

    for layer in range(LAYERS):
        if layer == 0:
            blocks, _, _ = gather(block)
            send = shape((2 * IN + 16, PART))
            keep, *sends = call(
                partial_in_body,
                [shape((2 * IN + 8, PART), F32), send, send, send],
                where,
                *blocks,
                q_own,
                kv_own,
                q_other,
                kv_other,
                specs=[SM] + [VM] * 5
                + [of_layer(0, HD, DEPTH), of_layer(0, QUARTER, DEPTH + HD)] * 2,
                scratch=[pltpu.VMEM((2 * IN, DEPTH), BF), pltpu.VMEM((DEPTH, WIDE), BF)],
            )
            arrived = [lax.ppermute(sends[k - 1], "grp", G_DOWN[k]) for k in (1, 2, 3)]
            q, kv = call(
                reduced_in_body,
                IN_OUTS,
                where,
                keep,
                *arrived,
                columns,
                kv_own,
                kv_other,
                cosine,
                sine,
                specs=[SM] + [VM] * 4 + in_specs_after(0),
            )
        else:
            blocks, _, late = gather(block)
            rest_own, rest_other = with_other(rest_all, late)
            q, kv = call(
                functools.partial(whole_in_body, layer),
                IN_OUTS,
                where,
                *blocks,
                soon_own,
                rest_own,
                soon_other,
                rest_other,
                columns,
                kv_own,
                kv_other,
                cosine,
                sine,
                specs=[SM] + [VM] * 5 + [SOON_SPEC, VM] * 2 + in_specs_after(layer),
                scratch=[
                    pltpu.VMEM((GRP, 2 * IN, DEPTH), BF),
                    pltpu.VMEM((GRP, DEPTH, PART), BF),
                ],
            )
        kvs = jnp.stack([kv] + [lax.ppermute(kv, "tp", Y_SLOT[s]) for s in (1, 2, 3)])
        block = call(
            attend_body,
            shape((ROWS, PART)),
            where,
            lengths,
            q,
            kvs,
            lax.ppermute(kvs, "tp", CORE_SWAP),
            cosine,
            sine,
            specs=[SM, SM] + [VM] * 5,
            scratch=[pltpu.VMEM((HD, TOK), BF)] * 3,
        )
        if layer == 0:
            block, soon_all = lax.optimization_barrier((block, soon_all))
            rest_all = lax.all_gather(rest(q_own, kv_own, block), "grp")
            last_all = lax.all_gather(turn_one(1, out_weight, block), "grp")
            blocks, both, _ = gather(block)
            soon_own, soon_other = with_other(soon_all, both)
            out_own, out_other = soon_own, soon_other
        else:
            blocks, _, late = gather(block)
            out_own, out_other = with_other(last_all, late)
        last = layer == LAYERS - 1
        outs = call(
            functools.partial(whole_out_body, layer),
            [tile, tile] + ([] if last else [shape((ROWS + 16, PART))]),
            where,
            *blocks,
            out_own,
            out_other,
            x_own,
            x_other,
            columns,
            specs=[SM] + [VM] * 5 + [OUT_SPEC] * 2 + [VM] * 3,
            scratch=[
                pltpu.VMEM((GRP, ROWS, DEPTH), BF),
                pltpu.VMEM((GRP, DEPTH, PART), BF),
            ],
        )
        if not last:
            x_own, x_other, block = outs
    mine, theirs = outs
    theirs = lax.ppermute(theirs, "tp", CORE_SWAP)
    return call(final_body, shape((1, TOK, HD)), where, mine, theirs, specs=[SM, VM, VM])


def solution(mesh):
    placed = (
        P("grp", None, "tp"),
        P("grp"),
        P(None, "tp"),
        P(None, None, "grp", "tp"),
        P(None, "tp"),
        P(None, None, "grp", "tp"),
        P(None, "tp"),
        P(None, None, "grp", "tp"),
    )
    return jax.shard_map(
        local, mesh=mesh, in_specs=placed, out_specs=P("grp", None, "tp"), check_vma=False
    )
```

```python
import functools

import jax
import jax.numpy as jnp
from jax import lax
from jax.experimental import pallas as pl
from jax.experimental.pallas import tpu as pltpu
from jax.sharding import PartitionSpec as P

D = 8192
HD = 128
LAYERS = 2
TOK = 256
GRP = 4
QUARTER = HD // GRP
PART = TOK // 2
WIDE = GRP * PART
DEPTH = 64 * QUARTER
IN = HD + QUARTER
ROWS = 2 * HD
BF = jnp.bfloat16
F32 = jnp.float32

VM = pl.BlockSpec(memory_space=pltpu.VMEM)
SM = pl.BlockSpec(memory_space=pltpu.SMEM)
ANY = pl.BlockSpec(memory_space=pl.ANY)
PARAMS = pltpu.CompilerParams(vmem_limit_bytes=40 * 1024 * 1024)


def tp_index(x, z, y, c):
    return ((x * 2 + z) * 4 + y) * 2 + c


COORDS = [
    (x, z, y, c) for x in range(4) for z in range(2) for y in range(4) for c in range(2)
]


def tp_perm(move):
    return [(tp_index(*at), tp_index(*move(*at))) for at in COORDS]


def along(x_first, s):
    def move(x, z, y, c):
        if (c == 0) == x_first:
            return ((x - s) % 4, z, y, c)
        return (x, z, (y - s) % 4, c)

    return tp_perm(move)


CORE_SWAP = tp_perm(lambda x, z, y, c: (x, z, y, 1 - c))
Z_SWAP = tp_perm(lambda x, z, y, c: (x, 1 - z, y, c))
FIRST = [along(True, s) for s in range(4)]
SECOND = [along(False, s) for s in range(4)]
Y_SLOT = [tp_perm(lambda x, z, y, c, s=s: (x, z, (y - s) % 4, c)) for s in range(4)]
G_UP = [[(g, (g + k) % GRP) for g in range(GRP)] for k in range(GRP)]
G_DOWN = [[(g, (g - k) % GRP) for g in range(GRP)] for k in range(GRP)]
KV_MOVE = [(m, 8 * ((m % 32) // 4) + 2 * (m % 4) + m // 32) for m in range(64)]


def split3(value):
    high = value.astype(BF)
    rest = value - high.astype(F32)
    middle = rest.astype(BF)
    low = (rest - middle.astype(F32)).astype(BF)
    return high, middle, low


def call(body, outs, *args, specs=None, scratch=()):
    return pl.pallas_call(
        body,
        grid=(1,),
        out_shape=outs,
        in_specs=specs or [VM] * len(args),
        out_specs=jax.tree.map(lambda _: VM, outs),
        scratch_shapes=list(scratch),
        compiler_params=PARAMS,
        cost_estimate=pl.CostEstimate(flops=0, bytes_accessed=1 << 10, transcendentals=0),
    )(*args)


def shape(dims, dtype=BF):
    return jax.ShapeDtypeStruct(dims, dtype)


def half_lanes(index):
    return pl.ds(pl.multiple_of(index * PART, PART), PART)


def pack_ss(ss):
    parts = [p.astype(F32) for p in split3(jnp.broadcast_to(ss, (16, ss.shape[1])))]
    row = lax.broadcasted_iota(jnp.int32, parts[0].shape, 0)
    out = jnp.zeros(parts[0].shape, F32)
    for i, part in enumerate(parts):
        out = jnp.where(row == i, part, out)
    return out.astype(BF)


def unpack_ss(rows):
    rows = rows.astype(F32)
    return rows[0:1] + rows[1:2] + rows[2:3]


def rotated(value, cosine, sine):
    first, second = value[:64], value[64:]
    return jnp.concatenate(
        [first * cosine - second * sine, second * cosine + first * sine], axis=0
    ).astype(BF)


def turn_body(weight, out):
    for layer in range(LAYERS):
        out[layer] = weight[layer].reshape(DEPTH, HD).T


def turn_one_body(weight, after, out):
    out[...] = weight[0].reshape(DEPTH, HD).T


def turn_one(layer, weight, after):
    return call(
        turn_one_body,
        shape((HD, DEPTH)),
        weight,
        after,
        specs=[pl.BlockSpec((1, 64, QUARTER, HD), lambda i: (layer, 0, 0, 0)), ANY],
    )


def turn_kv_body(weight, bias, out):
    for layer in range(LAYERS):
        out[layer, :, :DEPTH] = weight[layer].reshape(DEPTH, QUARTER).T
        out[layer, :, DEPTH:] = jnp.broadcast_to(bias[:, layer : layer + 1], (QUARTER, HD))


def bundle_body(wide, narrow, after, out):
    out[:HD, :] = wide[0]
    out[HD:, :] = narrow[0, :, :DEPTH]


def bundle(layer, wide, narrow, after):
    return call(
        bundle_body,
        shape((IN, DEPTH)),
        wide,
        narrow,
        after,
        specs=[of_layer(layer, HD, DEPTH), of_layer(layer, QUARTER, DEPTH + HD), ANY],
    )


def of_layer(layer, rows, depth, at=0):
    return pl.BlockSpec((1, rows, depth), lambda i: (layer, 0, at))


def with_other(mine, after):
    mine, *_ = lax.optimization_barrier((mine, *after))
    return mine, lax.ppermute(mine, "tp", CORE_SWAP)


def init_body(where, hidden, mine, theirs):
    c = where[3]
    mine[...] = hidden[0, half_lanes(c), :].astype(F32).T.astype(BF)
    theirs[...] = hidden[0, half_lanes(1 - c), :].astype(F32).T.astype(BF)


def spread_body(where, own, other, columns, first, second, third, fourth, tall, sums):
    g = where[4]
    values = [own[...].astype(F32), other[...].astype(F32)]
    for dc in range(2):
        scaled = (values[dc] * columns[:, 4 * dc : 4 * dc + 1]).astype(BF)
        tall[:, dc] = scaled.reshape(4, QUARTER, PART)
    for i in range(4):
        rows = slice(i * QUARTER, (i + 1) * QUARTER)
        squares = values[0][rows] * values[0][rows] + values[1][rows] * values[1][rows]
        sums[i] = pack_ss(jnp.sum(squares, axis=0, keepdims=True))
    for k, out in enumerate((first, second, third, fourth)):
        at = (g + k) & 3
        out[0:QUARTER, :] = tall[at, 0]
        out[QUARTER : 2 * QUARTER, :] = tall[at, 1]
        out[2 * QUARTER :, :] = sums[at]


def join_body(first, second, third, fourth, out):
    sums = []
    for slot, ref in enumerate((first, second, third, fourth)):
        out[slot * 64 : slot * 64 + 64, :] = ref[0:64, :]
        sums.append(ref[64:80, :].astype(F32)[0:3])
    sums.append(jnp.zeros((4, PART), F32))
    out[ROWS:, :] = jnp.concatenate(sums, axis=0).astype(BF)


def gather(block):
    other = lax.ppermute(block, "tp", Z_SWAP)
    both = jnp.stack([block, other])
    up = lax.ppermute(both, "tp", FIRST[1])
    across = lax.ppermute(both, "tp", FIRST[2])
    down = lax.ppermute(both, "tp", FIRST[3])
    up, across, down = lax.optimization_barrier((up, across, down))
    low, high = jnp.stack([both, up]), jnp.stack([across, down])
    low_up = lax.ppermute(low, "tp", SECOND[1])
    high_down = lax.ppermute(high, "tp", SECOND[3])
    high_up = lax.ppermute(high, "tp", SECOND[1])
    low_down = lax.ppermute(low, "tp", SECOND[3])
    low_across = lax.ppermute(low_up, "tp", SECOND[1])
    high_across = lax.ppermute(high_down, "tp", SECOND[3])
    blocks = (low, high, low_up, high_up, low_across, high_across, low_down, high_down)
    return blocks, blocks[2:], both


def arrivals(where, refs):
    x, z, y, c = where[0], where[1], where[2], where[3]
    for second in range(4):
        for first in range(4):
            ref, at = refs[2 * second + first // 2], first % 2
            col = (x + jnp.where(c == 0, first, second)) & 3
            row = (y + jnp.where(c == 0, second, first)) & 3
            for dz in range(2):
                yield (col * 2 + (z ^ dz)) * 4 + row, ref, at, dz


def block_rows(where, pair, dc):
    start = (2 * pair + (where[3] ^ dc)) * QUARTER
    return pl.ds(pl.multiple_of(start, QUARTER), QUARTER)


def place_quarters(where, blocks, placed):
    ss = jnp.zeros((1, PART), F32)
    for pair, ref, at, dz in arrivals(where, blocks):
        for dc in range(2):
            rows = block_rows(where, pair, dc)
            for k in range(GRP):
                start = dc * HD + k * QUARTER
                placed[k, rows, :] = ref[at, dz, start : start + QUARTER, :]
        if ref.shape[2] > ROWS:
            ss = ss + unpack_ss(ref[at, dz, ROWS : ROWS + 16, :])
    return ss


def multiply_quarters(parts, weight, placed):
    out = jnp.zeros((weight.shape[1], PART), F32)
    for k in range(GRP):
        base = 0
        for ref in parts:
            weight[k, base : base + ref.shape[1], :] = ref[k]
            base += ref.shape[1]
        out = out + jnp.dot(weight[k], placed[k], preferred_element_type=F32)
    return out


def partial_in_body(where, *refs):
    blocks = refs[0:8]
    own, own_kv, other, other_kv = refs[8:12]
    keep, sends, (weight, placed) = refs[12], refs[13:16], refs[16:]
    for base, wide, narrow in ((0, own, own_kv), (IN, other, other_kv)):
        weight[base : base + HD, :] = wide[0]
        weight[base + HD : base + IN, :] = narrow[0, :, :DEPTH]
    ss = [jnp.zeros((1, PART), F32) for _ in range(GRP)]
    for pair, ref, at, dz in arrivals(where, blocks):
        sums = ref[at, dz, ROWS : ROWS + 16, :].astype(F32)
        for slot in range(GRP):
            lanes = slice(slot * PART, (slot + 1) * PART)
            for dc in range(2):
                start = slot * 64 + dc * QUARTER
                placed[block_rows(where, pair, dc), lanes] = ref[
                    at, dz, start : start + QUARTER, :
                ]
            for i in range(3):
                ss[slot] = ss[slot] + sums[3 * slot + i : 3 * slot + i + 1]
    out = jnp.dot(weight[...], placed[...], preferred_element_type=F32)
    keep[0 : 2 * IN, :] = out[:, :PART]
    keep[2 * IN :, :] = jnp.broadcast_to(ss[0], (8, PART))
    for k, send in enumerate(sends, start=1):
        send[0 : 2 * IN, :] = out[:, k * PART : (k + 1) * PART].astype(BF)
        send[2 * IN :, :] = pack_ss(ss[k])


def finish(where, rows, scale, columns, layer, bias, cosine, sine, q, kv):
    c = where[3]
    half = half_lanes(c)
    cos, sin = cosine[:, half], sine[:, half]
    for dc in range(2):
        base = dc * IN
        lane = 4 * dc + 2 + layer
        value = rows[base : base + HD] * scale + columns[:, lane : lane + 1]
        q[:, dc * PART : (dc + 1) * PART] = rotated(value, cos, sin)
        column = bias[dc][0, :, 0:1].astype(F32)
        value = rows[base + HD : base + IN] * scale + column
        kv[c if dc == 0 else 1 - c] = value.astype(BF)


def reduced_in_body(where, keep, a, b, c, columns, bias, other_bias, cosine, sine, q, kv):
    rows = keep[...]
    sums, ss = rows[: 2 * IN], rows[2 * IN : 2 * IN + 1]
    for ref in (a, b, c):
        sums = sums + ref[0 : 2 * IN, :].astype(F32)
        ss = ss + unpack_ss(ref[2 * IN :, :])
    scale = lax.rsqrt(ss / D + 1e-06)
    finish(where, sums, scale, columns, 0, (bias, other_bias), cosine, sine, q, kv)


def whole_in_body(layer, where, *refs):
    blocks, parts = refs[0:8], refs[8:10]
    columns, bias, other_bias, cosine, sine, q, kv, weight, placed = refs[10:]
    ss = place_quarters(where, blocks, placed)
    out = multiply_quarters(parts, weight, placed)
    scale = lax.rsqrt(ss / D + 1e-06)
    finish(where, out, scale, columns, layer, (bias, other_bias), cosine, sine, q, kv)


def in_specs_after(layer):
    bias = of_layer(layer, QUARTER, HD, DEPTH // HD)
    return [VM, bias, bias, VM, VM]


IN_OUTS = [shape((HD, 2 * PART)), shape((2, QUARTER, PART))]


def attend_body(where, length, q, own, other, cosine, sine, out, raw, keys, vals):
    y, c = where[2], where[3]
    for ref, half in ((own, half_lanes(c)), (other, half_lanes(1 - c))):
        for i in range(4):
            rows = slice(i * QUARTER, (i + 1) * QUARTER)
            slot = (i - y) & 3
            raw[rows, half] = ref[slot, 0]
            vals[rows, half] = ref[slot, 1]
    keys[...] = rotated(raw[...].astype(F32), cosine[...], sine[...])
    scores = lax.dot_general(
        keys[...], q[...], (((0,), (0,)), ((), ())), preferred_element_type=F32
    ) / jnp.sqrt(jnp.float32(HD))
    s_at = lax.broadcasted_iota(jnp.int32, (TOK, TOK), 0)
    t_at = (lax.broadcasted_iota(jnp.int32, (TOK, TOK), 1) & (PART - 1)) + c * PART
    allowed = (s_at <= t_at) & (s_at < length[0])
    scores = jnp.where(allowed, scores, -1e30)
    weights = jnp.exp(scores - jnp.max(scores, axis=0, keepdims=True))
    probs = (weights / jnp.sum(weights, axis=0, keepdims=True)).astype(BF)
    attended = jnp.dot(vals[...], probs, preferred_element_type=F32).astype(BF)
    out[0:HD, :] = attended[:, :PART]
    out[HD:, :] = attended[:, PART:]


def whole_out_body(layer, where, *refs):
    blocks, parts = refs[0:8], refs[8:10]
    x_own, x_other, columns = refs[10:13]
    outs, (weight, placed) = refs[13:-2], refs[-2:]
    place_quarters(where, blocks, placed)
    mixed = multiply_quarters(parts, weight, placed)
    new = []
    for dc, x in enumerate((x_own, x_other)):
        value = (x[...].astype(F32) + mixed[dc * HD : (dc + 1) * HD]).astype(BF)
        outs[dc][...] = value
        new.append(value.astype(F32))
    if layer < LAYERS - 1:
        squares = jnp.zeros((HD, PART), F32)
        for dc in range(2):
            lane = 4 * dc + layer + 1
            scaled = new[dc] * columns[:, lane : lane + 1]
            outs[2][dc * HD : (dc + 1) * HD, :] = scaled.astype(BF)
            squares = squares + new[dc] * new[dc]
        outs[2][ROWS:, :] = pack_ss(jnp.sum(squares, axis=0, keepdims=True))


def final_body(where, mine, theirs, out):
    c = where[3]
    out[0, half_lanes(c), :] = mine[...].astype(F32).T.astype(BF)
    out[0, half_lanes(1 - c), :] = theirs[...].astype(F32).T.astype(BF)


def local(hidden, lengths, norm_gain, q_weight, q_bias, kv_weight, kv_bias, out_weight):
    tp = lax.axis_index("tp").astype(jnp.int32)
    g = lax.axis_index("grp").astype(jnp.int32)
    where = jnp.stack([tp // 16, (tp // 8) % 2, (tp // 2) % 4, tp % 2, g, g, g, g])

    tile = shape((HD, PART))
    x_own, theirs = call(init_body, [tile, tile], where, hidden, specs=[SM, VM])
    x_other = lax.ppermute(theirs, "tp", CORE_SWAP)
    lines = jnp.concatenate([norm_gain, q_bias.astype(F32)])
    columns = jnp.concatenate([lines, lax.ppermute(lines, "tp", CORE_SWAP)]).T
    piece = shape((80, PART))
    pieces = call(
        spread_body,
        [piece] * 4,
        where,
        x_own,
        x_other,
        columns,
        specs=[SM, VM, VM, VM],
        scratch=[pltpu.VMEM((4, 2, QUARTER, PART), BF), pltpu.VMEM((4, 16, PART), BF)],
    )
    slots = [pieces[0]] + [lax.ppermute(pieces[k], "grp", G_UP[k]) for k in (1, 2, 3)]
    kv_turned = call(
        turn_kv_body, shape((LAYERS, QUARTER, DEPTH + HD)), kv_weight, kv_bias.T
    )
    kv_own = lax.ppermute(kv_turned, "tp", KV_MOVE)
    *slots, kv_own = lax.optimization_barrier((*slots, kv_own))
    kv_other = lax.ppermute(kv_own, "tp", CORE_SWAP)
    block = call(join_body, shape((ROWS + 16, PART)), *slots)
    q_own = call(turn_body, shape((LAYERS, HD, DEPTH)), q_weight)
    q_other = lax.ppermute(q_own, "tp", CORE_SWAP)

    inv = 1.0 / 1000000.0 ** (jnp.arange(HD // 2, dtype=F32) * 2.0 / HD)
    angle = inv[:, None] * jnp.arange(TOK, dtype=F32)[None, :]
    cosine, sine = jnp.cos(angle), jnp.sin(angle)

    for layer in range(LAYERS):
        if layer == 0:
            blocks, _, both = gather(block)
            out_all = lax.all_gather(turn_one(0, out_weight, both), "grp")
            send = shape((2 * IN + 16, PART))
            keep, *sends = call(
                partial_in_body,
                [shape((2 * IN + 8, PART), F32), send, send, send],
                where,
                *blocks,
                q_own,
                kv_own,
                q_other,
                kv_other,
                specs=[SM] + [VM] * 8
                + [of_layer(0, HD, DEPTH), of_layer(0, QUARTER, DEPTH + HD)] * 2,
                scratch=[pltpu.VMEM((2 * IN, DEPTH), BF), pltpu.VMEM((DEPTH, WIDE), BF)],
            )
            arrived = [lax.ppermute(sends[k - 1], "grp", G_DOWN[k]) for k in (1, 2, 3)]
            q, kv = call(
                reduced_in_body,
                IN_OUTS,
                where,
                keep,
                *arrived,
                columns,
                kv_own,
                kv_other,
                cosine,
                sine,
                specs=[SM] + [VM] * 4 + in_specs_after(0),
            )
        else:
            blocks, late, _ = gather(block)
            in_own, in_other = with_other(in_all, late)
            q, kv = call(
                functools.partial(whole_in_body, layer),
                IN_OUTS,
                where,
                *blocks,
                in_own,
                in_other,
                columns,
                kv_own,
                kv_other,
                cosine,
                sine,
                specs=[SM] + [VM] * 10 + in_specs_after(layer),
                scratch=[
                    pltpu.VMEM((GRP, 2 * IN, DEPTH), BF),
                    pltpu.VMEM((GRP, DEPTH, PART), BF),
                ],
            )
        if layer == 0:
            out_own, out_other = with_other(out_all, (q,))
            in_all = lax.all_gather(bundle(1, q_own, kv_own, q), "grp")
            last_all = lax.all_gather(turn_one(1, out_weight, q), "grp")
        kvs = jnp.stack([kv] + [lax.ppermute(kv, "tp", Y_SLOT[s]) for s in (1, 2, 3)])
        block = call(
            attend_body,
            shape((ROWS, PART)),
            where,
            lengths,
            q,
            kvs,
            lax.ppermute(kvs, "tp", CORE_SWAP),
            cosine,
            sine,
            specs=[SM, SM] + [VM] * 5,
            scratch=[pltpu.VMEM((HD, TOK), BF)] * 3,
        )
        blocks, late, _ = gather(block)
        if layer == LAYERS - 1:
            out_own, out_other = with_other(last_all, late)
        last = layer == LAYERS - 1
        outs = call(
            functools.partial(whole_out_body, layer),
            [tile, tile] + ([] if last else [shape((ROWS + 16, PART))]),
            where,
            *blocks,
            out_own,
            out_other,
            x_own,
            x_other,
            columns,
            specs=[SM] + [VM] * 13,
            scratch=[
                pltpu.VMEM((GRP, ROWS, DEPTH), BF),
                pltpu.VMEM((GRP, DEPTH, PART), BF),
            ],
        )
        if not last:
            x_own, x_other, block = outs
    mine, theirs = outs
    theirs = lax.ppermute(theirs, "tp", CORE_SWAP)
    return call(final_body, shape((1, TOK, HD)), where, mine, theirs, specs=[SM, VM, VM])


def solution(mesh):
    placed = (
        P("grp", None, "tp"),
        P("grp"),
        P(None, "tp"),
        P(None, None, "grp", "tp"),
        P(None, "tp"),
        P(None, None, "grp", "tp"),
        P(None, "tp"),
        P(None, None, "grp", "tp"),
    )
    return jax.shard_map(
        local, mesh=mesh, in_specs=placed, out_specs=P("grp", None, "tp"), check_vma=False
    )
```

```python
import functools

import jax
import jax.numpy as jnp
from jax import lax
from jax.experimental import pallas as pl
from jax.experimental.pallas import tpu as pltpu
from jax.sharding import PartitionSpec as P

D = 8192
HD = 128
LAYERS = 2
TOK = 256
GRP = 4
QUARTER = HD // GRP
PART = TOK // 2
WIDE = GRP * PART
DEPTH = 64 * QUARTER
IN = HD + QUARTER
ROWS = 2 * HD
BF = jnp.bfloat16
F32 = jnp.float32

VM = pl.BlockSpec(memory_space=pltpu.VMEM)
SM = pl.BlockSpec(memory_space=pltpu.SMEM)
ANY = pl.BlockSpec(memory_space=pl.ANY)
PARAMS = pltpu.CompilerParams(vmem_limit_bytes=40 * 1024 * 1024)


def tp_index(x, z, y, c):
    return ((x * 2 + z) * 4 + y) * 2 + c


COORDS = [
    (x, z, y, c) for x in range(4) for z in range(2) for y in range(4) for c in range(2)
]


def tp_perm(move):
    return [(tp_index(*at), tp_index(*move(*at))) for at in COORDS]


def along(x_first, s):
    def move(x, z, y, c):
        if (c == 0) == x_first:
            return ((x - s) % 4, z, y, c)
        return (x, z, (y - s) % 4, c)

    return tp_perm(move)


CORE_SWAP = tp_perm(lambda x, z, y, c: (x, z, y, 1 - c))
Z_SWAP = tp_perm(lambda x, z, y, c: (x, 1 - z, y, c))
FIRST = [along(True, s) for s in range(4)]
SECOND = [along(False, s) for s in range(4)]
Y_SLOT = [tp_perm(lambda x, z, y, c, s=s: (x, z, (y - s) % 4, c)) for s in range(4)]
WORK_SWAP = [(g, g ^ 1) for g in range(GRP)]
WEIGHT_SWAP = [(g, g ^ 2) for g in range(GRP)]
KV_MOVE = [(m, 8 * ((m % 32) // 4) + 2 * (m % 4) + m // 32) for m in range(64)]


def split3(value):
    high = value.astype(BF)
    rest = value - high.astype(F32)
    middle = rest.astype(BF)
    low = (rest - middle.astype(F32)).astype(BF)
    return high, middle, low


def call(body, outs, *args, specs=None, scratch=()):
    return pl.pallas_call(
        body,
        grid=(1,),
        out_shape=outs,
        in_specs=specs or [VM] * len(args),
        out_specs=jax.tree.map(lambda _: VM, outs),
        scratch_shapes=list(scratch),
        compiler_params=PARAMS,
        cost_estimate=pl.CostEstimate(flops=0, bytes_accessed=1 << 10, transcendentals=0),
    )(*args)


def shape(dims, dtype=BF):
    return jax.ShapeDtypeStruct(dims, dtype)


def half_lanes(index):
    return pl.ds(pl.multiple_of(index * PART, PART), PART)


def pack_ss(ss):
    parts = [p.astype(F32) for p in split3(jnp.broadcast_to(ss, (16, ss.shape[1])))]
    row = lax.broadcasted_iota(jnp.int32, parts[0].shape, 0)
    out = jnp.zeros(parts[0].shape, F32)
    for i, part in enumerate(parts):
        out = jnp.where(row == i, part, out)
    return out.astype(BF)


def unpack_ss(rows):
    rows = rows.astype(F32)
    return rows[0:1] + rows[1:2] + rows[2:3]


def rotated(value, cosine, sine):
    first, second = value[:64], value[64:]
    return jnp.concatenate(
        [first * cosine - second * sine, second * cosine + first * sine], axis=0
    ).astype(BF)


def turn_body(weight, first, second):
    for layer, out in enumerate((first, second)):
        out[...] = weight[layer].reshape(DEPTH, HD).T


def turn(weight):
    return call(turn_body, [shape((HD, DEPTH))] * 2, weight)


def turn_kv_body(weight, bias, out):
    for layer in range(LAYERS):
        out[layer, :, :DEPTH] = weight[layer].reshape(DEPTH, QUARTER).T
        out[layer, :, DEPTH:] = jnp.broadcast_to(bias[:, layer : layer + 1], (QUARTER, HD))


def of_layer(layer, rows, depth, at=0):
    return pl.BlockSpec((1, rows, depth), lambda i: (layer, 0, at))


def both_quarters(own, after, late):
    held, _ = lax.optimization_barrier((own, after))
    partner = lax.ppermute(held, "grp", WEIGHT_SWAP)
    here, *_ = lax.optimization_barrier((partner, *late))
    return [
        own,
        partner,
        lax.ppermute(own, "tp", CORE_SWAP),
        lax.ppermute(here, "tp", CORE_SWAP),
    ]


def rows_at(prompt, dc, qi):
    start = ((prompt * 2 + dc) * 2 + qi) * QUARTER
    return slice(start, start + QUARTER)


def share(where, tall, keep, send):
    g = where[4]
    for dc in range(2):
        for qi in range(2):
            keep[rows_at(0, dc, qi), :] = tall[dc, g ^ (2 * qi)]
            send[rows_at(0, dc, qi), :] = tall[dc, (g ^ 1) ^ (2 * qi)]


def init_body(where, hidden, mine, theirs):
    c = where[3]
    mine[...] = hidden[0, half_lanes(c), :].astype(F32).T.astype(BF)
    theirs[...] = hidden[0, half_lanes(1 - c), :].astype(F32).T.astype(BF)


def spread_body(where, own, other, keep, send, tall):
    tall[0] = own[...].reshape(GRP, QUARTER, PART)
    tall[1] = other[...].reshape(GRP, QUARTER, PART)
    share(where, tall, keep, send)


def emit_block(layer, where, values, columns, block):
    g = where[4]
    sums = []
    for prompt in range(2):
        squares = jnp.zeros((QUARTER, PART), F32)
        for dc in range(2):
            for qi in range(2):
                rows = rows_at(prompt, dc, qi)
                start = pl.multiple_of((g ^ (2 * qi)) * QUARTER, QUARTER)
                lane = 4 * dc + layer
                gain = columns[pl.ds(start, QUARTER), lane : lane + 1]
                value = values[rows]
                block[rows, :] = (value * gain).astype(BF)
                squares = squares + value * value
        ss = jnp.sum(squares, axis=0, keepdims=True)
        sums += [p.astype(F32) for p in split3(jnp.broadcast_to(ss, (8, PART)))]
    tile = jnp.concatenate([p[0:1] for p in sums] + [jnp.zeros((10, PART), F32)], axis=0)
    block[ROWS:, :] = tile.astype(BF)


def join_body(where, keep, came, columns, x, block):
    x[: ROWS // 2, :] = keep[...]
    x[ROWS // 2 :, :] = came[...]
    emit_block(0, where, x[...].astype(F32), columns, block)


def gather(block, early=None):
    other = lax.ppermute(block, "tp", Z_SWAP)
    if early is not None:
        other, early = lax.optimization_barrier((other, early))
    both = jnp.stack([block, other])
    up = lax.ppermute(both, "tp", FIRST[1])
    across = lax.ppermute(both, "tp", FIRST[2])
    down = lax.ppermute(both, "tp", FIRST[3])
    up, across, down = lax.optimization_barrier((up, across, down))
    low, high = jnp.stack([both, up]), jnp.stack([across, down])
    low_up = lax.ppermute(low, "tp", SECOND[1])
    high_down = lax.ppermute(high, "tp", SECOND[3])
    high_up = lax.ppermute(high, "tp", SECOND[1])
    low_down = lax.ppermute(low, "tp", SECOND[3])
    low_across = lax.ppermute(low_up, "tp", SECOND[1])
    high_across = lax.ppermute(high_down, "tp", SECOND[3])
    blocks = (low, high, low_up, high_up, low_across, high_across, low_down, high_down)
    return blocks, both, blocks[2:], early


def arrivals(where, refs):
    x, z, y, c = where[0], where[1], where[2], where[3]
    for second in range(4):
        for first in range(4):
            ref, at = refs[2 * second + first // 2], first % 2
            col = (x + jnp.where(c == 0, first, second)) & 3
            row = (y + jnp.where(c == 0, second, first)) & 3
            for dz in range(2):
                yield (col * 2 + (z ^ dz)) * 4 + row, ref, at, dz


def block_rows(where, pair, dc):
    start = (2 * pair + (where[3] ^ dc)) * QUARTER
    return pl.ds(pl.multiple_of(start, QUARTER), QUARTER)


def place(where, blocks, placed):
    ss = [jnp.zeros((1, PART), F32) for _ in range(2)]
    for pair, ref, at, dz in arrivals(where, blocks):
        for prompt in range(2):
            lanes = slice(prompt * PART, (prompt + 1) * PART)
            for dc in range(2):
                for qi in range(2):
                    placed[qi, block_rows(where, pair, dc), lanes] = ref[
                        at, dz, rows_at(prompt, dc, qi), :
                    ]
        if ref.shape[2] > ROWS:
            sums = ref[at, dz, ROWS : ROWS + 16, :].astype(F32)
            for i in range(6):
                ss[i // 3] = ss[i // 3] + sums[i : i + 1]
    return ss


def pack_ss(ss):
    parts = [p.astype(F32) for p in split3(jnp.broadcast_to(ss, (16, ss.shape[1])))]
    row = lax.broadcasted_iota(jnp.int32, parts[0].shape, 0)
    out = jnp.zeros(parts[0].shape, F32)
    for i, part in enumerate(parts):
        out = jnp.where(row == i, part, out)
    return out.astype(BF)


def unpack_ss(rows):
    rows = rows.astype(F32)
    return rows[0:1] + rows[1:2] + rows[2:3]


def rotated(value, cosine, sine):
    first, second = value[:64], value[64:]
    return jnp.concatenate(
        [first * cosine - second * sine, second * cosine + first * sine], axis=0
    ).astype(BF)


def partial_in_body(where, *refs):
    blocks, wide, narrow = refs[0:8], refs[8:12], refs[12:16]
    keep, send, weight, placed = refs[16:]
    ss = place(where, blocks, placed)
    out = jnp.zeros((2 * IN, 2 * PART), F32)
    for qi in range(2):
        for dc in range(2):
            weight[qi, dc * IN : dc * IN + HD, :] = wide[2 * dc + qi][...]
            weight[qi, dc * IN + HD : (dc + 1) * IN, :] = narrow[2 * dc + qi][0, :, :DEPTH]
        out = out + jnp.dot(weight[qi], placed[qi], preferred_element_type=F32)
    keep[0 : 2 * IN, :] = out[:, :PART]
    keep[2 * IN :, :] = jnp.broadcast_to(ss[0], (8, PART))
    send[0 : 2 * IN, :] = out[:, PART:].astype(BF)
    send[2 * IN :, :] = pack_ss(ss[1])


def finish(where, rows, scale, columns, layer, bias, cosine, sine, q, kv):
    c = where[3]
    half = half_lanes(c)
    cos, sin = cosine[:, half], sine[:, half]
    for dc in range(2):
        base = dc * IN
        lane = 4 * dc + 2 + layer
        value = rows[base : base + HD] * scale + columns[:, lane : lane + 1]
        q[:, dc * PART : (dc + 1) * PART] = rotated(value, cos, sin)
        column = bias[dc][0, :, 0:1].astype(F32)
        value = rows[base + HD : base + IN] * scale + column
        kv[c if dc == 0 else 1 - c] = value.astype(BF)


def reduced_in_body(layer, where, keep, came, columns, *refs):
    bias, other_bias, cosine, sine, q, kv = refs
    rows = keep[...]
    sums = rows[: 2 * IN] + came[0 : 2 * IN, :].astype(F32)
    ss = rows[2 * IN : 2 * IN + 1] + unpack_ss(came[2 * IN :, :])
    scale = lax.rsqrt(ss / D + 1e-06)
    finish(where, sums, scale, columns, layer, (bias, other_bias), cosine, sine, q, kv)


def attend_body(
    where, length, q, own, other, cosine, sine, keep, send, raw, keys, vals, tall
):
    y, c = where[2], where[3]
    for ref, half in ((own, half_lanes(c)), (other, half_lanes(1 - c))):
        for i in range(4):
            rows = slice(i * QUARTER, (i + 1) * QUARTER)
            slot = (i - y) & 3
            raw[rows, half] = ref[slot, 0]
            vals[rows, half] = ref[slot, 1]
    keys[...] = rotated(raw[...].astype(F32), cosine[...], sine[...])
    scores = lax.dot_general(
        keys[...], q[...], (((0,), (0,)), ((), ())), preferred_element_type=F32
    ) / jnp.sqrt(jnp.float32(HD))
    s_at = lax.broadcasted_iota(jnp.int32, (TOK, TOK), 0)
    t_at = (lax.broadcasted_iota(jnp.int32, (TOK, TOK), 1) & (PART - 1)) + c * PART
    allowed = (s_at <= t_at) & (s_at < length[0])
    scores = jnp.where(allowed, scores, -1e30)
    weights = jnp.exp(scores - jnp.max(scores, axis=0, keepdims=True))
    probs = (weights / jnp.sum(weights, axis=0, keepdims=True)).astype(BF)
    attended = jnp.dot(vals[...], probs, preferred_element_type=F32).astype(BF)
    for dc in range(2):
        part = attended[:, dc * PART : (dc + 1) * PART]
        tall[dc] = part.reshape(GRP, QUARTER, PART)
    share(where, tall, keep, send)


def multiply_out(where, blocks, parts, weight, placed, total):
    place(where, blocks, placed)
    out = jnp.zeros((ROWS, 2 * PART), F32)
    for qi in range(2):
        for dc in range(2):
            weight[qi, dc * HD : (dc + 1) * HD, :] = parts[2 * dc + qi][...]
        out = out + jnp.dot(weight[qi], placed[qi], preferred_element_type=F32)
    total[...] = out


def partial_out_body(where, *refs):
    blocks, parts = refs[0:8], refs[8:12]
    keep, send, weight, placed, total = refs[12:]
    g = where[4]
    multiply_out(where, blocks, parts, weight, placed, total)
    for prompt in range(2):
        lanes = slice(prompt * PART, (prompt + 1) * PART)
        for dc in range(2):
            for qi in range(2):
                here = pl.multiple_of(dc * HD + (g ^ (2 * qi)) * QUARTER, QUARTER)
                there = pl.multiple_of(dc * HD + ((g ^ 1) ^ (2 * qi)) * QUARTER, QUARTER)
                keep[rows_at(prompt, dc, qi), :] = total[pl.ds(here, QUARTER), lanes]
                sent = total[pl.ds(there, QUARTER), lanes].astype(BF)
                send[rows_at(1 - prompt, dc, qi), :] = sent


def advance_body(layer, where, x, keep, came, columns, new, block):
    value = x[...].astype(F32) + (keep[...] + came[...].astype(F32))
    new[...] = value.astype(BF)
    emit_block(layer, where, new[...].astype(F32), columns, block)


def last_out_body(where, *refs):
    blocks, parts, x = refs[0:8], refs[8:12], refs[12]
    keep, send, weight, placed, total = refs[13:]
    multiply_out(where, blocks, parts, weight, placed, total)
    keep[...] = total[:, :PART]
    send[:ROWS, :] = total[:, PART:].astype(BF)
    send[ROWS:, :] = x[ROWS // 2 :, :]


def total_body(where, x, keep, came, mine, theirs, tall):
    g = where[4]
    for dc in range(2):
        for qi in range(2):
            tall[dc, g ^ (2 * qi)] = x[rows_at(0, dc, qi), :]
            at = rows_at(0, dc, qi)
            tall[dc, (g ^ 1) ^ (2 * qi)] = came[ROWS + at.start : ROWS + at.stop, :]
    for dc, out in enumerate((mine, theirs)):
        rows = slice(dc * HD, (dc + 1) * HD)
        mixed = keep[rows, :] + came[rows, :].astype(F32)
        out[...] = (tall[dc].reshape(HD, PART).astype(F32) + mixed).astype(BF)


def final_body(where, mine, theirs, out):
    c = where[3]
    out[0, half_lanes(c), :] = mine[...].astype(F32).T.astype(BF)
    out[0, half_lanes(1 - c), :] = theirs[...].astype(F32).T.astype(BF)


def local(hidden, lengths, norm_gain, q_weight, q_bias, kv_weight, kv_bias, out_weight):
    tp = lax.axis_index("tp").astype(jnp.int32)
    g = lax.axis_index("grp").astype(jnp.int32)
    where = jnp.stack([tp // 16, (tp // 8) % 2, (tp // 2) % 4, tp % 2, g, g, g, g])

    tile = shape((HD, PART))
    quarters = pltpu.VMEM((2, GRP, QUARTER, PART), BF)
    x_own, theirs = call(init_body, [tile, tile], where, hidden, specs=[SM, VM])
    x_other = lax.ppermute(theirs, "tp", CORE_SWAP)
    lines = jnp.concatenate([norm_gain, q_bias.astype(F32)])
    columns = jnp.concatenate([lines, lax.ppermute(lines, "tp", CORE_SWAP)]).T
    keep, send = call(
        spread_body,
        [tile, tile],
        where,
        x_own,
        x_other,
        specs=[SM, VM, VM],
        scratch=[quarters],
    )
    x, block = call(
        join_body,
        [shape((ROWS, PART)), shape((ROWS + 16, PART))],
        where,
        keep,
        lax.ppermute(send, "grp", WORK_SWAP),
        columns,
        specs=[SM] + [VM] * 3,
    )

    kv_turned = call(
        turn_kv_body, shape((LAYERS, QUARTER, DEPTH + HD)), kv_weight, kv_bias.T
    )
    kv_own = lax.ppermute(kv_turned, "tp", KV_MOVE)
    q_turned = turn(q_weight)
    out_turned = turn(out_weight)

    inv = 1.0 / 1000000.0 ** (jnp.arange(HD // 2, dtype=F32) * 2.0 / HD)
    angle = inv[:, None] * jnp.arange(TOK, dtype=F32)[None, :]
    cosine, sine = jnp.cos(angle), jnp.sin(angle)

    narrow = None
    for layer in range(LAYERS):
        if layer == 0:
            blocks, both, late, kv_own = gather(block, kv_own)
            narrow = both_quarters(kv_own, both, late)
        else:
            blocks, both, late, _ = gather(block)
        wide = both_quarters(q_turned[layer], both, late)
        keep, send = call(
            partial_in_body,
            [shape((2 * IN + 8, PART), F32), shape((2 * IN + 16, PART))],
            where,
            *blocks,
            *wide,
            *narrow,
            specs=[SM] + [VM] * 12 + [of_layer(layer, QUARTER, DEPTH + HD)] * 4,
            scratch=[
                pltpu.VMEM((2, 2 * IN, DEPTH), BF),
                pltpu.VMEM((2, DEPTH, 2 * PART), BF),
            ],
        )
        bias = of_layer(layer, QUARTER, HD, DEPTH // HD)
        q, kv = call(
            functools.partial(reduced_in_body, layer),
            [shape((HD, 2 * PART)), shape((2, QUARTER, PART))],
            where,
            keep,
            lax.ppermute(send, "grp", WORK_SWAP),
            columns,
            narrow[0],
            narrow[2],
            cosine,
            sine,
            specs=[SM] + [VM] * 3 + [bias, bias, VM, VM],
        )
        kvs = jnp.stack([kv] + [lax.ppermute(kv, "tp", Y_SLOT[s]) for s in (1, 2, 3)])
        keep, send = call(
            attend_body,
            [tile, tile],
            where,
            lengths,
            q,
            kvs,
            lax.ppermute(kvs, "tp", CORE_SWAP),
            cosine,
            sine,
            specs=[SM, SM] + [VM] * 5,
            scratch=[pltpu.VMEM((HD, TOK), BF)] * 3 + [quarters],
        )
        block = jnp.concatenate([keep, lax.ppermute(send, "grp", WORK_SWAP)])
        blocks, both, late, _ = gather(block)
        wide = both_quarters(out_turned[layer], both, late)
        scratch = [
            pltpu.VMEM((2, ROWS, DEPTH), BF),
            pltpu.VMEM((2, DEPTH, 2 * PART), BF),
            pltpu.VMEM((ROWS, 2 * PART), F32),
        ]
        if layer < LAYERS - 1:
            keep, send = call(
                partial_out_body,
                [shape((ROWS, PART), F32), shape((ROWS, PART))],
                where,
                *blocks,
                *wide,
                specs=[SM] + [VM] * 12,
                scratch=scratch,
            )
            x, block = call(
                functools.partial(advance_body, layer + 1),
                [shape((ROWS, PART)), shape((ROWS + 16, PART))],
                where,
                x,
                keep,
                lax.ppermute(send, "grp", WORK_SWAP),
                columns,
                specs=[SM] + [VM] * 4,
            )
    keep, send = call(
        last_out_body,
        [shape((ROWS, PART), F32), shape((ROWS + HD, PART))],
        where,
        *blocks,
        *wide,
        x,
        specs=[SM] + [VM] * 13,
        scratch=scratch,
    )
    mine, theirs = call(
        total_body,
        [tile, tile],
        where,
        x,
        keep,
        lax.ppermute(send, "grp", WORK_SWAP),
        specs=[SM] + [VM] * 3,
        scratch=[quarters],
    )
    theirs = lax.ppermute(theirs, "tp", CORE_SWAP)
    return call(final_body, shape((1, TOK, HD)), where, mine, theirs, specs=[SM, VM, VM])


def solution(mesh):
    placed = (
        P("grp", None, "tp"),
        P("grp"),
        P(None, "tp"),
        P(None, None, "grp", "tp"),
        P(None, "tp"),
        P(None, None, "grp", "tp"),
        P(None, "tp"),
        P(None, None, "grp", "tp"),
    )
    return jax.shard_map(
        local, mesh=mesh, in_specs=placed, out_specs=P("grp", None, "tp"), check_vma=False
    )
```

```python
import functools

import jax
import jax.numpy as jnp
from jax import lax
from jax.experimental import pallas as pl
from jax.experimental.pallas import tpu as pltpu
from jax.sharding import PartitionSpec as P

D = 8192
HD = 128
LAYERS = 2
TOK = 256
GRP = 4
QUARTER = HD // GRP
PART = TOK // 2
WIDE = GRP * PART
DEPTH = 64 * QUARTER
IN = HD + QUARTER
ROWS = 2 * HD
BF = jnp.bfloat16
F32 = jnp.float32

VM = pl.BlockSpec(memory_space=pltpu.VMEM)
SM = pl.BlockSpec(memory_space=pltpu.SMEM)
ANY = pl.BlockSpec(memory_space=pl.ANY)
PARAMS = pltpu.CompilerParams(vmem_limit_bytes=40 * 1024 * 1024)


def tp_index(x, z, y, c):
    return ((x * 2 + z) * 4 + y) * 2 + c


COORDS = [
    (x, z, y, c) for x in range(4) for z in range(2) for y in range(4) for c in range(2)
]


def tp_perm(move):
    return [(tp_index(*at), tp_index(*move(*at))) for at in COORDS]


def along(x_first, s):
    def move(x, z, y, c):
        if (c == 0) == x_first:
            return ((x - s) % 4, z, y, c)
        return (x, z, (y - s) % 4, c)

    return tp_perm(move)


CORE_SWAP = tp_perm(lambda x, z, y, c: (x, z, y, 1 - c))
Z_SWAP = tp_perm(lambda x, z, y, c: (x, 1 - z, y, c))
FIRST = [along(True, s) for s in range(4)]
SECOND = [along(False, s) for s in range(4)]
Y_SLOT = [tp_perm(lambda x, z, y, c, s=s: (x, z, (y - s) % 4, c)) for s in range(4)]
WORK_SWAP = [(g, g ^ 1) for g in range(GRP)]
SECOND_STEP = [(g, g ^ 3) for g in range(GRP)]
KV_MOVE = [(m, 8 * ((m % 32) // 4) + 2 * (m % 4) + m // 32) for m in range(64)]
KV_PARTNER = [(64 * g + m, 64 * (g ^ 2) + to) for g in range(GRP) for m, to in KV_MOVE]


def split3(value):
    high = value.astype(BF)
    rest = value - high.astype(F32)
    middle = rest.astype(BF)
    low = (rest - middle.astype(F32)).astype(BF)
    return high, middle, low


def call(body, outs, *args, specs=None, scratch=()):
    return pl.pallas_call(
        body,
        grid=(1,),
        out_shape=outs,
        in_specs=specs or [VM] * len(args),
        out_specs=jax.tree.map(lambda _: VM, outs),
        scratch_shapes=list(scratch),
        compiler_params=PARAMS,
        cost_estimate=pl.CostEstimate(flops=0, bytes_accessed=1 << 10, transcendentals=0),
    )(*args)


def shape(dims, dtype=BF):
    return jax.ShapeDtypeStruct(dims, dtype)


def half_lanes(index):
    return pl.ds(pl.multiple_of(index * PART, PART), PART)


def pack_ss(ss):
    parts = [p.astype(F32) for p in split3(jnp.broadcast_to(ss, (16, ss.shape[1])))]
    row = lax.broadcasted_iota(jnp.int32, parts[0].shape, 0)
    out = jnp.zeros(parts[0].shape, F32)
    for i, part in enumerate(parts):
        out = jnp.where(row == i, part, out)
    return out.astype(BF)


def unpack_ss(rows):
    rows = rows.astype(F32)
    return rows[0:1] + rows[1:2] + rows[2:3]


def rotated(value, cosine, sine):
    first, second = value[:64], value[64:]
    return jnp.concatenate(
        [first * cosine - second * sine, second * cosine + first * sine], axis=0
    ).astype(BF)


def turn_body(weight, first, second):
    for layer, out in enumerate((first, second)):
        out[...] = weight[layer].reshape(DEPTH, HD).T


def turn(weight):
    return call(turn_body, [shape((HD, DEPTH))] * 2, weight)


def turn_kv_body(weight, bias, *outs):
    for layer, out in enumerate(outs):
        out[:, :DEPTH] = weight[layer].reshape(DEPTH, QUARTER).T
        out[:, DEPTH:] = jnp.broadcast_to(bias[:, layer : layer + 1], (QUARTER, HD))


BIAS = pl.BlockSpec((QUARTER, HD), lambda i: (0, DEPTH // HD))


def with_other(own, partner):
    return [
        own,
        partner,
        lax.ppermute(own, "tp", CORE_SWAP),
        lax.ppermute(partner, "tp", CORE_SWAP),
    ]


def rows_at(prompt, dc, qi):
    start = ((prompt * 2 + dc) * 2 + qi) * QUARTER
    return slice(start, start + QUARTER)


def share(where, tall, keep, send):
    g = where[4]
    for dc in range(2):
        for qi in range(2):
            keep[rows_at(0, dc, qi), :] = tall[dc, g ^ (2 * qi)]
            send[rows_at(0, dc, qi), :] = tall[dc, (g ^ 1) ^ (2 * qi)]


def init_body(where, hidden, mine, theirs):
    c = where[3]
    mine[...] = hidden[0, half_lanes(c), :].astype(F32).T.astype(BF)
    theirs[...] = hidden[0, half_lanes(1 - c), :].astype(F32).T.astype(BF)


def spread_body(where, own, other, keep, send, tall):
    tall[0] = own[...].reshape(GRP, QUARTER, PART)
    tall[1] = other[...].reshape(GRP, QUARTER, PART)
    share(where, tall, keep, send)


def emit_block(layer, where, values, columns, block):
    g = where[4]
    sums = []
    for prompt in range(2):
        squares = jnp.zeros((QUARTER, PART), F32)
        for dc in range(2):
            for qi in range(2):
                rows = rows_at(prompt, dc, qi)
                start = pl.multiple_of((g ^ (2 * qi)) * QUARTER, QUARTER)
                lane = 4 * dc + layer
                gain = columns[pl.ds(start, QUARTER), lane : lane + 1]
                value = values[rows]
                block[rows, :] = (value * gain).astype(BF)
                squares = squares + value * value
        ss = jnp.sum(squares, axis=0, keepdims=True)
        sums += [p.astype(F32) for p in split3(jnp.broadcast_to(ss, (8, PART)))]
    tile = jnp.concatenate([p[0:1] for p in sums] + [jnp.zeros((10, PART), F32)], axis=0)
    block[ROWS:, :] = tile.astype(BF)


def join_body(where, keep, came, columns, x, block):
    x[: ROWS // 2, :] = keep[...]
    x[ROWS // 2 :, :] = came[...]
    emit_block(0, where, x[...].astype(F32), columns, block)


def gather(block, weight, early=()):
    other = lax.ppermute(block, "tp", Z_SWAP)
    other, *early = lax.optimization_barrier((other, *early))
    both = jnp.stack([block, other])
    held, _ = lax.optimization_barrier((weight, both))
    step = lax.ppermute(held, "grp", WORK_SWAP)
    up = lax.ppermute(both, "tp", FIRST[1])
    across = lax.ppermute(both, "tp", FIRST[2])
    down = lax.ppermute(both, "tp", FIRST[3])
    up, across, down, step = lax.optimization_barrier((up, across, down, step))
    partner = lax.ppermute(step, "grp", SECOND_STEP)
    low, high = jnp.stack([both, up]), jnp.stack([across, down])
    low_up = lax.ppermute(low, "tp", SECOND[1])
    high_down = lax.ppermute(high, "tp", SECOND[3])
    high_up = lax.ppermute(high, "tp", SECOND[1])
    low_down = lax.ppermute(low, "tp", SECOND[3])
    low_across = lax.ppermute(low_up, "tp", SECOND[1])
    high_across = lax.ppermute(high_down, "tp", SECOND[3])
    blocks = (low, high, low_up, high_up, low_across, high_across, low_down, high_down)
    partner, *_ = lax.optimization_barrier((partner, *blocks[2:]))
    return blocks, with_other(weight, partner), early


def arrivals(where, refs):
    x, z, y, c = where[0], where[1], where[2], where[3]
    for second in range(4):
        for first in range(4):
            ref, at = refs[2 * second + first // 2], first % 2
            col = (x + jnp.where(c == 0, first, second)) & 3
            row = (y + jnp.where(c == 0, second, first)) & 3
            for dz in range(2):
                yield (col * 2 + (z ^ dz)) * 4 + row, ref, at, dz


def block_rows(where, pair, dc):
    start = (2 * pair + (where[3] ^ dc)) * QUARTER
    return pl.ds(pl.multiple_of(start, QUARTER), QUARTER)


def place(where, blocks, placed):
    ss = [jnp.zeros((1, PART), F32) for _ in range(2)]
    for pair, ref, at, dz in arrivals(where, blocks):
        for prompt in range(2):
            lanes = slice(prompt * PART, (prompt + 1) * PART)
            for dc in range(2):
                for qi in range(2):
                    placed[qi, block_rows(where, pair, dc), lanes] = ref[
                        at, dz, rows_at(prompt, dc, qi), :
                    ]
        if ref.shape[2] > ROWS:
            sums = ref[at, dz, ROWS : ROWS + 16, :].astype(F32)
            for i in range(6):
                ss[i // 3] = ss[i // 3] + sums[i : i + 1]
    return ss


def pack_ss(ss):
    parts = [p.astype(F32) for p in split3(jnp.broadcast_to(ss, (16, ss.shape[1])))]
    row = lax.broadcasted_iota(jnp.int32, parts[0].shape, 0)
    out = jnp.zeros(parts[0].shape, F32)
    for i, part in enumerate(parts):
        out = jnp.where(row == i, part, out)
    return out.astype(BF)


def unpack_ss(rows):
    rows = rows.astype(F32)
    return rows[0:1] + rows[1:2] + rows[2:3]


def rotated(value, cosine, sine):
    first, second = value[:64], value[64:]
    return jnp.concatenate(
        [first * cosine - second * sine, second * cosine + first * sine], axis=0
    ).astype(BF)


def partial_in_body(where, *refs):
    blocks, wide, narrow = refs[0:8], refs[8:12], refs[12:16]
    keep, send, weight, placed = refs[16:]
    ss = place(where, blocks, placed)
    out = jnp.zeros((2 * IN, 2 * PART), F32)
    for qi in range(2):
        for dc in range(2):
            weight[qi, dc * IN : dc * IN + HD, :] = wide[2 * dc + qi][...]
            weight[qi, dc * IN + HD : (dc + 1) * IN, :] = narrow[2 * dc + qi][:, :DEPTH]
        out = out + jnp.dot(weight[qi], placed[qi], preferred_element_type=F32)
    keep[0 : 2 * IN, :] = out[:, :PART]
    keep[2 * IN :, :] = jnp.broadcast_to(ss[0], (8, PART))
    send[0 : 2 * IN, :] = out[:, PART:].astype(BF)
    send[2 * IN :, :] = pack_ss(ss[1])


def finish(where, rows, scale, columns, layer, bias, cosine, sine, q, kv):
    c = where[3]
    half = half_lanes(c)
    cos, sin = cosine[:, half], sine[:, half]
    for dc in range(2):
        base = dc * IN
        lane = 4 * dc + 2 + layer
        value = rows[base : base + HD] * scale + columns[:, lane : lane + 1]
        q[:, dc * PART : (dc + 1) * PART] = rotated(value, cos, sin)
        column = bias[dc][:, 0:1].astype(F32)
        value = rows[base + HD : base + IN] * scale + column
        kv[c if dc == 0 else 1 - c] = value.astype(BF)


def reduced_in_body(layer, where, keep, came, columns, *refs):
    bias, other_bias, cosine, sine, q, kv = refs
    rows = keep[...]
    sums = rows[: 2 * IN] + came[0 : 2 * IN, :].astype(F32)
    ss = rows[2 * IN : 2 * IN + 1] + unpack_ss(came[2 * IN :, :])
    scale = lax.rsqrt(ss / D + 1e-06)
    finish(where, sums, scale, columns, layer, (bias, other_bias), cosine, sine, q, kv)


def attend_body(
    where, length, q, own, other, cosine, sine, keep, send, raw, keys, vals, tall
):
    y, c = where[2], where[3]
    for ref, half in ((own, half_lanes(c)), (other, half_lanes(1 - c))):
        for i in range(4):
            rows = slice(i * QUARTER, (i + 1) * QUARTER)
            slot = (i - y) & 3
            raw[rows, half] = ref[slot, 0]
            vals[rows, half] = ref[slot, 1]
    keys[...] = rotated(raw[...].astype(F32), cosine[...], sine[...])
    scores = lax.dot_general(
        keys[...], q[...], (((0,), (0,)), ((), ())), preferred_element_type=F32
    ) / jnp.sqrt(jnp.float32(HD))
    s_at = lax.broadcasted_iota(jnp.int32, (TOK, TOK), 0)
    t_at = (lax.broadcasted_iota(jnp.int32, (TOK, TOK), 1) & (PART - 1)) + c * PART
    allowed = (s_at <= t_at) & (s_at < length[0])
    scores = jnp.where(allowed, scores, -1e30)
    weights = jnp.exp(scores - jnp.max(scores, axis=0, keepdims=True))
    probs = (weights / jnp.sum(weights, axis=0, keepdims=True)).astype(BF)
    attended = jnp.dot(vals[...], probs, preferred_element_type=F32).astype(BF)
    for dc in range(2):
        part = attended[:, dc * PART : (dc + 1) * PART]
        tall[dc] = part.reshape(GRP, QUARTER, PART)
    share(where, tall, keep, send)


def multiply_out(where, blocks, parts, weight, placed, total):
    place(where, blocks, placed)
    out = jnp.zeros((ROWS, 2 * PART), F32)
    for qi in range(2):
        for dc in range(2):
            weight[qi, dc * HD : (dc + 1) * HD, :] = parts[2 * dc + qi][...]
        out = out + jnp.dot(weight[qi], placed[qi], preferred_element_type=F32)
    total[...] = out


def partial_out_body(where, *refs):
    blocks, parts = refs[0:8], refs[8:12]
    keep, send, weight, placed, total = refs[12:]
    g = where[4]
    multiply_out(where, blocks, parts, weight, placed, total)
    for prompt in range(2):
        lanes = slice(prompt * PART, (prompt + 1) * PART)
        for dc in range(2):
            for qi in range(2):
                here = pl.multiple_of(dc * HD + (g ^ (2 * qi)) * QUARTER, QUARTER)
                there = pl.multiple_of(dc * HD + ((g ^ 1) ^ (2 * qi)) * QUARTER, QUARTER)
                keep[rows_at(prompt, dc, qi), :] = total[pl.ds(here, QUARTER), lanes]
                sent = total[pl.ds(there, QUARTER), lanes].astype(BF)
                send[rows_at(1 - prompt, dc, qi), :] = sent


def advance_body(layer, where, x, keep, came, columns, new, block):
    value = x[...].astype(F32) + (keep[...] + came[...].astype(F32))
    new[...] = value.astype(BF)
    emit_block(layer, where, new[...].astype(F32), columns, block)


def last_out_body(where, *refs):
    blocks, parts, x = refs[0:8], refs[8:12], refs[12]
    keep, send, weight, placed, total = refs[13:]
    multiply_out(where, blocks, parts, weight, placed, total)
    keep[...] = total[:, :PART]
    send[:ROWS, :] = total[:, PART:].astype(BF)
    send[ROWS:, :] = x[ROWS // 2 :, :]


def total_body(where, x, keep, came, mine, theirs, tall):
    g = where[4]
    for dc in range(2):
        for qi in range(2):
            tall[dc, g ^ (2 * qi)] = x[rows_at(0, dc, qi), :]
            at = rows_at(0, dc, qi)
            tall[dc, (g ^ 1) ^ (2 * qi)] = came[ROWS + at.start : ROWS + at.stop, :]
    for dc, out in enumerate((mine, theirs)):
        rows = slice(dc * HD, (dc + 1) * HD)
        mixed = keep[rows, :] + came[rows, :].astype(F32)
        out[...] = (tall[dc].reshape(HD, PART).astype(F32) + mixed).astype(BF)


def final_body(where, mine, theirs, out):
    c = where[3]
    out[0, half_lanes(c), :] = mine[...].astype(F32).T.astype(BF)
    out[0, half_lanes(1 - c), :] = theirs[...].astype(F32).T.astype(BF)


def local(hidden, lengths, norm_gain, q_weight, q_bias, kv_weight, kv_bias, out_weight):
    tp = lax.axis_index("tp").astype(jnp.int32)
    g = lax.axis_index("grp").astype(jnp.int32)
    where = jnp.stack([tp // 16, (tp // 8) % 2, (tp // 2) % 4, tp % 2, g, g, g, g])

    tile = shape((HD, PART))
    quarters = pltpu.VMEM((2, GRP, QUARTER, PART), BF)
    x_own, theirs = call(init_body, [tile, tile], where, hidden, specs=[SM, VM])
    x_other = lax.ppermute(theirs, "tp", CORE_SWAP)
    lines = jnp.concatenate([norm_gain, q_bias.astype(F32)])
    columns = jnp.concatenate([lines, lax.ppermute(lines, "tp", CORE_SWAP)]).T
    keep, send = call(
        spread_body,
        [tile, tile],
        where,
        x_own,
        x_other,
        specs=[SM, VM, VM],
        scratch=[quarters],
    )
    x, block = call(
        join_body,
        [shape((ROWS, PART)), shape((ROWS + 16, PART))],
        where,
        keep,
        lax.ppermute(send, "grp", WORK_SWAP),
        columns,
        specs=[SM] + [VM] * 3,
    )

    moved = [
        (
            lax.ppermute(turned, "tp", KV_MOVE),
            lax.ppermute(turned, ("grp", "tp"), KV_PARTNER),
        )
        for turned in call(
            turn_kv_body, [shape((QUARTER, DEPTH + HD))] * LAYERS, kv_weight, kv_bias.T
        )
    ]
    q_turned = turn(q_weight)
    out_turned = turn(out_weight)

    inv = 1.0 / 1000000.0 ** (jnp.arange(HD // 2, dtype=F32) * 2.0 / HD)
    angle = inv[:, None] * jnp.arange(TOK, dtype=F32)[None, :]
    cosine, sine = jnp.cos(angle), jnp.sin(angle)

    for layer in range(LAYERS):
        if layer == 0:
            blocks, wide, moved[0] = gather(block, q_turned[layer], moved[0])
        else:
            blocks, wide, _ = gather(block, q_turned[layer])
        narrow = with_other(*moved[layer])
        keep, send = call(
            partial_in_body,
            [shape((2 * IN + 8, PART), F32), shape((2 * IN + 16, PART))],
            where,
            *blocks,
            *wide,
            *narrow,
            specs=[SM] + [VM] * 16,
            scratch=[
                pltpu.VMEM((2, 2 * IN, DEPTH), BF),
                pltpu.VMEM((2, DEPTH, 2 * PART), BF),
            ],
        )
        q, kv = call(
            functools.partial(reduced_in_body, layer),
            [shape((HD, 2 * PART)), shape((2, QUARTER, PART))],
            where,
            keep,
            lax.ppermute(send, "grp", WORK_SWAP),
            columns,
            narrow[0],
            narrow[2],
            cosine,
            sine,
            specs=[SM] + [VM] * 3 + [BIAS, BIAS, VM, VM],
        )
        kvs = jnp.stack([kv] + [lax.ppermute(kv, "tp", Y_SLOT[s]) for s in (1, 2, 3)])
        keep, send = call(
            attend_body,
            [tile, tile],
            where,
            lengths,
            q,
            kvs,
            lax.ppermute(kvs, "tp", CORE_SWAP),
            cosine,
            sine,
            specs=[SM, SM] + [VM] * 5,
            scratch=[pltpu.VMEM((HD, TOK), BF)] * 3 + [quarters],
        )
        block = jnp.concatenate([keep, lax.ppermute(send, "grp", WORK_SWAP)])
        soon = moved[1] if layer == 0 else ()
        blocks, wide, soon = gather(block, out_turned[layer], soon)
        scratch = [
            pltpu.VMEM((2, ROWS, DEPTH), BF),
            pltpu.VMEM((2, DEPTH, 2 * PART), BF),
            pltpu.VMEM((ROWS, 2 * PART), F32),
        ]
        if layer < LAYERS - 1:
            keep, send = call(
                partial_out_body,
                [shape((ROWS, PART), F32), shape((ROWS, PART))],
                where,
                *blocks,
                *wide,
                specs=[SM] + [VM] * 12,
                scratch=scratch,
            )
            moved[1] = soon
            x, block = call(
                functools.partial(advance_body, layer + 1),
                [shape((ROWS, PART)), shape((ROWS + 16, PART))],
                where,
                x,
                keep,
                lax.ppermute(send, "grp", WORK_SWAP),
                columns,
                specs=[SM] + [VM] * 4,
            )
    keep, send = call(
        last_out_body,
        [shape((ROWS, PART), F32), shape((ROWS + HD, PART))],
        where,
        *blocks,
        *wide,
        x,
        specs=[SM] + [VM] * 13,
        scratch=scratch,
    )
    mine, theirs = call(
        total_body,
        [tile, tile],
        where,
        x,
        keep,
        lax.ppermute(send, "grp", WORK_SWAP),
        specs=[SM] + [VM] * 3,
        scratch=[quarters],
    )
    theirs = lax.ppermute(theirs, "tp", CORE_SWAP)
    return call(final_body, shape((1, TOK, HD)), where, mine, theirs, specs=[SM, VM, VM])


def solution(mesh):
    placed = (
        P("grp", None, "tp"),
        P("grp"),
        P(None, "tp"),
        P(None, None, "grp", "tp"),
        P(None, "tp"),
        P(None, None, "grp", "tp"),
        P(None, "tp"),
        P(None, None, "grp", "tp"),
    )
    return jax.shard_map(
        local, mesh=mesh, in_specs=placed, out_specs=P("grp", None, "tp"), check_vma=False
    )
```

```python
import functools

import jax
import jax.numpy as jnp
from jax import lax
from jax.experimental import pallas as pl
from jax.experimental.pallas import tpu as pltpu
from jax.sharding import PartitionSpec as P

D = 8192
HD = 128
LAYERS = 2
TOK = 256
GRP = 4
QUARTER = HD // GRP
PART = TOK // 2
WIDE = GRP * PART
DEPTH = 64 * QUARTER
IN = HD + QUARTER
ROWS = 2 * HD
BF = jnp.bfloat16
F32 = jnp.float32

VM = pl.BlockSpec(memory_space=pltpu.VMEM)
SM = pl.BlockSpec(memory_space=pltpu.SMEM)
ANY = pl.BlockSpec(memory_space=pl.ANY)
PARAMS = pltpu.CompilerParams(vmem_limit_bytes=40 * 1024 * 1024)


def tp_index(x, z, y, c):
    return ((x * 2 + z) * 4 + y) * 2 + c


COORDS = [
    (x, z, y, c) for x in range(4) for z in range(2) for y in range(4) for c in range(2)
]


def tp_perm(move):
    return [(tp_index(*at), tp_index(*move(*at))) for at in COORDS]


def along(x_first, s):
    def move(x, z, y, c):
        if (c == 0) == x_first:
            return ((x - s) % 4, z, y, c)
        return (x, z, (y - s) % 4, c)

    return tp_perm(move)


CORE_SWAP = tp_perm(lambda x, z, y, c: (x, z, y, 1 - c))
Z_SWAP = tp_perm(lambda x, z, y, c: (x, 1 - z, y, c))
FIRST = [along(True, s) for s in range(4)]
SECOND = [along(False, s) for s in range(4)]
Y_SLOT = [tp_perm(lambda x, z, y, c, s=s: (x, z, (y - s) % 4, c)) for s in range(4)]
WORK_SWAP = [(g, g ^ 1) for g in range(GRP)]
WEIGHT_SWAP = [(g, g ^ 2) for g in range(GRP)]
KV_MOVE = [(m, 8 * ((m % 32) // 4) + 2 * (m % 4) + m // 32) for m in range(64)]


def split3(value):
    high = value.astype(BF)
    rest = value - high.astype(F32)
    middle = rest.astype(BF)
    low = (rest - middle.astype(F32)).astype(BF)
    return high, middle, low


def call(body, outs, *args, specs=None, scratch=()):
    return pl.pallas_call(
        body,
        grid=(1,),
        out_shape=outs,
        in_specs=specs or [VM] * len(args),
        out_specs=jax.tree.map(lambda _: VM, outs),
        scratch_shapes=list(scratch),
        compiler_params=PARAMS,
        cost_estimate=pl.CostEstimate(flops=0, bytes_accessed=1 << 10, transcendentals=0),
    )(*args)


def shape(dims, dtype=BF):
    return jax.ShapeDtypeStruct(dims, dtype)


def half_lanes(index):
    return pl.ds(pl.multiple_of(index * PART, PART), PART)


def pack_ss(ss):
    parts = [p.astype(F32) for p in split3(jnp.broadcast_to(ss, (16, ss.shape[1])))]
    row = lax.broadcasted_iota(jnp.int32, parts[0].shape, 0)
    out = jnp.zeros(parts[0].shape, F32)
    for i, part in enumerate(parts):
        out = jnp.where(row == i, part, out)
    return out.astype(BF)


def unpack_ss(rows):
    rows = rows.astype(F32)
    return rows[0:1] + rows[1:2] + rows[2:3]


def rotated(value, cosine, sine):
    first, second = value[:64], value[64:]
    return jnp.concatenate(
        [first * cosine - second * sine, second * cosine + first * sine], axis=0
    ).astype(BF)


def turn_body(weight, first, second):
    for layer, out in enumerate((first, second)):
        out[...] = weight[layer].reshape(DEPTH, HD).T


def turn(weight):
    return call(turn_body, [shape((HD, DEPTH))] * 2, weight)


def turn_kv_body(weight, bias, out):
    for layer in range(LAYERS):
        out[layer, :, :DEPTH] = weight[layer].reshape(DEPTH, QUARTER).T
        out[layer, :, DEPTH:] = jnp.broadcast_to(bias[:, layer : layer + 1], (QUARTER, HD))


def of_layer(layer, rows, depth, at=0):
    return pl.BlockSpec((1, rows, depth), lambda i: (layer, 0, at))


def bundle_body(wide, narrow, out):
    out[:HD, :] = wide[...]
    out[HD:, :] = narrow[0, :, :DEPTH]


def bundle(layer, wide, narrow):
    return call(
        bundle_body,
        shape((IN, DEPTH)),
        wide,
        narrow,
        specs=[VM, of_layer(layer, QUARTER, DEPTH + HD)],
    )


def both_quarters(own, after, late):
    held, _ = lax.optimization_barrier((own, after))
    partner = lax.ppermute(held, "grp", WEIGHT_SWAP)
    here, *_ = lax.optimization_barrier((partner, *late))
    return [
        own,
        partner,
        lax.ppermute(own, "tp", CORE_SWAP),
        lax.ppermute(here, "tp", CORE_SWAP),
    ]


def rows_at(prompt, dc, qi):
    start = ((prompt * 2 + dc) * 2 + qi) * QUARTER
    return slice(start, start + QUARTER)


def share(where, tall, keep, send):
    g = where[4]
    for dc in range(2):
        for qi in range(2):
            keep[rows_at(0, dc, qi), :] = tall[dc, g ^ (2 * qi)]
            send[rows_at(0, dc, qi), :] = tall[dc, (g ^ 1) ^ (2 * qi)]


def init_body(where, hidden, mine, theirs):
    c = where[3]
    mine[...] = hidden[0, half_lanes(c), :].astype(F32).T.astype(BF)
    theirs[...] = hidden[0, half_lanes(1 - c), :].astype(F32).T.astype(BF)


def spread_body(where, own, other, keep, send, tall):
    tall[0] = own[...].reshape(GRP, QUARTER, PART)
    tall[1] = other[...].reshape(GRP, QUARTER, PART)
    share(where, tall, keep, send)


def emit_block(layer, where, values, columns, block):
    g = where[4]
    sums = []
    for prompt in range(2):
        squares = jnp.zeros((QUARTER, PART), F32)
        for dc in range(2):
            for qi in range(2):
                rows = rows_at(prompt, dc, qi)
                start = pl.multiple_of((g ^ (2 * qi)) * QUARTER, QUARTER)
                lane = 4 * dc + layer
                gain = columns[pl.ds(start, QUARTER), lane : lane + 1]
                value = values[rows]
                block[rows, :] = (value * gain).astype(BF)
                squares = squares + value * value
        ss = jnp.sum(squares, axis=0, keepdims=True)
        sums += [p.astype(F32) for p in split3(jnp.broadcast_to(ss, (8, PART)))]
    tile = jnp.concatenate([p[0:1] for p in sums] + [jnp.zeros((10, PART), F32)], axis=0)
    block[ROWS:, :] = tile.astype(BF)


def join_body(where, keep, came, columns, x, block):
    x[: ROWS // 2, :] = keep[...]
    x[ROWS // 2 :, :] = came[...]
    emit_block(0, where, x[...].astype(F32), columns, block)


def gather(block, early=None):
    other = lax.ppermute(block, "tp", Z_SWAP)
    if early is not None:
        other, early = lax.optimization_barrier((other, early))
    both = jnp.stack([block, other])
    up = lax.ppermute(both, "tp", FIRST[1])
    across = lax.ppermute(both, "tp", FIRST[2])
    down = lax.ppermute(both, "tp", FIRST[3])
    up, across, down = lax.optimization_barrier((up, across, down))
    low, high = jnp.stack([both, up]), jnp.stack([across, down])
    low_up = lax.ppermute(low, "tp", SECOND[1])
    high_down = lax.ppermute(high, "tp", SECOND[3])
    high_up = lax.ppermute(high, "tp", SECOND[1])
    low_down = lax.ppermute(low, "tp", SECOND[3])
    low_across = lax.ppermute(low_up, "tp", SECOND[1])
    high_across = lax.ppermute(high_down, "tp", SECOND[3])
    blocks = (low, high, low_up, high_up, low_across, high_across, low_down, high_down)
    return blocks, both, blocks[2:], early


def arrivals(where, refs):
    x, z, y, c = where[0], where[1], where[2], where[3]
    for second in range(4):
        for first in range(4):
            ref, at = refs[2 * second + first // 2], first % 2
            col = (x + jnp.where(c == 0, first, second)) & 3
            row = (y + jnp.where(c == 0, second, first)) & 3
            for dz in range(2):
                yield (col * 2 + (z ^ dz)) * 4 + row, ref, at, dz


def block_rows(where, pair, dc):
    start = (2 * pair + (where[3] ^ dc)) * QUARTER
    return pl.ds(pl.multiple_of(start, QUARTER), QUARTER)


def place(where, blocks, placed):
    ss = [jnp.zeros((1, PART), F32) for _ in range(2)]
    for pair, ref, at, dz in arrivals(where, blocks):
        for prompt in range(2):
            lanes = slice(prompt * PART, (prompt + 1) * PART)
            for dc in range(2):
                for qi in range(2):
                    placed[qi, block_rows(where, pair, dc), lanes] = ref[
                        at, dz, rows_at(prompt, dc, qi), :
                    ]
        if ref.shape[2] > ROWS:
            sums = ref[at, dz, ROWS : ROWS + 16, :].astype(F32)
            for i in range(6):
                ss[i // 3] = ss[i // 3] + sums[i : i + 1]
    return ss


def pack_ss(ss):
    parts = [p.astype(F32) for p in split3(jnp.broadcast_to(ss, (16, ss.shape[1])))]
    row = lax.broadcasted_iota(jnp.int32, parts[0].shape, 0)
    out = jnp.zeros(parts[0].shape, F32)
    for i, part in enumerate(parts):
        out = jnp.where(row == i, part, out)
    return out.astype(BF)


def unpack_ss(rows):
    rows = rows.astype(F32)
    return rows[0:1] + rows[1:2] + rows[2:3]


def rotated(value, cosine, sine):
    first, second = value[:64], value[64:]
    return jnp.concatenate(
        [first * cosine - second * sine, second * cosine + first * sine], axis=0
    ).astype(BF)


def partial_in_body(where, *refs):
    blocks, parts = refs[0:8], refs[8:12]
    keep, send, weight, placed = refs[12:]
    ss = place(where, blocks, placed)
    out = jnp.zeros((2 * IN, 2 * PART), F32)
    for qi in range(2):
        for dc in range(2):
            weight[qi, dc * IN : (dc + 1) * IN, :] = parts[2 * dc + qi][...]
        out = out + jnp.dot(weight[qi], placed[qi], preferred_element_type=F32)
    keep[0 : 2 * IN, :] = out[:, :PART]
    keep[2 * IN :, :] = jnp.broadcast_to(ss[0], (8, PART))
    send[0 : 2 * IN, :] = out[:, PART:].astype(BF)
    send[2 * IN :, :] = pack_ss(ss[1])


def finish(where, rows, scale, columns, layer, bias, cosine, sine, q, kv):
    c = where[3]
    half = half_lanes(c)
    cos, sin = cosine[:, half], sine[:, half]
    for dc in range(2):
        base = dc * IN
        lane = 4 * dc + 2 + layer
        value = rows[base : base + HD] * scale + columns[:, lane : lane + 1]
        q[:, dc * PART : (dc + 1) * PART] = rotated(value, cos, sin)
        column = bias[dc][0, :, 0:1].astype(F32)
        value = rows[base + HD : base + IN] * scale + column
        kv[c if dc == 0 else 1 - c] = value.astype(BF)


def reduced_in_body(layer, where, keep, came, columns, *refs):
    bias, other_bias, cosine, sine, q, kv = refs
    rows = keep[...]
    sums = rows[: 2 * IN] + came[0 : 2 * IN, :].astype(F32)
    ss = rows[2 * IN : 2 * IN + 1] + unpack_ss(came[2 * IN :, :])
    scale = lax.rsqrt(ss / D + 1e-06)
    finish(where, sums, scale, columns, layer, (bias, other_bias), cosine, sine, q, kv)


def attend_body(
    where, length, q, own, other, cosine, sine, keep, send, raw, keys, vals, tall
):
    y, c = where[2], where[3]
    for ref, half in ((own, half_lanes(c)), (other, half_lanes(1 - c))):
        for i in range(4):
            rows = slice(i * QUARTER, (i + 1) * QUARTER)
            slot = (i - y) & 3
            raw[rows, half] = ref[slot, 0]
            vals[rows, half] = ref[slot, 1]
    keys[...] = rotated(raw[...].astype(F32), cosine[...], sine[...])
    scores = lax.dot_general(
        keys[...], q[...], (((0,), (0,)), ((), ())), preferred_element_type=F32
    ) / jnp.sqrt(jnp.float32(HD))
    s_at = lax.broadcasted_iota(jnp.int32, (TOK, TOK), 0)
    t_at = (lax.broadcasted_iota(jnp.int32, (TOK, TOK), 1) & (PART - 1)) + c * PART
    allowed = (s_at <= t_at) & (s_at < length[0])
    scores = jnp.where(allowed, scores, -1e30)
    weights = jnp.exp(scores - jnp.max(scores, axis=0, keepdims=True))
    probs = (weights / jnp.sum(weights, axis=0, keepdims=True)).astype(BF)
    attended = jnp.dot(vals[...], probs, preferred_element_type=F32).astype(BF)
    for dc in range(2):
        part = attended[:, dc * PART : (dc + 1) * PART]
        tall[dc] = part.reshape(GRP, QUARTER, PART)
    share(where, tall, keep, send)


def multiply_out(where, blocks, parts, weight, placed, total):
    place(where, blocks, placed)
    out = jnp.zeros((ROWS, 2 * PART), F32)
    for qi in range(2):
        for dc in range(2):
            weight[qi, dc * HD : (dc + 1) * HD, :] = parts[2 * dc + qi][...]
        out = out + jnp.dot(weight[qi], placed[qi], preferred_element_type=F32)
    total[...] = out


def partial_out_body(where, *refs):
    blocks, parts = refs[0:8], refs[8:12]
    keep, send, weight, placed, total = refs[12:]
    g = where[4]
    multiply_out(where, blocks, parts, weight, placed, total)
    for prompt in range(2):
        lanes = slice(prompt * PART, (prompt + 1) * PART)
        for dc in range(2):
            for qi in range(2):
                here = pl.multiple_of(dc * HD + (g ^ (2 * qi)) * QUARTER, QUARTER)
                there = pl.multiple_of(dc * HD + ((g ^ 1) ^ (2 * qi)) * QUARTER, QUARTER)
                keep[rows_at(prompt, dc, qi), :] = total[pl.ds(here, QUARTER), lanes]
                sent = total[pl.ds(there, QUARTER), lanes].astype(BF)
                send[rows_at(1 - prompt, dc, qi), :] = sent


def advance_body(layer, where, x, keep, came, columns, new, block):
    value = x[...].astype(F32) + (keep[...] + came[...].astype(F32))
    new[...] = value.astype(BF)
    emit_block(layer, where, new[...].astype(F32), columns, block)


def last_out_body(where, *refs):
    blocks, parts, x = refs[0:8], refs[8:12], refs[12]
    keep, send, weight, placed, total = refs[13:]
    multiply_out(where, blocks, parts, weight, placed, total)
    keep[...] = total[:, :PART]
    send[:ROWS, :] = total[:, PART:].astype(BF)
    send[ROWS:, :] = x[ROWS // 2 :, :]


def total_body(where, x, keep, came, mine, theirs, tall):
    g = where[4]
    for dc in range(2):
        for qi in range(2):
            tall[dc, g ^ (2 * qi)] = x[rows_at(0, dc, qi), :]
            at = rows_at(0, dc, qi)
            tall[dc, (g ^ 1) ^ (2 * qi)] = came[ROWS + at.start : ROWS + at.stop, :]
    for dc, out in enumerate((mine, theirs)):
        rows = slice(dc * HD, (dc + 1) * HD)
        mixed = keep[rows, :] + came[rows, :].astype(F32)
        out[...] = (tall[dc].reshape(HD, PART).astype(F32) + mixed).astype(BF)


def final_body(where, mine, theirs, out):
    c = where[3]
    out[0, half_lanes(c), :] = mine[...].astype(F32).T.astype(BF)
    out[0, half_lanes(1 - c), :] = theirs[...].astype(F32).T.astype(BF)


def local(hidden, lengths, norm_gain, q_weight, q_bias, kv_weight, kv_bias, out_weight):
    tp = lax.axis_index("tp").astype(jnp.int32)
    g = lax.axis_index("grp").astype(jnp.int32)
    where = jnp.stack([tp // 16, (tp // 8) % 2, (tp // 2) % 4, tp % 2, g, g, g, g])

    tile = shape((HD, PART))
    quarters = pltpu.VMEM((2, GRP, QUARTER, PART), BF)
    x_own, theirs = call(init_body, [tile, tile], where, hidden, specs=[SM, VM])
    x_other = lax.ppermute(theirs, "tp", CORE_SWAP)
    lines = jnp.concatenate([norm_gain, q_bias.astype(F32)])
    columns = jnp.concatenate([lines, lax.ppermute(lines, "tp", CORE_SWAP)]).T
    keep, send = call(
        spread_body,
        [tile, tile],
        where,
        x_own,
        x_other,
        specs=[SM, VM, VM],
        scratch=[quarters],
    )
    x, block = call(
        join_body,
        [shape((ROWS, PART)), shape((ROWS + 16, PART))],
        where,
        keep,
        lax.ppermute(send, "grp", WORK_SWAP),
        columns,
        specs=[SM] + [VM] * 3,
    )

    kv_turned = call(
        turn_kv_body, shape((LAYERS, QUARTER, DEPTH + HD)), kv_weight, kv_bias.T
    )
    kv_own = lax.ppermute(kv_turned, "tp", KV_MOVE)
    q_turned = turn(q_weight)
    out_turned = turn(out_weight)

    inv = 1.0 / 1000000.0 ** (jnp.arange(HD // 2, dtype=F32) * 2.0 / HD)
    angle = inv[:, None] * jnp.arange(TOK, dtype=F32)[None, :]
    cosine, sine = jnp.cos(angle), jnp.sin(angle)

    for layer in range(LAYERS):
        if layer == 0:
            blocks, both, late, kv_own = gather(block, kv_own)
            bias = kv_own[:, :, DEPTH:]
            biases = (bias, lax.ppermute(bias, "tp", CORE_SWAP))
        else:
            blocks, both, late, _ = gather(block)
        wide = both_quarters(bundle(layer, q_turned[layer], kv_own), both, late)
        keep, send = call(
            partial_in_body,
            [shape((2 * IN + 8, PART), F32), shape((2 * IN + 16, PART))],
            where,
            *blocks,
            *wide,
            specs=[SM] + [VM] * 12,
            scratch=[
                pltpu.VMEM((2, 2 * IN, DEPTH), BF),
                pltpu.VMEM((2, DEPTH, 2 * PART), BF),
            ],
        )
        bias = of_layer(layer, QUARTER, HD)
        q, kv = call(
            functools.partial(reduced_in_body, layer),
            [shape((HD, 2 * PART)), shape((2, QUARTER, PART))],
            where,
            keep,
            lax.ppermute(send, "grp", WORK_SWAP),
            columns,
            *biases,
            cosine,
            sine,
            specs=[SM] + [VM] * 3 + [bias, bias, VM, VM],
        )
        kvs = jnp.stack([kv] + [lax.ppermute(kv, "tp", Y_SLOT[s]) for s in (1, 2, 3)])
        keep, send = call(
            attend_body,
            [tile, tile],
            where,
            lengths,
            q,
            kvs,
            lax.ppermute(kvs, "tp", CORE_SWAP),
            cosine,
            sine,
            specs=[SM, SM] + [VM] * 5,
            scratch=[pltpu.VMEM((HD, TOK), BF)] * 3 + [quarters],
        )
        block = jnp.concatenate([keep, lax.ppermute(send, "grp", WORK_SWAP)])
        blocks, both, late, _ = gather(block)
        wide = both_quarters(out_turned[layer], both, late)
        scratch = [
            pltpu.VMEM((2, ROWS, DEPTH), BF),
            pltpu.VMEM((2, DEPTH, 2 * PART), BF),
            pltpu.VMEM((ROWS, 2 * PART), F32),
        ]
        if layer < LAYERS - 1:
            keep, send = call(
                partial_out_body,
                [shape((ROWS, PART), F32), shape((ROWS, PART))],
                where,
                *blocks,
                *wide,
                specs=[SM] + [VM] * 12,
                scratch=scratch,
            )
            x, block = call(
                functools.partial(advance_body, layer + 1),
                [shape((ROWS, PART)), shape((ROWS + 16, PART))],
                where,
                x,
                keep,
                lax.ppermute(send, "grp", WORK_SWAP),
                columns,
                specs=[SM] + [VM] * 4,
            )
    keep, send = call(
        last_out_body,
        [shape((ROWS, PART), F32), shape((ROWS + HD, PART))],
        where,
        *blocks,
        *wide,
        x,
        specs=[SM] + [VM] * 13,
        scratch=scratch,
    )
    mine, theirs = call(
        total_body,
        [tile, tile],
        where,
        x,
        keep,
        lax.ppermute(send, "grp", WORK_SWAP),
        specs=[SM] + [VM] * 3,
        scratch=[quarters],
    )
    theirs = lax.ppermute(theirs, "tp", CORE_SWAP)
    return call(final_body, shape((1, TOK, HD)), where, mine, theirs, specs=[SM, VM, VM])


def solution(mesh):
    placed = (
        P("grp", None, "tp"),
        P("grp"),
        P(None, "tp"),
        P(None, None, "grp", "tp"),
        P(None, "tp"),
        P(None, None, "grp", "tp"),
        P(None, "tp"),
        P(None, None, "grp", "tp"),
    )
    return jax.shard_map(
        local, mesh=mesh, in_specs=placed, out_specs=P("grp", None, "tp"), check_vma=False
    )
```

```python
import functools

import jax
import jax.numpy as jnp
from jax import lax
from jax.experimental import pallas as pl
from jax.experimental.pallas import tpu as pltpu
from jax.sharding import PartitionSpec as P

D = 8192
HD = 128
LAYERS = 2
TOK = 256
GRP = 4
QUARTER = HD // GRP
PART = TOK // 2
WIDE = GRP * PART
DEPTH = 64 * QUARTER
IN = HD + QUARTER
ROWS = 2 * HD
BF = jnp.bfloat16
F32 = jnp.float32

VM = pl.BlockSpec(memory_space=pltpu.VMEM)
SM = pl.BlockSpec(memory_space=pltpu.SMEM)
ANY = pl.BlockSpec(memory_space=pl.ANY)
PARAMS = pltpu.CompilerParams(vmem_limit_bytes=40 * 1024 * 1024)


def tp_index(x, z, y, c):
    return ((x * 2 + z) * 4 + y) * 2 + c


COORDS = [
    (x, z, y, c) for x in range(4) for z in range(2) for y in range(4) for c in range(2)
]


def tp_perm(move):
    return [(tp_index(*at), tp_index(*move(*at))) for at in COORDS]


def along(x_first, s):
    def move(x, z, y, c):
        if (c == 0) == x_first:
            return ((x - s) % 4, z, y, c)
        return (x, z, (y - s) % 4, c)

    return tp_perm(move)


CORE_SWAP = tp_perm(lambda x, z, y, c: (x, z, y, 1 - c))
Z_SWAP = tp_perm(lambda x, z, y, c: (x, 1 - z, y, c))
FIRST = [along(True, s) for s in range(4)]
SECOND = [along(False, s) for s in range(4)]
Y_SLOT = [tp_perm(lambda x, z, y, c, s=s: (x, z, (y - s) % 4, c)) for s in range(4)]
WORK_SWAP = [(g, g ^ 1) for g in range(GRP)]
KV_MOVE = [(m, 8 * ((m % 32) // 4) + 2 * (m % 4) + m // 32) for m in range(64)]


def split3(value):
    high = value.astype(BF)
    rest = value - high.astype(F32)
    middle = rest.astype(BF)
    low = (rest - middle.astype(F32)).astype(BF)
    return high, middle, low


def call(body, outs, *args, specs=None, scratch=()):
    return pl.pallas_call(
        body,
        grid=(1,),
        out_shape=outs,
        in_specs=specs or [VM] * len(args),
        out_specs=jax.tree.map(lambda _: VM, outs),
        scratch_shapes=list(scratch),
        compiler_params=PARAMS,
        cost_estimate=pl.CostEstimate(flops=0, bytes_accessed=1 << 10, transcendentals=0),
    )(*args)


def shape(dims, dtype=BF):
    return jax.ShapeDtypeStruct(dims, dtype)


def half_lanes(index):
    return pl.ds(pl.multiple_of(index * PART, PART), PART)


def pack_ss(ss):
    parts = [p.astype(F32) for p in split3(jnp.broadcast_to(ss, (16, ss.shape[1])))]
    row = lax.broadcasted_iota(jnp.int32, parts[0].shape, 0)
    out = jnp.zeros(parts[0].shape, F32)
    for i, part in enumerate(parts):
        out = jnp.where(row == i, part, out)
    return out.astype(BF)


def unpack_ss(rows):
    rows = rows.astype(F32)
    return rows[0:1] + rows[1:2] + rows[2:3]


def rotated(value, cosine, sine):
    first, second = value[:64], value[64:]
    return jnp.concatenate(
        [first * cosine - second * sine, second * cosine + first * sine], axis=0
    ).astype(BF)


def turn_body(weight, first, second):
    for layer, out in enumerate((first, second)):
        out[...] = weight[layer].reshape(DEPTH, HD).T


def turn(weight):
    return call(turn_body, [shape((HD, DEPTH))] * 2, weight)


def turn_kv_body(weight, bias, out):
    for layer in range(LAYERS):
        out[layer, :, :DEPTH] = weight[layer].reshape(DEPTH, QUARTER).T
        out[layer, :, DEPTH:] = jnp.broadcast_to(bias[:, layer : layer + 1], (QUARTER, HD))


def of_layer(layer, rows, depth, at=0):
    return pl.BlockSpec((1, rows, depth), lambda i: (layer, 0, at))


def bundle_body(wide, narrow, out):
    out[:HD, :] = wide[...]
    out[HD:, :] = narrow[0, :, :DEPTH]


def bundle(layer, wide, narrow):
    return call(
        bundle_body,
        shape((IN, DEPTH)),
        wide,
        narrow,
        specs=[VM, of_layer(layer, QUARTER, DEPTH + HD)],
    )


def both_quarters(own, after, late):
    held, _ = lax.optimization_barrier((own, after))
    pair = lax.all_gather(held, "grp", axis_index_groups=[[0, 2], [1, 3]])
    here, *_ = lax.optimization_barrier((pair, *late))
    return [pair, lax.ppermute(here, "tp", CORE_SWAP)]


def rows_at(prompt, dc, qi):
    start = ((prompt * 2 + dc) * 2 + qi) * QUARTER
    return slice(start, start + QUARTER)


def share(where, tall, keep, send):
    g = where[4]
    for dc in range(2):
        for qi in range(2):
            keep[rows_at(0, dc, qi), :] = tall[dc, g ^ (2 * qi)]
            send[rows_at(0, dc, qi), :] = tall[dc, (g ^ 1) ^ (2 * qi)]


def init_body(where, hidden, mine, theirs):
    c = where[3]
    mine[...] = hidden[0, half_lanes(c), :].astype(F32).T.astype(BF)
    theirs[...] = hidden[0, half_lanes(1 - c), :].astype(F32).T.astype(BF)


def spread_body(where, own, other, keep, send, tall):
    tall[0] = own[...].reshape(GRP, QUARTER, PART)
    tall[1] = other[...].reshape(GRP, QUARTER, PART)
    share(where, tall, keep, send)


def emit_block(layer, where, values, columns, block):
    g = where[4]
    sums = []
    for prompt in range(2):
        squares = jnp.zeros((QUARTER, PART), F32)
        for dc in range(2):
            for qi in range(2):
                rows = rows_at(prompt, dc, qi)
                start = pl.multiple_of((g ^ (2 * qi)) * QUARTER, QUARTER)
                lane = 4 * dc + layer
                gain = columns[pl.ds(start, QUARTER), lane : lane + 1]
                value = values[rows]
                block[rows, :] = (value * gain).astype(BF)
                squares = squares + value * value
        ss = jnp.sum(squares, axis=0, keepdims=True)
        sums += [p.astype(F32) for p in split3(jnp.broadcast_to(ss, (8, PART)))]
    tile = jnp.concatenate([p[0:1] for p in sums] + [jnp.zeros((10, PART), F32)], axis=0)
    block[ROWS:, :] = tile.astype(BF)


def join_body(where, keep, came, columns, x, block):
    x[: ROWS // 2, :] = keep[...]
    x[ROWS // 2 :, :] = came[...]
    emit_block(0, where, x[...].astype(F32), columns, block)


def gather(block, early=None):
    other = lax.ppermute(block, "tp", Z_SWAP)
    if early is not None:
        other, early = lax.optimization_barrier((other, early))
    both = jnp.stack([block, other])
    up = lax.ppermute(both, "tp", FIRST[1])
    across = lax.ppermute(both, "tp", FIRST[2])
    down = lax.ppermute(both, "tp", FIRST[3])
    up, across, down = lax.optimization_barrier((up, across, down))
    low, high = jnp.stack([both, up]), jnp.stack([across, down])
    low_up = lax.ppermute(low, "tp", SECOND[1])
    high_down = lax.ppermute(high, "tp", SECOND[3])
    high_up = lax.ppermute(high, "tp", SECOND[1])
    low_down = lax.ppermute(low, "tp", SECOND[3])
    low_across = lax.ppermute(low_up, "tp", SECOND[1])
    high_across = lax.ppermute(high_down, "tp", SECOND[3])
    blocks = (low, high, low_up, high_up, low_across, high_across, low_down, high_down)
    return blocks, both, blocks[2:], early


def arrivals(where, refs):
    x, z, y, c = where[0], where[1], where[2], where[3]
    for second in range(4):
        for first in range(4):
            ref, at = refs[2 * second + first // 2], first % 2
            col = (x + jnp.where(c == 0, first, second)) & 3
            row = (y + jnp.where(c == 0, second, first)) & 3
            for dz in range(2):
                yield (col * 2 + (z ^ dz)) * 4 + row, ref, at, dz


def block_rows(where, pair, dc):
    start = (2 * pair + (where[3] ^ dc)) * QUARTER
    return pl.ds(pl.multiple_of(start, QUARTER), QUARTER)


def place(where, blocks, placed):
    ss = [jnp.zeros((1, PART), F32) for _ in range(2)]
    for pair, ref, at, dz in arrivals(where, blocks):
        for prompt in range(2):
            lanes = slice(prompt * PART, (prompt + 1) * PART)
            for dc in range(2):
                for qi in range(2):
                    placed[qi, block_rows(where, pair, dc), lanes] = ref[
                        at, dz, rows_at(prompt, dc, qi), :
                    ]
        if ref.shape[2] > ROWS:
            sums = ref[at, dz, ROWS : ROWS + 16, :].astype(F32)
            for i in range(6):
                ss[i // 3] = ss[i // 3] + sums[i : i + 1]
    return ss


def pack_ss(ss):
    parts = [p.astype(F32) for p in split3(jnp.broadcast_to(ss, (16, ss.shape[1])))]
    row = lax.broadcasted_iota(jnp.int32, parts[0].shape, 0)
    out = jnp.zeros(parts[0].shape, F32)
    for i, part in enumerate(parts):
        out = jnp.where(row == i, part, out)
    return out.astype(BF)


def unpack_ss(rows):
    rows = rows.astype(F32)
    return rows[0:1] + rows[1:2] + rows[2:3]


def rotated(value, cosine, sine):
    first, second = value[:64], value[64:]
    return jnp.concatenate(
        [first * cosine - second * sine, second * cosine + first * sine], axis=0
    ).astype(BF)


def partial_in_body(where, *refs):
    blocks, parts = refs[0:8], refs[8:10]
    keep, send, weight, placed = refs[10:]
    ss = place(where, blocks, placed)
    out = jnp.zeros((2 * IN, 2 * PART), F32)
    for qi in range(2):
        for dc in range(2):
            weight[qi, dc * IN : (dc + 1) * IN, :] = parts[dc][(where[4] >> 1) ^ qi]
        out = out + jnp.dot(weight[qi], placed[qi], preferred_element_type=F32)
    keep[0 : 2 * IN, :] = out[:, :PART]
    keep[2 * IN :, :] = jnp.broadcast_to(ss[0], (8, PART))
    send[0 : 2 * IN, :] = out[:, PART:].astype(BF)
    send[2 * IN :, :] = pack_ss(ss[1])


def finish(where, rows, scale, columns, layer, bias, cosine, sine, q, kv):
    c = where[3]
    half = half_lanes(c)
    cos, sin = cosine[:, half], sine[:, half]
    for dc in range(2):
        base = dc * IN
        lane = 4 * dc + 2 + layer
        value = rows[base : base + HD] * scale + columns[:, lane : lane + 1]
        q[:, dc * PART : (dc + 1) * PART] = rotated(value, cos, sin)
        column = bias[dc][0, :, 0:1].astype(F32)
        value = rows[base + HD : base + IN] * scale + column
        kv[c if dc == 0 else 1 - c] = value.astype(BF)


def reduced_in_body(layer, where, keep, came, columns, *refs):
    bias, other_bias, cosine, sine, q, kv = refs
    rows = keep[...]
    sums = rows[: 2 * IN] + came[0 : 2 * IN, :].astype(F32)
    ss = rows[2 * IN : 2 * IN + 1] + unpack_ss(came[2 * IN :, :])
    scale = lax.rsqrt(ss / D + 1e-06)
    finish(where, sums, scale, columns, layer, (bias, other_bias), cosine, sine, q, kv)


def attend_body(
    where, length, q, own, other, cosine, sine, keep, send, raw, keys, vals, tall
):
    y, c = where[2], where[3]
    for ref, half in ((own, half_lanes(c)), (other, half_lanes(1 - c))):
        for i in range(4):
            rows = slice(i * QUARTER, (i + 1) * QUARTER)
            slot = (i - y) & 3
            raw[rows, half] = ref[slot, 0]
            vals[rows, half] = ref[slot, 1]
    keys[...] = rotated(raw[...].astype(F32), cosine[...], sine[...])
    scores = lax.dot_general(
        keys[...], q[...], (((0,), (0,)), ((), ())), preferred_element_type=F32
    ) / jnp.sqrt(jnp.float32(HD))
    s_at = lax.broadcasted_iota(jnp.int32, (TOK, TOK), 0)
    t_at = (lax.broadcasted_iota(jnp.int32, (TOK, TOK), 1) & (PART - 1)) + c * PART
    allowed = (s_at <= t_at) & (s_at < length[0])
    scores = jnp.where(allowed, scores, -1e30)
    weights = jnp.exp(scores - jnp.max(scores, axis=0, keepdims=True))
    probs = (weights / jnp.sum(weights, axis=0, keepdims=True)).astype(BF)
    attended = jnp.dot(vals[...], probs, preferred_element_type=F32).astype(BF)
    for dc in range(2):
        part = attended[:, dc * PART : (dc + 1) * PART]
        tall[dc] = part.reshape(GRP, QUARTER, PART)
    share(where, tall, keep, send)


def multiply_out(where, blocks, parts, weight, placed, total):
    place(where, blocks, placed)
    out = jnp.zeros((ROWS, 2 * PART), F32)
    for qi in range(2):
        for dc in range(2):
            weight[qi, dc * HD : (dc + 1) * HD, :] = parts[dc][(where[4] >> 1) ^ qi]
        out = out + jnp.dot(weight[qi], placed[qi], preferred_element_type=F32)
    total[...] = out


def partial_out_body(where, *refs):
    blocks, parts = refs[0:8], refs[8:10]
    keep, send, weight, placed, total = refs[10:]
    g = where[4]
    multiply_out(where, blocks, parts, weight, placed, total)
    for prompt in range(2):
        lanes = slice(prompt * PART, (prompt + 1) * PART)
        for dc in range(2):
            for qi in range(2):
                here = pl.multiple_of(dc * HD + (g ^ (2 * qi)) * QUARTER, QUARTER)
                there = pl.multiple_of(dc * HD + ((g ^ 1) ^ (2 * qi)) * QUARTER, QUARTER)
                keep[rows_at(prompt, dc, qi), :] = total[pl.ds(here, QUARTER), lanes]
                sent = total[pl.ds(there, QUARTER), lanes].astype(BF)
                send[rows_at(1 - prompt, dc, qi), :] = sent


def advance_body(layer, where, x, keep, came, columns, new, block):
    value = x[...].astype(F32) + (keep[...] + came[...].astype(F32))
    new[...] = value.astype(BF)
    emit_block(layer, where, new[...].astype(F32), columns, block)


def last_out_body(where, *refs):
    blocks, parts, x = refs[0:8], refs[8:10], refs[10]
    keep, send, weight, placed, total = refs[11:]
    multiply_out(where, blocks, parts, weight, placed, total)
    keep[...] = total[:, :PART]
    send[:ROWS, :] = total[:, PART:].astype(BF)
    send[ROWS:, :] = x[ROWS // 2 :, :]


def total_body(where, x, keep, came, mine, theirs, tall):
    g = where[4]
    for dc in range(2):
        for qi in range(2):
            tall[dc, g ^ (2 * qi)] = x[rows_at(0, dc, qi), :]
            at = rows_at(0, dc, qi)
            tall[dc, (g ^ 1) ^ (2 * qi)] = came[ROWS + at.start : ROWS + at.stop, :]
    for dc, out in enumerate((mine, theirs)):
        rows = slice(dc * HD, (dc + 1) * HD)
        mixed = keep[rows, :] + came[rows, :].astype(F32)
        out[...] = (tall[dc].reshape(HD, PART).astype(F32) + mixed).astype(BF)


def final_body(where, mine, theirs, out):
    c = where[3]
    out[0, half_lanes(c), :] = mine[...].astype(F32).T.astype(BF)
    out[0, half_lanes(1 - c), :] = theirs[...].astype(F32).T.astype(BF)


def local(hidden, lengths, norm_gain, q_weight, q_bias, kv_weight, kv_bias, out_weight):
    tp = lax.axis_index("tp").astype(jnp.int32)
    g = lax.axis_index("grp").astype(jnp.int32)
    where = jnp.stack([tp // 16, (tp // 8) % 2, (tp // 2) % 4, tp % 2, g, g, g, g])

    tile = shape((HD, PART))
    quarters = pltpu.VMEM((2, GRP, QUARTER, PART), BF)
    x_own, theirs = call(init_body, [tile, tile], where, hidden, specs=[SM, VM])
    x_other = lax.ppermute(theirs, "tp", CORE_SWAP)
    lines = jnp.concatenate([norm_gain, q_bias.astype(F32)])
    columns = jnp.concatenate([lines, lax.ppermute(lines, "tp", CORE_SWAP)]).T
    keep, send = call(
        spread_body,
        [tile, tile],
        where,
        x_own,
        x_other,
        specs=[SM, VM, VM],
        scratch=[quarters],
    )
    x, block = call(
        join_body,
        [shape((ROWS, PART)), shape((ROWS + 16, PART))],
        where,
        keep,
        lax.ppermute(send, "grp", WORK_SWAP),
        columns,
        specs=[SM] + [VM] * 3,
    )

    kv_turned = call(
        turn_kv_body, shape((LAYERS, QUARTER, DEPTH + HD)), kv_weight, kv_bias.T
    )
    kv_own = lax.ppermute(kv_turned, "tp", KV_MOVE)
    q_turned = turn(q_weight)
    out_turned = turn(out_weight)

    inv = 1.0 / 1000000.0 ** (jnp.arange(HD // 2, dtype=F32) * 2.0 / HD)
    angle = inv[:, None] * jnp.arange(TOK, dtype=F32)[None, :]
    cosine, sine = jnp.cos(angle), jnp.sin(angle)

    for layer in range(LAYERS):
        if layer == 0:
            blocks, both, late, kv_own = gather(block, kv_own)
            bias = kv_own[:, :, DEPTH:]
            biases = (bias, lax.ppermute(bias, "tp", CORE_SWAP))
        else:
            blocks, both, late, _ = gather(block)
        wide = both_quarters(bundle(layer, q_turned[layer], kv_own), both, late)
        keep, send = call(
            partial_in_body,
            [shape((2 * IN + 8, PART), F32), shape((2 * IN + 16, PART))],
            where,
            *blocks,
            *wide,
            specs=[SM] + [VM] * 10,
            scratch=[
                pltpu.VMEM((2, 2 * IN, DEPTH), BF),
                pltpu.VMEM((2, DEPTH, 2 * PART), BF),
            ],
        )
        bias = of_layer(layer, QUARTER, HD)
        q, kv = call(
            functools.partial(reduced_in_body, layer),
            [shape((HD, 2 * PART)), shape((2, QUARTER, PART))],
            where,
            keep,
            lax.ppermute(send, "grp", WORK_SWAP),
            columns,
            *biases,
            cosine,
            sine,
            specs=[SM] + [VM] * 3 + [bias, bias, VM, VM],
        )
        kvs = jnp.stack([kv] + [lax.ppermute(kv, "tp", Y_SLOT[s]) for s in (1, 2, 3)])
        keep, send = call(
            attend_body,
            [tile, tile],
            where,
            lengths,
            q,
            kvs,
            lax.ppermute(kvs, "tp", CORE_SWAP),
            cosine,
            sine,
            specs=[SM, SM] + [VM] * 5,
            scratch=[pltpu.VMEM((HD, TOK), BF)] * 3 + [quarters],
        )
        block = jnp.concatenate([keep, lax.ppermute(send, "grp", WORK_SWAP)])
        blocks, both, late, _ = gather(block)
        wide = both_quarters(out_turned[layer], both, late)
        scratch = [
            pltpu.VMEM((2, ROWS, DEPTH), BF),
            pltpu.VMEM((2, DEPTH, 2 * PART), BF),
            pltpu.VMEM((ROWS, 2 * PART), F32),
        ]
        if layer < LAYERS - 1:
            keep, send = call(
                partial_out_body,
                [shape((ROWS, PART), F32), shape((ROWS, PART))],
                where,
                *blocks,
                *wide,
                specs=[SM] + [VM] * 10,
                scratch=scratch,
            )
            x, block = call(
                functools.partial(advance_body, layer + 1),
                [shape((ROWS, PART)), shape((ROWS + 16, PART))],
                where,
                x,
                keep,
                lax.ppermute(send, "grp", WORK_SWAP),
                columns,
                specs=[SM] + [VM] * 4,
            )
    keep, send = call(
        last_out_body,
        [shape((ROWS, PART), F32), shape((ROWS + HD, PART))],
        where,
        *blocks,
        *wide,
        x,
        specs=[SM] + [VM] * 11,
        scratch=scratch,
    )
    mine, theirs = call(
        total_body,
        [tile, tile],
        where,
        x,
        keep,
        lax.ppermute(send, "grp", WORK_SWAP),
        specs=[SM] + [VM] * 3,
        scratch=[quarters],
    )
    theirs = lax.ppermute(theirs, "tp", CORE_SWAP)
    return call(final_body, shape((1, TOK, HD)), where, mine, theirs, specs=[SM, VM, VM])


def solution(mesh):
    placed = (
        P("grp", None, "tp"),
        P("grp"),
        P(None, "tp"),
        P(None, None, "grp", "tp"),
        P(None, "tp"),
        P(None, None, "grp", "tp"),
        P(None, "tp"),
        P(None, None, "grp", "tp"),
    )
    return jax.shard_map(
        local, mesh=mesh, in_specs=placed, out_specs=P("grp", None, "tp"), check_vma=False
    )
```

```python
import functools

import jax
import jax.numpy as jnp
from jax import lax
from jax.experimental import pallas as pl
from jax.experimental.pallas import tpu as pltpu
from jax.sharding import PartitionSpec as P

D = 8192
HD = 128
LAYERS = 2
TOK = 256
GRP = 4
QUARTER = HD // GRP
PART = TOK // 2
WIDE = GRP * PART
DEPTH = 64 * QUARTER
IN = HD + QUARTER
ROWS = 2 * HD
BF = jnp.bfloat16
F32 = jnp.float32

VM = pl.BlockSpec(memory_space=pltpu.VMEM)
SM = pl.BlockSpec(memory_space=pltpu.SMEM)
ANY = pl.BlockSpec(memory_space=pl.ANY)
PARAMS = pltpu.CompilerParams(vmem_limit_bytes=40 * 1024 * 1024)


def tp_index(x, z, y, c):
    return ((x * 2 + z) * 4 + y) * 2 + c


COORDS = [
    (x, z, y, c) for x in range(4) for z in range(2) for y in range(4) for c in range(2)
]


def tp_perm(move):
    return [(tp_index(*at), tp_index(*move(*at))) for at in COORDS]


def along(x_first, s):
    def move(x, z, y, c):
        if (c == 0) == x_first:
            return ((x - s) % 4, z, y, c)
        return (x, z, (y - s) % 4, c)

    return tp_perm(move)


CORE_SWAP = tp_perm(lambda x, z, y, c: (x, z, y, 1 - c))
Z_SWAP = tp_perm(lambda x, z, y, c: (x, 1 - z, y, c))
FIRST = [along(True, s) for s in range(4)]
SECOND = [along(False, s) for s in range(4)]
Y_SLOT = [tp_perm(lambda x, z, y, c, s=s: (x, z, (y - s) % 4, c)) for s in range(4)]
G_XOR = [[(g, g ^ k) for g in range(GRP)] for k in range(GRP)]
WORK_SWAP, WEIGHT_SWAP = G_XOR[1], G_XOR[2]
KV_MOVE = [(m, 8 * ((m % 32) // 4) + 2 * (m % 4) + m // 32) for m in range(64)]


def split3(value):
    high = value.astype(BF)
    rest = value - high.astype(F32)
    middle = rest.astype(BF)
    low = (rest - middle.astype(F32)).astype(BF)
    return high, middle, low


def call(body, outs, *args, specs=None, scratch=()):
    return pl.pallas_call(
        body,
        grid=(1,),
        out_shape=outs,
        in_specs=specs or [VM] * len(args),
        out_specs=jax.tree.map(lambda _: VM, outs),
        scratch_shapes=list(scratch),
        compiler_params=PARAMS,
        cost_estimate=pl.CostEstimate(flops=0, bytes_accessed=1 << 10, transcendentals=0),
    )(*args)


def shape(dims, dtype=BF):
    return jax.ShapeDtypeStruct(dims, dtype)


def half_lanes(index):
    return pl.ds(pl.multiple_of(index * PART, PART), PART)


def pack_ss(ss):
    parts = [p.astype(F32) for p in split3(jnp.broadcast_to(ss, (16, ss.shape[1])))]
    row = lax.broadcasted_iota(jnp.int32, parts[0].shape, 0)
    out = jnp.zeros(parts[0].shape, F32)
    for i, part in enumerate(parts):
        out = jnp.where(row == i, part, out)
    return out.astype(BF)


def unpack_ss(rows):
    rows = rows.astype(F32)
    return rows[0:1] + rows[1:2] + rows[2:3]


def rotated(value, cosine, sine):
    first, second = value[:64], value[64:]
    return jnp.concatenate(
        [first * cosine - second * sine, second * cosine + first * sine], axis=0
    ).astype(BF)


def turn_body(weight, first, second):
    for layer, out in enumerate((first, second)):
        out[...] = weight[layer].reshape(DEPTH, HD).T


def turn(weight):
    return call(turn_body, [shape((HD, DEPTH))] * 2, weight)


def turn_kv_body(weight, bias, out):
    for layer in range(LAYERS):
        out[layer, :, :DEPTH] = weight[layer].reshape(DEPTH, QUARTER).T
        out[layer, :, DEPTH:] = jnp.broadcast_to(bias[:, layer : layer + 1], (QUARTER, HD))


def of_layer(layer, rows, depth, at=0):
    return pl.BlockSpec((1, rows, depth), lambda i: (layer, 0, at))


def bundle_body(wide, narrow, out):
    out[:HD, :] = wide[...]
    out[HD:, :] = narrow[0, :, :DEPTH]


def bundle(layer, wide, narrow):
    return call(
        bundle_body,
        shape((IN, DEPTH)),
        wide,
        narrow,
        specs=[VM, of_layer(layer, QUARTER, DEPTH + HD)],
    )


def with_other(*quarters):
    return [*quarters, *(lax.ppermute(w, "tp", CORE_SWAP) for w in quarters)]


def both_quarters(own, after, late):
    held, _ = lax.optimization_barrier((own, after))
    partner = lax.ppermute(held, "grp", WEIGHT_SWAP)
    here, *_ = lax.optimization_barrier((partner, *late))
    return [
        own,
        partner,
        lax.ppermute(own, "tp", CORE_SWAP),
        lax.ppermute(here, "tp", CORE_SWAP),
    ]


def rows_at(prompt, dc, qi):
    start = ((prompt * 2 + dc) * 2 + qi) * QUARTER
    return slice(start, start + QUARTER)


def share(where, tall, keep, send):
    g = where[4]
    for dc in range(2):
        for qi in range(2):
            keep[rows_at(0, dc, qi), :] = tall[dc, g ^ (2 * qi)]
            send[rows_at(0, dc, qi), :] = tall[dc, (g ^ 1) ^ (2 * qi)]


def init_body(where, hidden, mine, theirs):
    c = where[3]
    mine[...] = hidden[0, half_lanes(c), :].astype(F32).T.astype(BF)
    theirs[...] = hidden[0, half_lanes(1 - c), :].astype(F32).T.astype(BF)


def spread_body(where, own, other, keep, send, third, fourth, tall):
    g = where[4]
    tall[0] = own[...].reshape(GRP, QUARTER, PART)
    tall[1] = other[...].reshape(GRP, QUARTER, PART)
    share(where, tall, keep, send)
    for dc in range(2):
        third[dc * QUARTER : (dc + 1) * QUARTER, :] = tall[dc, g ^ 2]
        fourth[dc * QUARTER : (dc + 1) * QUARTER, :] = tall[dc, g ^ 3]


def emit_block(layer, where, values, columns, block):
    g = where[4]
    sums = []
    for prompt in range(2):
        squares = jnp.zeros((QUARTER, PART), F32)
        for dc in range(2):
            for qi in range(2):
                rows = rows_at(prompt, dc, qi)
                start = pl.multiple_of((g ^ (2 * qi)) * QUARTER, QUARTER)
                lane = 4 * dc + layer
                gain = columns[pl.ds(start, QUARTER), lane : lane + 1]
                value = values[rows]
                block[rows, :] = (value * gain).astype(BF)
                squares = squares + value * value
        ss = jnp.sum(squares, axis=0, keepdims=True)
        sums += [p.astype(F32) for p in split3(jnp.broadcast_to(ss, (8, PART)))]
    tile = jnp.concatenate([p[0:1] for p in sums] + [jnp.zeros((10, PART), F32)], axis=0)
    block[ROWS:, :] = tile.astype(BF)


def join_body(where, keep, came, third, fourth, columns, x, block):
    x[: ROWS // 2, :] = keep[...]
    x[ROWS // 2 :, :] = came[...]
    sums = []
    for prompt in range(GRP):
        squares = jnp.zeros((QUARTER, PART), F32)
        for dc in range(2):
            start = pl.multiple_of(where[4] * QUARTER, QUARTER)
            gain = columns[pl.ds(start, QUARTER), 4 * dc : 4 * dc + 1]
            if prompt < 2:
                value = x[rows_at(prompt, dc, 0), :].astype(F32)
            else:
                rows = slice(dc * QUARTER, (dc + 1) * QUARTER)
                value = (third, fourth)[prompt - 2][rows, :].astype(F32)
            at = (2 * prompt + dc) * QUARTER
            block[at : at + QUARTER, :] = (value * gain).astype(BF)
            squares = squares + value * value
        ss = jnp.sum(squares, axis=0, keepdims=True)
        sums += [p.astype(F32) for p in split3(jnp.broadcast_to(ss, (8, PART)))]
    tile = jnp.concatenate([p[0:1] for p in sums] + [jnp.zeros((4, PART), F32)], axis=0)
    block[ROWS:, :] = tile.astype(BF)


def gather(block, early=None):
    other = lax.ppermute(block, "tp", Z_SWAP)
    if early is not None:
        other, early = lax.optimization_barrier((other, early))
    both = jnp.stack([block, other])
    up = lax.ppermute(both, "tp", FIRST[1])
    across = lax.ppermute(both, "tp", FIRST[2])
    down = lax.ppermute(both, "tp", FIRST[3])
    up, across, down = lax.optimization_barrier((up, across, down))
    low, high = jnp.stack([both, up]), jnp.stack([across, down])
    low_up = lax.ppermute(low, "tp", SECOND[1])
    high_down = lax.ppermute(high, "tp", SECOND[3])
    high_up = lax.ppermute(high, "tp", SECOND[1])
    low_down = lax.ppermute(low, "tp", SECOND[3])
    low_across = lax.ppermute(low_up, "tp", SECOND[1])
    high_across = lax.ppermute(high_down, "tp", SECOND[3])
    blocks = (low, high, low_up, high_up, low_across, high_across, low_down, high_down)
    return blocks, both, blocks[2:], early


def arrivals(where, refs):
    x, z, y, c = where[0], where[1], where[2], where[3]
    for second in range(4):
        for first in range(4):
            ref, at = refs[2 * second + first // 2], first % 2
            col = (x + jnp.where(c == 0, first, second)) & 3
            row = (y + jnp.where(c == 0, second, first)) & 3
            for dz in range(2):
                yield (col * 2 + (z ^ dz)) * 4 + row, ref, at, dz


def block_rows(where, pair, dc):
    start = (2 * pair + (where[3] ^ dc)) * QUARTER
    return pl.ds(pl.multiple_of(start, QUARTER), QUARTER)


def place(where, blocks, placed):
    ss = [jnp.zeros((1, PART), F32) for _ in range(2)]
    for pair, ref, at, dz in arrivals(where, blocks):
        for prompt in range(2):
            lanes = slice(prompt * PART, (prompt + 1) * PART)
            for dc in range(2):
                for qi in range(2):
                    placed[qi, block_rows(where, pair, dc), lanes] = ref[
                        at, dz, rows_at(prompt, dc, qi), :
                    ]
        if ref.shape[2] > ROWS:
            sums = ref[at, dz, ROWS : ROWS + 16, :].astype(F32)
            for i in range(6):
                ss[i // 3] = ss[i // 3] + sums[i : i + 1]
    return ss


def pack_ss(ss):
    parts = [p.astype(F32) for p in split3(jnp.broadcast_to(ss, (16, ss.shape[1])))]
    row = lax.broadcasted_iota(jnp.int32, parts[0].shape, 0)
    out = jnp.zeros(parts[0].shape, F32)
    for i, part in enumerate(parts):
        out = jnp.where(row == i, part, out)
    return out.astype(BF)


def unpack_ss(rows):
    rows = rows.astype(F32)
    return rows[0:1] + rows[1:2] + rows[2:3]


def rotated(value, cosine, sine):
    first, second = value[:64], value[64:]
    return jnp.concatenate(
        [first * cosine - second * sine, second * cosine + first * sine], axis=0
    ).astype(BF)


def partial_in_body(where, *refs):
    blocks, parts = refs[0:8], refs[8:12]
    keep, send, weight, placed = refs[12:]
    ss = place(where, blocks, placed)
    out = jnp.zeros((2 * IN, 2 * PART), F32)
    for qi in range(2):
        for dc in range(2):
            weight[qi, dc * IN : (dc + 1) * IN, :] = parts[2 * dc + qi][...]
        out = out + jnp.dot(weight[qi], placed[qi], preferred_element_type=F32)
    keep[0 : 2 * IN, :] = out[:, :PART]
    keep[2 * IN :, :] = jnp.broadcast_to(ss[0], (8, PART))
    send[0 : 2 * IN, :] = out[:, PART:].astype(BF)
    send[2 * IN :, :] = pack_ss(ss[1])


def first_in_body(where, *refs):
    blocks, own, other = refs[0:8], refs[8], refs[9]
    keep, sends, (weight, placed) = refs[10], refs[11:14], refs[14:]
    weight[:IN, :] = own[...]
    weight[IN:, :] = other[...]
    ss = [jnp.zeros((1, PART), F32) for _ in range(GRP)]
    for pair, ref, at, dz in arrivals(where, blocks):
        sums = ref[at, dz, ROWS : ROWS + 16, :].astype(F32)
        for prompt in range(GRP):
            lanes = slice(prompt * PART, (prompt + 1) * PART)
            for dc in range(2):
                start = (2 * prompt + dc) * QUARTER
                placed[block_rows(where, pair, dc), lanes] = ref[
                    at, dz, start : start + QUARTER, :
                ]
            for i in range(3):
                ss[prompt] = ss[prompt] + sums[3 * prompt + i : 3 * prompt + i + 1]
    out = jnp.dot(weight[...], placed[...], preferred_element_type=F32)
    keep[0 : 2 * IN, :] = out[:, :PART]
    keep[2 * IN :, :] = jnp.broadcast_to(ss[0], (8, PART))
    for k, send in enumerate(sends, start=1):
        send[0 : 2 * IN, :] = out[:, k * PART : (k + 1) * PART].astype(BF)
        send[2 * IN :, :] = pack_ss(ss[k])


def finish(where, rows, scale, columns, layer, bias, cosine, sine, q, kv):
    c = where[3]
    half = half_lanes(c)
    cos, sin = cosine[:, half], sine[:, half]
    for dc in range(2):
        base = dc * IN
        lane = 4 * dc + 2 + layer
        value = rows[base : base + HD] * scale + columns[:, lane : lane + 1]
        q[:, dc * PART : (dc + 1) * PART] = rotated(value, cos, sin)
        column = bias[dc][0, :, 0:1].astype(F32)
        value = rows[base + HD : base + IN] * scale + column
        kv[c if dc == 0 else 1 - c] = value.astype(BF)


def reduced_in_body(layer, where, keep, *refs):
    came, (columns, bias, other_bias, cosine, sine, q, kv) = refs[:-7], refs[-7:]
    rows = keep[...]
    sums, ss = rows[: 2 * IN], rows[2 * IN : 2 * IN + 1]
    for ref in came:
        sums = sums + ref[0 : 2 * IN, :].astype(F32)
        ss = ss + unpack_ss(ref[2 * IN :, :])
    scale = lax.rsqrt(ss / D + 1e-06)
    finish(where, sums, scale, columns, layer, (bias, other_bias), cosine, sine, q, kv)


def attend_body(
    where, length, q, own, other, cosine, sine, keep, send, raw, keys, vals, tall
):
    y, c = where[2], where[3]
    for ref, half in ((own, half_lanes(c)), (other, half_lanes(1 - c))):
        for i in range(4):
            rows = slice(i * QUARTER, (i + 1) * QUARTER)
            slot = (i - y) & 3
            raw[rows, half] = ref[slot, 0]
            vals[rows, half] = ref[slot, 1]
    keys[...] = rotated(raw[...].astype(F32), cosine[...], sine[...])
    scores = lax.dot_general(
        keys[...], q[...], (((0,), (0,)), ((), ())), preferred_element_type=F32
    ) / jnp.sqrt(jnp.float32(HD))
    s_at = lax.broadcasted_iota(jnp.int32, (TOK, TOK), 0)
    t_at = (lax.broadcasted_iota(jnp.int32, (TOK, TOK), 1) & (PART - 1)) + c * PART
    allowed = (s_at <= t_at) & (s_at < length[0])
    scores = jnp.where(allowed, scores, -1e30)
    weights = jnp.exp(scores - jnp.max(scores, axis=0, keepdims=True))
    probs = (weights / jnp.sum(weights, axis=0, keepdims=True)).astype(BF)
    attended = jnp.dot(vals[...], probs, preferred_element_type=F32).astype(BF)
    for dc in range(2):
        part = attended[:, dc * PART : (dc + 1) * PART]
        tall[dc] = part.reshape(GRP, QUARTER, PART)
    share(where, tall, keep, send)


def multiply_out(where, blocks, parts, weight, placed, total):
    place(where, blocks, placed)
    out = jnp.zeros((ROWS, 2 * PART), F32)
    for qi in range(2):
        for dc in range(2):
            weight[qi, dc * HD : (dc + 1) * HD, :] = parts[2 * dc + qi][...]
        out = out + jnp.dot(weight[qi], placed[qi], preferred_element_type=F32)
    total[...] = out


def partial_out_body(where, *refs):
    blocks, parts = refs[0:8], refs[8:12]
    keep, send, weight, placed, total = refs[12:]
    g = where[4]
    multiply_out(where, blocks, parts, weight, placed, total)
    for prompt in range(2):
        lanes = slice(prompt * PART, (prompt + 1) * PART)
        for dc in range(2):
            for qi in range(2):
                here = pl.multiple_of(dc * HD + (g ^ (2 * qi)) * QUARTER, QUARTER)
                there = pl.multiple_of(dc * HD + ((g ^ 1) ^ (2 * qi)) * QUARTER, QUARTER)
                keep[rows_at(prompt, dc, qi), :] = total[pl.ds(here, QUARTER), lanes]
                sent = total[pl.ds(there, QUARTER), lanes].astype(BF)
                send[rows_at(1 - prompt, dc, qi), :] = sent


def advance_body(layer, where, x, keep, came, columns, new, block):
    value = x[...].astype(F32) + (keep[...] + came[...].astype(F32))
    new[...] = value.astype(BF)
    emit_block(layer, where, new[...].astype(F32), columns, block)


def last_out_body(where, *refs):
    blocks, parts, x = refs[0:8], refs[8:12], refs[12]
    keep, send, weight, placed, total = refs[13:]
    multiply_out(where, blocks, parts, weight, placed, total)
    keep[...] = total[:, :PART]
    send[:ROWS, :] = total[:, PART:].astype(BF)
    send[ROWS:, :] = x[ROWS // 2 :, :]


def total_body(where, x, keep, came, mine, theirs, tall):
    g = where[4]
    for dc in range(2):
        for qi in range(2):
            tall[dc, g ^ (2 * qi)] = x[rows_at(0, dc, qi), :]
            at = rows_at(0, dc, qi)
            tall[dc, (g ^ 1) ^ (2 * qi)] = came[ROWS + at.start : ROWS + at.stop, :]
    for dc, out in enumerate((mine, theirs)):
        rows = slice(dc * HD, (dc + 1) * HD)
        mixed = keep[rows, :] + came[rows, :].astype(F32)
        out[...] = (tall[dc].reshape(HD, PART).astype(F32) + mixed).astype(BF)


def final_body(where, mine, theirs, out):
    c = where[3]
    out[0, half_lanes(c), :] = mine[...].astype(F32).T.astype(BF)
    out[0, half_lanes(1 - c), :] = theirs[...].astype(F32).T.astype(BF)


def local(hidden, lengths, norm_gain, q_weight, q_bias, kv_weight, kv_bias, out_weight):
    tp = lax.axis_index("tp").astype(jnp.int32)
    g = lax.axis_index("grp").astype(jnp.int32)
    where = jnp.stack([tp // 16, (tp // 8) % 2, (tp // 2) % 4, tp % 2, g, g, g, g])

    tile = shape((HD, PART))
    quarters = pltpu.VMEM((2, GRP, QUARTER, PART), BF)
    x_own, theirs = call(init_body, [tile, tile], where, hidden, specs=[SM, VM])
    x_other = lax.ppermute(theirs, "tp", CORE_SWAP)
    lines = jnp.concatenate([norm_gain, q_bias.astype(F32)])
    columns = jnp.concatenate([lines, lax.ppermute(lines, "tp", CORE_SWAP)]).T
    part = shape((2 * QUARTER, PART))
    keep, *sends = call(
        spread_body,
        [tile, tile, part, part],
        where,
        x_own,
        x_other,
        specs=[SM, VM, VM],
        scratch=[quarters],
    )
    x, block = call(
        join_body,
        [shape((ROWS, PART)), shape((ROWS + 16, PART))],
        where,
        keep,
        *(lax.ppermute(sends[k - 1], "grp", G_XOR[k]) for k in (1, 2, 3)),
        columns,
        specs=[SM] + [VM] * 5,
    )

    kv_turned = call(
        turn_kv_body, shape((LAYERS, QUARTER, DEPTH + HD)), kv_weight, kv_bias.T
    )
    kv_own = lax.ppermute(kv_turned, "tp", KV_MOVE)
    q_turned = turn(q_weight)
    out_turned = turn(out_weight)

    inv = 1.0 / 1000000.0 ** (jnp.arange(HD // 2, dtype=F32) * 2.0 / HD)
    angle = inv[:, None] * jnp.arange(TOK, dtype=F32)[None, :]
    cosine, sine = jnp.cos(angle), jnp.sin(angle)

    for layer in range(LAYERS):
        if layer == 0:
            blocks, _, _, kv_own = gather(block, kv_own)
            bias = kv_own[:, :, DEPTH:]
            biases = (bias, lax.ppermute(bias, "tp", CORE_SWAP))
            bundles = [bundle(i, q_turned[i], kv_own) for i in range(LAYERS)]
            keep, *sends = call(
                first_in_body,
                [shape((2 * IN + 8, PART), F32)] + [shape((2 * IN + 16, PART))] * 3,
                where,
                *blocks,
                *with_other(bundles[0]),
                specs=[SM] + [VM] * 10,
                scratch=[pltpu.VMEM((2 * IN, DEPTH), BF), pltpu.VMEM((DEPTH, WIDE), BF)],
            )
        else:
            blocks, both, late, _ = gather(block)
            wide = both_quarters(bundles[layer], both, late)
            keep, *sends = call(
                partial_in_body,
                [shape((2 * IN + 8, PART), F32), shape((2 * IN + 16, PART))],
                where,
                *blocks,
                *wide,
                specs=[SM] + [VM] * 12,
                scratch=[
                    pltpu.VMEM((2, 2 * IN, DEPTH), BF),
                    pltpu.VMEM((2, DEPTH, 2 * PART), BF),
                ],
            )
        came = [lax.ppermute(send, "grp", G_XOR[k]) for k, send in enumerate(sends, start=1)]
        bias = of_layer(layer, QUARTER, HD)
        q, kv = call(
            functools.partial(reduced_in_body, layer),
            [shape((HD, 2 * PART)), shape((2, QUARTER, PART))],
            where,
            keep,
            *came,
            columns,
            *biases,
            cosine,
            sine,
            specs=[SM] + [VM] * (2 + len(came)) + [bias, bias, VM, VM],
        )
        kvs = jnp.stack([kv] + [lax.ppermute(kv, "tp", Y_SLOT[s]) for s in (1, 2, 3)])
        keep, send = call(
            attend_body,
            [tile, tile],
            where,
            lengths,
            q,
            kvs,
            lax.ppermute(kvs, "tp", CORE_SWAP),
            cosine,
            sine,
            specs=[SM, SM] + [VM] * 5,
            scratch=[pltpu.VMEM((HD, TOK), BF)] * 3 + [quarters],
        )
        block = jnp.concatenate([keep, lax.ppermute(send, "grp", WORK_SWAP)])
        blocks, both, late, _ = gather(block)
        wide = both_quarters(out_turned[layer], both, late)
        scratch = [
            pltpu.VMEM((2, ROWS, DEPTH), BF),
            pltpu.VMEM((2, DEPTH, 2 * PART), BF),
            pltpu.VMEM((ROWS, 2 * PART), F32),
        ]
        if layer < LAYERS - 1:
            keep, send = call(
                partial_out_body,
                [shape((ROWS, PART), F32), shape((ROWS, PART))],
                where,
                *blocks,
                *wide,
                specs=[SM] + [VM] * 12,
                scratch=scratch,
            )
            x, block = call(
                functools.partial(advance_body, layer + 1),
                [shape((ROWS, PART)), shape((ROWS + 16, PART))],
                where,
                x,
                keep,
                lax.ppermute(send, "grp", WORK_SWAP),
                columns,
                specs=[SM] + [VM] * 4,
            )
    keep, send = call(
        last_out_body,
        [shape((ROWS, PART), F32), shape((ROWS + HD, PART))],
        where,
        *blocks,
        *wide,
        x,
        specs=[SM] + [VM] * 13,
        scratch=scratch,
    )
    mine, theirs = call(
        total_body,
        [tile, tile],
        where,
        x,
        keep,
        lax.ppermute(send, "grp", WORK_SWAP),
        specs=[SM] + [VM] * 3,
        scratch=[quarters],
    )
    theirs = lax.ppermute(theirs, "tp", CORE_SWAP)
    return call(final_body, shape((1, TOK, HD)), where, mine, theirs, specs=[SM, VM, VM])


def solution(mesh):
    placed = (
        P("grp", None, "tp"),
        P("grp"),
        P(None, "tp"),
        P(None, None, "grp", "tp"),
        P(None, "tp"),
        P(None, None, "grp", "tp"),
        P(None, "tp"),
        P(None, None, "grp", "tp"),
    )
    return jax.shard_map(
        local, mesh=mesh, in_specs=placed, out_specs=P("grp", None, "tp"), check_vma=False
    )
```

```python
import functools

import jax
import jax.numpy as jnp
from jax import lax
from jax.experimental import pallas as pl
from jax.experimental.pallas import tpu as pltpu
from jax.sharding import PartitionSpec as P

D = 8192
HD = 128
LAYERS = 2
TOK = 256
GRP = 4
QUARTER = HD // GRP
PART = TOK // 2
WIDE = GRP * PART
DEPTH = 64 * QUARTER
IN = HD + QUARTER
ROWS = 2 * HD
BF = jnp.bfloat16
F32 = jnp.float32

VM = pl.BlockSpec(memory_space=pltpu.VMEM)
SM = pl.BlockSpec(memory_space=pltpu.SMEM)
ANY = pl.BlockSpec(memory_space=pl.ANY)
PARAMS = pltpu.CompilerParams(vmem_limit_bytes=40 * 1024 * 1024)


def tp_index(x, z, y, c):
    return ((x * 2 + z) * 4 + y) * 2 + c


COORDS = [
    (x, z, y, c) for x in range(4) for z in range(2) for y in range(4) for c in range(2)
]


def tp_perm(move):
    return [(tp_index(*at), tp_index(*move(*at))) for at in COORDS]


def along(x_first, s):
    def move(x, z, y, c):
        if (c == 0) == x_first:
            return ((x - s) % 4, z, y, c)
        return (x, z, (y - s) % 4, c)

    return tp_perm(move)


CORE_SWAP = tp_perm(lambda x, z, y, c: (x, z, y, 1 - c))
Z_SWAP = tp_perm(lambda x, z, y, c: (x, 1 - z, y, c))
FIRST = [along(True, s) for s in range(4)]
SECOND = [along(False, s) for s in range(4)]
Y_SLOT = [tp_perm(lambda x, z, y, c, s=s: (x, z, (y - s) % 4, c)) for s in range(4)]
G_XOR = [[(g, g ^ k) for g in range(GRP)] for k in range(GRP)]
WORK_SWAP, WEIGHT_SWAP = G_XOR[1], G_XOR[2]
KV_MOVE = [(m, 8 * ((m % 32) // 4) + 2 * (m % 4) + m // 32) for m in range(64)]


def split3(value):
    high = value.astype(BF)
    rest = value - high.astype(F32)
    middle = rest.astype(BF)
    low = (rest - middle.astype(F32)).astype(BF)
    return high, middle, low


def call(body, outs, *args, specs=None, scratch=()):
    return pl.pallas_call(
        body,
        grid=(1,),
        out_shape=outs,
        in_specs=specs or [VM] * len(args),
        out_specs=jax.tree.map(lambda _: VM, outs),
        scratch_shapes=list(scratch),
        compiler_params=PARAMS,
        cost_estimate=pl.CostEstimate(flops=0, bytes_accessed=1 << 10, transcendentals=0),
    )(*args)


def shape(dims, dtype=BF):
    return jax.ShapeDtypeStruct(dims, dtype)


def half_lanes(index):
    return pl.ds(pl.multiple_of(index * PART, PART), PART)


def pack_ss(ss):
    parts = [p.astype(F32) for p in split3(jnp.broadcast_to(ss, (16, ss.shape[1])))]
    row = lax.broadcasted_iota(jnp.int32, parts[0].shape, 0)
    out = jnp.zeros(parts[0].shape, F32)
    for i, part in enumerate(parts):
        out = jnp.where(row == i, part, out)
    return out.astype(BF)


def unpack_ss(rows):
    rows = rows.astype(F32)
    return rows[0:1] + rows[1:2] + rows[2:3]


def rotated(value, cosine, sine):
    first, second = value[:64], value[64:]
    return jnp.concatenate(
        [first * cosine - second * sine, second * cosine + first * sine], axis=0
    ).astype(BF)


def turn_body(weight, first, second):
    for layer, out in enumerate((first, second)):
        out[...] = weight[layer].reshape(DEPTH, HD).T


def turn(weight):
    return call(turn_body, [shape((HD, DEPTH))] * 2, weight)


def turn_kv_body(weight, bias, out):
    for layer in range(LAYERS):
        out[layer, :, :DEPTH] = weight[layer].reshape(DEPTH, QUARTER).T
        out[layer, :, DEPTH:] = jnp.broadcast_to(bias[:, layer : layer + 1], (QUARTER, HD))


def of_layer(layer, rows, depth, at=0):
    return pl.BlockSpec((1, rows, depth), lambda i: (layer, 0, at))


def bundle_body(wide, narrow, out):
    out[:HD, :] = wide[...]
    out[HD:, :] = narrow[0, :, :DEPTH]


def bundle(layer, wide, narrow):
    return call(
        bundle_body,
        shape((IN, DEPTH)),
        wide,
        narrow,
        specs=[VM, of_layer(layer, QUARTER, DEPTH + HD)],
    )


def with_other(*quarters):
    return [*quarters, *(lax.ppermute(w, "tp", CORE_SWAP) for w in quarters)]


def both_quarters(own, after, late):
    held, _ = lax.optimization_barrier((own, after))
    partner = lax.ppermute(held, "grp", WEIGHT_SWAP)
    here, *_ = lax.optimization_barrier((partner, *late))
    return [
        own,
        partner,
        lax.ppermute(own, "tp", CORE_SWAP),
        lax.ppermute(here, "tp", CORE_SWAP),
    ]


def rows_at(prompt, dc, qi):
    start = ((prompt * 2 + dc) * 2 + qi) * QUARTER
    return slice(start, start + QUARTER)


def share(where, tall, keep, send):
    g = where[4]
    for dc in range(2):
        for qi in range(2):
            keep[rows_at(0, dc, qi), :] = tall[dc, g ^ (2 * qi)]
            send[rows_at(0, dc, qi), :] = tall[dc, (g ^ 1) ^ (2 * qi)]


def init_body(where, hidden, mine, theirs):
    c = where[3]
    mine[...] = hidden[0, half_lanes(c), :].astype(F32).T.astype(BF)
    theirs[...] = hidden[0, half_lanes(1 - c), :].astype(F32).T.astype(BF)


def spread_body(where, own, other, keep, send, third, fourth, tall):
    g = where[4]
    tall[0] = own[...].reshape(GRP, QUARTER, PART)
    tall[1] = other[...].reshape(GRP, QUARTER, PART)
    share(where, tall, keep, send)
    for dc in range(2):
        third[dc * QUARTER : (dc + 1) * QUARTER, :] = tall[dc, g ^ 2]
        fourth[dc * QUARTER : (dc + 1) * QUARTER, :] = tall[dc, g ^ 3]


def emit_block(layer, where, values, columns, block):
    g = where[4]
    sums = []
    for prompt in range(2):
        squares = jnp.zeros((QUARTER, PART), F32)
        for dc in range(2):
            for qi in range(2):
                rows = rows_at(prompt, dc, qi)
                start = pl.multiple_of((g ^ (2 * qi)) * QUARTER, QUARTER)
                lane = 4 * dc + layer
                gain = columns[pl.ds(start, QUARTER), lane : lane + 1]
                value = values[rows]
                block[rows, :] = (value * gain).astype(BF)
                squares = squares + value * value
        ss = jnp.sum(squares, axis=0, keepdims=True)
        sums += [p.astype(F32) for p in split3(jnp.broadcast_to(ss, (8, PART)))]
    tile = jnp.concatenate([p[0:1] for p in sums] + [jnp.zeros((10, PART), F32)], axis=0)
    block[ROWS:, :] = tile.astype(BF)


def join_body(where, keep, came, third, fourth, columns, x, block):
    x[: ROWS // 2, :] = keep[...]
    x[ROWS // 2 :, :] = came[...]
    sums = []
    for prompt in range(GRP):
        squares = jnp.zeros((QUARTER, PART), F32)
        for dc in range(2):
            start = pl.multiple_of(where[4] * QUARTER, QUARTER)
            gain = columns[pl.ds(start, QUARTER), 4 * dc : 4 * dc + 1]
            if prompt < 2:
                value = x[rows_at(prompt, dc, 0), :].astype(F32)
            else:
                rows = slice(dc * QUARTER, (dc + 1) * QUARTER)
                value = (third, fourth)[prompt - 2][rows, :].astype(F32)
            at = (2 * prompt + dc) * QUARTER
            block[at : at + QUARTER, :] = (value * gain).astype(BF)
            squares = squares + value * value
        ss = jnp.sum(squares, axis=0, keepdims=True)
        sums += [p.astype(F32) for p in split3(jnp.broadcast_to(ss, (8, PART)))]
    tile = jnp.concatenate([p[0:1] for p in sums] + [jnp.zeros((4, PART), F32)], axis=0)
    block[ROWS:, :] = tile.astype(BF)


def gather(block, early=None):
    other = lax.ppermute(block, "tp", Z_SWAP)
    if early is not None:
        other, early = lax.optimization_barrier((other, early))
    both = jnp.stack([block, other])
    up = lax.ppermute(both, "tp", FIRST[1])
    across = lax.ppermute(both, "tp", FIRST[2])
    down = lax.ppermute(both, "tp", FIRST[3])
    up, across, down = lax.optimization_barrier((up, across, down))
    low, high = jnp.stack([both, up]), jnp.stack([across, down])
    low_up = lax.ppermute(low, "tp", SECOND[1])
    high_down = lax.ppermute(high, "tp", SECOND[3])
    high_up = lax.ppermute(high, "tp", SECOND[1])
    low_down = lax.ppermute(low, "tp", SECOND[3])
    low_across = lax.ppermute(low_up, "tp", SECOND[1])
    high_across = lax.ppermute(high_down, "tp", SECOND[3])
    blocks = (low, high, low_up, high_up, low_across, high_across, low_down, high_down)
    return blocks, both, blocks[2:], early


def each_arrival(where, refs, visit):
    x, z, y, c = where[0], where[1], where[2], where[3]
    for index, ref in enumerate(refs):
        second, half = index // 2, index % 2

        def body(i, carry, ref=ref, second=second, half=half):
            at, dz = i // 2, i % 2
            first = 2 * half + at
            col = (x + jnp.where(c == 0, first, second)) & 3
            row = (y + jnp.where(c == 0, second, first)) & 3
            visit((col * 2 + (z ^ dz)) * 4 + row, ref, at, dz)
            return carry

        lax.fori_loop(0, 4, body, 0)


CHUNK = 512


def multiply(own, other, placed, total, index=None):
    def body(i, carry):
        at = pl.ds(pl.multiple_of(i * CHUNK, CHUNK), CHUNK)
        left = jnp.concatenate([own[:, at], other[:, at]], axis=0)
        right = placed[at, :] if index is None else placed[index, at, :]
        total[...] += jnp.dot(left, right, preferred_element_type=F32)
        return carry

    lax.fori_loop(0, DEPTH // CHUNK, body, 0)


def block_rows(where, pair, dc):
    start = (2 * pair + (where[3] ^ dc)) * QUARTER
    return pl.ds(pl.multiple_of(start, QUARTER), QUARTER)


def place(where, blocks, placed, sums):
    if sums is not None:
        sums[...] = jnp.zeros_like(sums)

    def visit(pair, ref, at, dz):
        for prompt in range(2):
            lanes = slice(prompt * PART, (prompt + 1) * PART)
            for dc in range(2):
                for qi in range(2):
                    placed[qi, block_rows(where, pair, dc), lanes] = ref[
                        at, dz, rows_at(prompt, dc, qi), :
                    ]
        if sums is not None:
            sums[...] += ref[at, dz, ROWS : ROWS + 16, :].astype(F32)

    each_arrival(where, blocks, visit)


def sum_of(sums, prompt):
    row = 3 * prompt
    return sums[row : row + 1, :] + sums[row + 1 : row + 2, :] + sums[row + 2 : row + 3, :]


def pack_ss(ss):
    parts = [p.astype(F32) for p in split3(jnp.broadcast_to(ss, (16, ss.shape[1])))]
    row = lax.broadcasted_iota(jnp.int32, parts[0].shape, 0)
    out = jnp.zeros(parts[0].shape, F32)
    for i, part in enumerate(parts):
        out = jnp.where(row == i, part, out)
    return out.astype(BF)


def unpack_ss(rows):
    rows = rows.astype(F32)
    return rows[0:1] + rows[1:2] + rows[2:3]


def rotated(value, cosine, sine):
    first, second = value[:64], value[64:]
    return jnp.concatenate(
        [first * cosine - second * sine, second * cosine + first * sine], axis=0
    ).astype(BF)


def partial_in_body(where, *refs):
    blocks, parts = refs[0:8], refs[8:12]
    keep, send, placed, total, sums = refs[12:]
    place(where, blocks, placed, sums)
    total[...] = jnp.zeros_like(total)
    for qi in range(2):
        multiply(parts[qi], parts[2 + qi], placed, total, qi)
    keep[0 : 2 * IN, :] = total[:, :PART]
    keep[2 * IN :, :] = jnp.broadcast_to(sum_of(sums, 0), (8, PART))
    send[0 : 2 * IN, :] = total[:, PART:].astype(BF)
    send[2 * IN :, :] = pack_ss(sum_of(sums, 1))


def first_in_body(where, *refs):
    blocks, own, other = refs[0:8], refs[8], refs[9]
    keep, sends, (placed, total, sums) = refs[10], refs[11:14], refs[14:]
    sums[...] = jnp.zeros_like(sums)

    def visit(pair, ref, at, dz):
        for prompt in range(GRP):
            lanes = slice(prompt * PART, (prompt + 1) * PART)
            for dc in range(2):
                start = (2 * prompt + dc) * QUARTER
                placed[block_rows(where, pair, dc), lanes] = ref[
                    at, dz, start : start + QUARTER, :
                ]
        sums[...] += ref[at, dz, ROWS : ROWS + 16, :].astype(F32)

    each_arrival(where, blocks, visit)
    total[...] = jnp.zeros_like(total)
    multiply(own, other, placed, total)
    keep[0 : 2 * IN, :] = total[:, :PART]
    keep[2 * IN :, :] = jnp.broadcast_to(sum_of(sums, 0), (8, PART))
    for k, send in enumerate(sends, start=1):
        send[0 : 2 * IN, :] = total[:, k * PART : (k + 1) * PART].astype(BF)
        send[2 * IN :, :] = pack_ss(sum_of(sums, k))


def finish(where, rows, scale, columns, layer, bias, cosine, sine, q, kv):
    c = where[3]
    half = half_lanes(c)
    cos, sin = cosine[:, half], sine[:, half]
    for dc in range(2):
        base = dc * IN
        lane = 4 * dc + 2 + layer
        value = rows[base : base + HD] * scale + columns[:, lane : lane + 1]
        q[:, dc * PART : (dc + 1) * PART] = rotated(value, cos, sin)
        column = bias[dc][0, :, 0:1].astype(F32)
        value = rows[base + HD : base + IN] * scale + column
        kv[c if dc == 0 else 1 - c] = value.astype(BF)


def reduced_in_body(layer, where, keep, *refs):
    came, (columns, bias, other_bias, cosine, sine, q, kv) = refs[:-7], refs[-7:]
    rows = keep[...]
    sums, ss = rows[: 2 * IN], rows[2 * IN : 2 * IN + 1]
    for ref in came:
        sums = sums + ref[0 : 2 * IN, :].astype(F32)
        ss = ss + unpack_ss(ref[2 * IN :, :])
    scale = lax.rsqrt(ss / D + 1e-06)
    finish(where, sums, scale, columns, layer, (bias, other_bias), cosine, sine, q, kv)


def attend_body(
    where, length, q, own, other, cosine, sine, keep, send, raw, keys, vals, tall
):
    y, c = where[2], where[3]
    for ref, half in ((own, half_lanes(c)), (other, half_lanes(1 - c))):
        for i in range(4):
            rows = slice(i * QUARTER, (i + 1) * QUARTER)
            slot = (i - y) & 3
            raw[rows, half] = ref[slot, 0]
            vals[rows, half] = ref[slot, 1]
    keys[...] = rotated(raw[...].astype(F32), cosine[...], sine[...])
    scores = lax.dot_general(
        keys[...], q[...], (((0,), (0,)), ((), ())), preferred_element_type=F32
    ) / jnp.sqrt(jnp.float32(HD))
    s_at = lax.broadcasted_iota(jnp.int32, (TOK, TOK), 0)
    t_at = (lax.broadcasted_iota(jnp.int32, (TOK, TOK), 1) & (PART - 1)) + c * PART
    allowed = (s_at <= t_at) & (s_at < length[0])
    scores = jnp.where(allowed, scores, -1e30)
    weights = jnp.exp(scores - jnp.max(scores, axis=0, keepdims=True))
    probs = (weights / jnp.sum(weights, axis=0, keepdims=True)).astype(BF)
    attended = jnp.dot(vals[...], probs, preferred_element_type=F32).astype(BF)
    for dc in range(2):
        part = attended[:, dc * PART : (dc + 1) * PART]
        tall[dc] = part.reshape(GRP, QUARTER, PART)
    share(where, tall, keep, send)


def multiply_out(where, blocks, parts, placed, total):
    place(where, blocks, placed, None)
    total[...] = jnp.zeros_like(total)
    for qi in range(2):
        multiply(parts[qi], parts[2 + qi], placed, total, qi)


def partial_out_body(where, *refs):
    blocks, parts = refs[0:8], refs[8:12]
    keep, send, placed, total = refs[12:]
    g = where[4]
    multiply_out(where, blocks, parts, placed, total)
    for prompt in range(2):
        lanes = slice(prompt * PART, (prompt + 1) * PART)
        for dc in range(2):
            for qi in range(2):
                here = pl.multiple_of(dc * HD + (g ^ (2 * qi)) * QUARTER, QUARTER)
                there = pl.multiple_of(dc * HD + ((g ^ 1) ^ (2 * qi)) * QUARTER, QUARTER)
                keep[rows_at(prompt, dc, qi), :] = total[pl.ds(here, QUARTER), lanes]
                sent = total[pl.ds(there, QUARTER), lanes].astype(BF)
                send[rows_at(1 - prompt, dc, qi), :] = sent


def advance_body(layer, where, x, keep, came, columns, new, block):
    value = x[...].astype(F32) + (keep[...] + came[...].astype(F32))
    new[...] = value.astype(BF)
    emit_block(layer, where, new[...].astype(F32), columns, block)


def last_out_body(where, *refs):
    blocks, parts, x = refs[0:8], refs[8:12], refs[12]
    keep, send, placed, total = refs[13:]
    multiply_out(where, blocks, parts, placed, total)
    keep[...] = total[:, :PART]
    send[:ROWS, :] = total[:, PART:].astype(BF)
    send[ROWS:, :] = x[ROWS // 2 :, :]


def total_body(where, x, keep, came, mine, theirs, tall):
    g = where[4]
    for dc in range(2):
        for qi in range(2):
            tall[dc, g ^ (2 * qi)] = x[rows_at(0, dc, qi), :]
            at = rows_at(0, dc, qi)
            tall[dc, (g ^ 1) ^ (2 * qi)] = came[ROWS + at.start : ROWS + at.stop, :]
    for dc, out in enumerate((mine, theirs)):
        rows = slice(dc * HD, (dc + 1) * HD)
        mixed = keep[rows, :] + came[rows, :].astype(F32)
        out[...] = (tall[dc].reshape(HD, PART).astype(F32) + mixed).astype(BF)


def final_body(where, mine, theirs, out):
    c = where[3]
    out[0, half_lanes(c), :] = mine[...].astype(F32).T.astype(BF)
    out[0, half_lanes(1 - c), :] = theirs[...].astype(F32).T.astype(BF)


def local(hidden, lengths, norm_gain, q_weight, q_bias, kv_weight, kv_bias, out_weight):
    tp = lax.axis_index("tp").astype(jnp.int32)
    g = lax.axis_index("grp").astype(jnp.int32)
    where = jnp.stack([tp // 16, (tp // 8) % 2, (tp // 2) % 4, tp % 2, g, g, g, g])

    tile = shape((HD, PART))
    quarters = pltpu.VMEM((2, GRP, QUARTER, PART), BF)
    x_own, theirs = call(init_body, [tile, tile], where, hidden, specs=[SM, VM])
    x_other = lax.ppermute(theirs, "tp", CORE_SWAP)
    lines = jnp.concatenate([norm_gain, q_bias.astype(F32)])
    columns = jnp.concatenate([lines, lax.ppermute(lines, "tp", CORE_SWAP)]).T
    part = shape((2 * QUARTER, PART))
    keep, *sends = call(
        spread_body,
        [tile, tile, part, part],
        where,
        x_own,
        x_other,
        specs=[SM, VM, VM],
        scratch=[quarters],
    )
    x, block = call(
        join_body,
        [shape((ROWS, PART)), shape((ROWS + 16, PART))],
        where,
        keep,
        *(lax.ppermute(sends[k - 1], "grp", G_XOR[k]) for k in (1, 2, 3)),
        columns,
        specs=[SM] + [VM] * 5,
    )

    kv_turned = call(
        turn_kv_body, shape((LAYERS, QUARTER, DEPTH + HD)), kv_weight, kv_bias.T
    )
    kv_own = lax.ppermute(kv_turned, "tp", KV_MOVE)
    q_turned = turn(q_weight)
    out_turned = turn(out_weight)

    inv = 1.0 / 1000000.0 ** (jnp.arange(HD // 2, dtype=F32) * 2.0 / HD)
    angle = inv[:, None] * jnp.arange(TOK, dtype=F32)[None, :]
    cosine, sine = jnp.cos(angle), jnp.sin(angle)

    for layer in range(LAYERS):
        if layer == 0:
            blocks, _, _, kv_own = gather(block, kv_own)
            bias = kv_own[:, :, DEPTH:]
            biases = (bias, lax.ppermute(bias, "tp", CORE_SWAP))
            bundles = [bundle(i, q_turned[i], kv_own) for i in range(LAYERS)]
            keep, *sends = call(
                first_in_body,
                [shape((2 * IN + 8, PART), F32)] + [shape((2 * IN + 16, PART))] * 3,
                where,
                *blocks,
                *with_other(bundles[0]),
                specs=[SM] + [VM] * 10,
                scratch=[
                    pltpu.VMEM((DEPTH, WIDE), BF),
                    pltpu.VMEM((2 * IN, WIDE), F32),
                    pltpu.VMEM((16, PART), F32),
                ],
            )
        else:
            blocks, both, late, _ = gather(block)
            wide = both_quarters(bundles[layer], both, late)
            keep, *sends = call(
                partial_in_body,
                [shape((2 * IN + 8, PART), F32), shape((2 * IN + 16, PART))],
                where,
                *blocks,
                *wide,
                specs=[SM] + [VM] * 12,
                scratch=[
                    pltpu.VMEM((2, DEPTH, 2 * PART), BF),
                    pltpu.VMEM((2 * IN, 2 * PART), F32),
                    pltpu.VMEM((16, PART), F32),
                ],
            )
        came = [lax.ppermute(send, "grp", G_XOR[k]) for k, send in enumerate(sends, start=1)]
        bias = of_layer(layer, QUARTER, HD)
        q, kv = call(
            functools.partial(reduced_in_body, layer),
            [shape((HD, 2 * PART)), shape((2, QUARTER, PART))],
            where,
            keep,
            *came,
            columns,
            *biases,
            cosine,
            sine,
            specs=[SM] + [VM] * (2 + len(came)) + [bias, bias, VM, VM],
        )
        kvs = jnp.stack([kv] + [lax.ppermute(kv, "tp", Y_SLOT[s]) for s in (1, 2, 3)])
        keep, send = call(
            attend_body,
            [tile, tile],
            where,
            lengths,
            q,
            kvs,
            lax.ppermute(kvs, "tp", CORE_SWAP),
            cosine,
            sine,
            specs=[SM, SM] + [VM] * 5,
            scratch=[pltpu.VMEM((HD, TOK), BF)] * 3 + [quarters],
        )
        block = jnp.concatenate([keep, lax.ppermute(send, "grp", WORK_SWAP)])
        blocks, both, late, _ = gather(block)
        wide = both_quarters(out_turned[layer], both, late)
        scratch = [
            pltpu.VMEM((2, DEPTH, 2 * PART), BF),
            pltpu.VMEM((ROWS, 2 * PART), F32),
        ]
        if layer < LAYERS - 1:
            keep, send = call(
                partial_out_body,
                [shape((ROWS, PART), F32), shape((ROWS, PART))],
                where,
                *blocks,
                *wide,
                specs=[SM] + [VM] * 12,
                scratch=scratch,
            )
            x, block = call(
                functools.partial(advance_body, layer + 1),
                [shape((ROWS, PART)), shape((ROWS + 16, PART))],
                where,
                x,
                keep,
                lax.ppermute(send, "grp", WORK_SWAP),
                columns,
                specs=[SM] + [VM] * 4,
            )
    keep, send = call(
        last_out_body,
        [shape((ROWS, PART), F32), shape((ROWS + HD, PART))],
        where,
        *blocks,
        *wide,
        x,
        specs=[SM] + [VM] * 13,
        scratch=scratch,
    )
    mine, theirs = call(
        total_body,
        [tile, tile],
        where,
        x,
        keep,
        lax.ppermute(send, "grp", WORK_SWAP),
        specs=[SM] + [VM] * 3,
        scratch=[quarters],
    )
    theirs = lax.ppermute(theirs, "tp", CORE_SWAP)
    return call(final_body, shape((1, TOK, HD)), where, mine, theirs, specs=[SM, VM, VM])


def solution(mesh):
    placed = (
        P("grp", None, "tp"),
        P("grp"),
        P(None, "tp"),
        P(None, None, "grp", "tp"),
        P(None, "tp"),
        P(None, None, "grp", "tp"),
        P(None, "tp"),
        P(None, None, "grp", "tp"),
    )
    return jax.shard_map(
        local, mesh=mesh, in_specs=placed, out_specs=P("grp", None, "tp"), check_vma=False
    )
```

```python
import functools

import jax
import jax.numpy as jnp
from jax import lax
from jax.experimental import pallas as pl
from jax.experimental.pallas import tpu as pltpu
from jax.sharding import PartitionSpec as P

D = 8192
HD = 128
LAYERS = 2
TOK = 256
GRP = 4
QUARTER = HD // GRP
PART = TOK // 2
WIDE = GRP * PART
DEPTH = 64 * QUARTER
IN = HD + QUARTER
ROWS = 2 * HD
BF = jnp.bfloat16
F32 = jnp.float32

VM = pl.BlockSpec(memory_space=pltpu.VMEM)
SM = pl.BlockSpec(memory_space=pltpu.SMEM)
ANY = pl.BlockSpec(memory_space=pl.ANY)
PARAMS = pltpu.CompilerParams(vmem_limit_bytes=40 * 1024 * 1024)


def tp_index(x, z, y, c):
    return ((x * 2 + z) * 4 + y) * 2 + c


COORDS = [
    (x, z, y, c) for x in range(4) for z in range(2) for y in range(4) for c in range(2)
]


def tp_perm(move):
    return [(tp_index(*at), tp_index(*move(*at))) for at in COORDS]


def along(x_first, s):
    def move(x, z, y, c):
        if (c == 0) == x_first:
            return ((x - s) % 4, z, y, c)
        return (x, z, (y - s) % 4, c)

    return tp_perm(move)


CORE_SWAP = tp_perm(lambda x, z, y, c: (x, z, y, 1 - c))
Z_SWAP = tp_perm(lambda x, z, y, c: (x, 1 - z, y, c))
FIRST = [along(True, s) for s in range(4)]
SECOND = [along(False, s) for s in range(4)]
Y_SLOT = [tp_perm(lambda x, z, y, c, s=s: (x, z, (y - s) % 4, c)) for s in range(4)]
G_XOR = [[(g, g ^ k) for g in range(GRP)] for k in range(GRP)]
WORK_SWAP, WEIGHT_SWAP = G_XOR[1], G_XOR[2]
KV_MOVE = [(m, 8 * ((m % 32) // 4) + 2 * (m % 4) + m // 32) for m in range(64)]


def split3(value):
    high = value.astype(BF)
    rest = value - high.astype(F32)
    middle = rest.astype(BF)
    low = (rest - middle.astype(F32)).astype(BF)
    return high, middle, low


def call(body, outs, *args, specs=None, scratch=()):
    return pl.pallas_call(
        body,
        grid=(1,),
        out_shape=outs,
        in_specs=specs or [VM] * len(args),
        out_specs=jax.tree.map(lambda _: VM, outs),
        scratch_shapes=list(scratch),
        compiler_params=PARAMS,
        cost_estimate=pl.CostEstimate(flops=0, bytes_accessed=1 << 10, transcendentals=0),
    )(*args)


def shape(dims, dtype=BF):
    return jax.ShapeDtypeStruct(dims, dtype)


def half_lanes(index):
    return pl.ds(pl.multiple_of(index * PART, PART), PART)


def pack_ss(ss):
    parts = [p.astype(F32) for p in split3(jnp.broadcast_to(ss, (16, ss.shape[1])))]
    row = lax.broadcasted_iota(jnp.int32, parts[0].shape, 0)
    out = jnp.zeros(parts[0].shape, F32)
    for i, part in enumerate(parts):
        out = jnp.where(row == i, part, out)
    return out.astype(BF)


def unpack_ss(rows):
    rows = rows.astype(F32)
    return rows[0:1] + rows[1:2] + rows[2:3]


def rotated(value, cosine, sine):
    first, second = value[:64], value[64:]
    return jnp.concatenate(
        [first * cosine - second * sine, second * cosine + first * sine], axis=0
    ).astype(BF)


def turn_body(weight, first, second):
    for layer, out in enumerate((first, second)):
        out[...] = weight[layer].reshape(DEPTH, HD).T


def turn(weight):
    return call(turn_body, [shape((HD, DEPTH))] * 2, weight)


def turn_kv_body(weight, bias, out):
    for layer in range(LAYERS):
        out[layer, :, :DEPTH] = weight[layer].reshape(DEPTH, QUARTER).T
        out[layer, :, DEPTH:] = jnp.broadcast_to(bias[:, layer : layer + 1], (QUARTER, HD))


def of_layer(layer, rows, depth, at=0):
    return pl.BlockSpec((1, rows, depth), lambda i: (layer, 0, at))


def bundle_body(wide, narrow, out):
    out[:HD, :] = wide[...]
    out[HD:, :] = narrow[0, :, :DEPTH]


def bundle(layer, wide, narrow):
    return call(
        bundle_body,
        shape((IN, DEPTH)),
        wide,
        narrow,
        specs=[VM, of_layer(layer, QUARTER, DEPTH + HD)],
    )


def with_other(*quarters):
    return [*quarters, *(lax.ppermute(w, "tp", CORE_SWAP) for w in quarters)]


def both_quarters(own, after, late):
    held, _ = lax.optimization_barrier((own, after))
    partner = lax.ppermute(held, "grp", WEIGHT_SWAP)
    here, *_ = lax.optimization_barrier((partner, *late))
    return [
        own,
        partner,
        lax.ppermute(own, "tp", CORE_SWAP),
        lax.ppermute(here, "tp", CORE_SWAP),
    ]


def rows_at(prompt, dc, qi):
    start = ((prompt * 2 + dc) * 2 + qi) * QUARTER
    return slice(start, start + QUARTER)


def share(where, tall, keep, send):
    g = where[4]
    for dc in range(2):
        for qi in range(2):
            keep[rows_at(0, dc, qi), :] = tall[dc, g ^ (2 * qi)]
            send[rows_at(0, dc, qi), :] = tall[dc, (g ^ 1) ^ (2 * qi)]


def init_body(where, hidden, mine, theirs):
    c = where[3]
    mine[...] = hidden[0, half_lanes(c), :].astype(F32).T.astype(BF)
    theirs[...] = hidden[0, half_lanes(1 - c), :].astype(F32).T.astype(BF)


def spread_body(where, own, other, keep, send, third, fourth, tall):
    g = where[4]
    tall[0] = own[...].reshape(GRP, QUARTER, PART)
    tall[1] = other[...].reshape(GRP, QUARTER, PART)
    share(where, tall, keep, send)
    for dc in range(2):
        third[dc * QUARTER : (dc + 1) * QUARTER, :] = tall[dc, g ^ 2]
        fourth[dc * QUARTER : (dc + 1) * QUARTER, :] = tall[dc, g ^ 3]


def emit_block(layer, where, values, columns, block):
    g = where[4]
    sums = []
    for prompt in range(2):
        squares = jnp.zeros((QUARTER, PART), F32)
        for dc in range(2):
            for qi in range(2):
                rows = rows_at(prompt, dc, qi)
                start = pl.multiple_of((g ^ (2 * qi)) * QUARTER, QUARTER)
                lane = 4 * dc + layer
                gain = columns[pl.ds(start, QUARTER), lane : lane + 1]
                value = values[rows]
                block[rows, :] = (value * gain).astype(BF)
                squares = squares + value * value
        ss = jnp.sum(squares, axis=0, keepdims=True)
        sums += [p.astype(F32) for p in split3(jnp.broadcast_to(ss, (8, PART)))]
    tile = jnp.concatenate([p[0:1] for p in sums] + [jnp.zeros((10, PART), F32)], axis=0)
    block[ROWS:, :] = tile.astype(BF)


def join_body(where, keep, came, third, fourth, columns, x, block):
    x[: ROWS // 2, :] = keep[...]
    x[ROWS // 2 :, :] = came[...]
    sums = []
    for prompt in range(GRP):
        squares = jnp.zeros((QUARTER, PART), F32)
        for dc in range(2):
            start = pl.multiple_of(where[4] * QUARTER, QUARTER)
            gain = columns[pl.ds(start, QUARTER), 4 * dc : 4 * dc + 1]
            if prompt < 2:
                value = x[rows_at(prompt, dc, 0), :].astype(F32)
            else:
                rows = slice(dc * QUARTER, (dc + 1) * QUARTER)
                value = (third, fourth)[prompt - 2][rows, :].astype(F32)
            at = (2 * prompt + dc) * QUARTER
            block[at : at + QUARTER, :] = (value * gain).astype(BF)
            squares = squares + value * value
        ss = jnp.sum(squares, axis=0, keepdims=True)
        sums += [p.astype(F32) for p in split3(jnp.broadcast_to(ss, (8, PART)))]
    tile = jnp.concatenate([p[0:1] for p in sums] + [jnp.zeros((4, PART), F32)], axis=0)
    block[ROWS:, :] = tile.astype(BF)


def gather(block, early=None):
    other = lax.ppermute(block, "tp", Z_SWAP)
    if early is not None:
        other, early = lax.optimization_barrier((other, early))
    both = jnp.stack([block, other])
    up = lax.ppermute(both, "tp", FIRST[1])
    across = lax.ppermute(both, "tp", FIRST[2])
    down = lax.ppermute(both, "tp", FIRST[3])
    low, high = jnp.stack([both, up]), jnp.stack([across, down])
    low_up = lax.ppermute(low, "tp", SECOND[1])
    high_down = lax.ppermute(high, "tp", SECOND[3])
    high_up = lax.ppermute(high, "tp", SECOND[1])
    low_down = lax.ppermute(low, "tp", SECOND[3])
    low_across = lax.ppermute(low_up, "tp", SECOND[1])
    high_across = lax.ppermute(high_down, "tp", SECOND[3])
    blocks = (low, high, low_up, high_up, low_across, high_across, low_down, high_down)
    return blocks, both, blocks[2:], early


def arrivals(where, refs):
    x, z, y, c = where[0], where[1], where[2], where[3]
    for second in range(4):
        for first in range(4):
            ref, at = refs[2 * second + first // 2], first % 2
            col = (x + jnp.where(c == 0, first, second)) & 3
            row = (y + jnp.where(c == 0, second, first)) & 3
            for dz in range(2):
                yield (col * 2 + (z ^ dz)) * 4 + row, ref, at, dz


def block_rows(where, pair, dc):
    start = (2 * pair + (where[3] ^ dc)) * QUARTER
    return pl.ds(pl.multiple_of(start, QUARTER), QUARTER)


def place(where, blocks, placed):
    ss = [jnp.zeros((1, PART), F32) for _ in range(2)]
    for pair, ref, at, dz in arrivals(where, blocks):
        for prompt in range(2):
            lanes = slice(prompt * PART, (prompt + 1) * PART)
            for dc in range(2):
                for qi in range(2):
                    placed[qi, block_rows(where, pair, dc), lanes] = ref[
                        at, dz, rows_at(prompt, dc, qi), :
                    ]
        if ref.shape[2] > ROWS:
            sums = ref[at, dz, ROWS : ROWS + 16, :].astype(F32)
            for i in range(6):
                ss[i // 3] = ss[i // 3] + sums[i : i + 1]
    return ss


def pack_ss(ss):
    parts = [p.astype(F32) for p in split3(jnp.broadcast_to(ss, (16, ss.shape[1])))]
    row = lax.broadcasted_iota(jnp.int32, parts[0].shape, 0)
    out = jnp.zeros(parts[0].shape, F32)
    for i, part in enumerate(parts):
        out = jnp.where(row == i, part, out)
    return out.astype(BF)


def unpack_ss(rows):
    rows = rows.astype(F32)
    return rows[0:1] + rows[1:2] + rows[2:3]


def rotated(value, cosine, sine):
    first, second = value[:64], value[64:]
    return jnp.concatenate(
        [first * cosine - second * sine, second * cosine + first * sine], axis=0
    ).astype(BF)


def partial_in_body(where, *refs):
    blocks, parts = refs[0:8], refs[8:12]
    keep, send, weight, placed = refs[12:]
    ss = place(where, blocks, placed)
    out = jnp.zeros((2 * IN, 2 * PART), F32)
    for qi in range(2):
        for dc in range(2):
            weight[qi, dc * IN : (dc + 1) * IN, :] = parts[2 * dc + qi][...]
        out = out + jnp.dot(weight[qi], placed[qi], preferred_element_type=F32)
    keep[0 : 2 * IN, :] = out[:, :PART]
    keep[2 * IN :, :] = jnp.broadcast_to(ss[0], (8, PART))
    send[0 : 2 * IN, :] = out[:, PART:].astype(BF)
    send[2 * IN :, :] = pack_ss(ss[1])


def first_in_body(where, *refs):
    blocks, own, other = refs[0:8], refs[8], refs[9]
    keep, sends, (weight, placed) = refs[10], refs[11:14], refs[14:]
    weight[:IN, :] = own[...]
    weight[IN:, :] = other[...]
    ss = [jnp.zeros((1, PART), F32) for _ in range(GRP)]
    for pair, ref, at, dz in arrivals(where, blocks):
        sums = ref[at, dz, ROWS : ROWS + 16, :].astype(F32)
        for prompt in range(GRP):
            lanes = slice(prompt * PART, (prompt + 1) * PART)
            for dc in range(2):
                start = (2 * prompt + dc) * QUARTER
                placed[block_rows(where, pair, dc), lanes] = ref[
                    at, dz, start : start + QUARTER, :
                ]
            for i in range(3):
                ss[prompt] = ss[prompt] + sums[3 * prompt + i : 3 * prompt + i + 1]
    out = jnp.dot(weight[...], placed[...], preferred_element_type=F32)
    keep[0 : 2 * IN, :] = out[:, :PART]
    keep[2 * IN :, :] = jnp.broadcast_to(ss[0], (8, PART))
    for k, send in enumerate(sends, start=1):
        send[0 : 2 * IN, :] = out[:, k * PART : (k + 1) * PART].astype(BF)
        send[2 * IN :, :] = pack_ss(ss[k])


def finish(where, rows, scale, columns, layer, bias, cosine, sine, q, kv):
    c = where[3]
    half = half_lanes(c)
    cos, sin = cosine[:, half], sine[:, half]
    for dc in range(2):
        base = dc * IN
        lane = 4 * dc + 2 + layer
        value = rows[base : base + HD] * scale + columns[:, lane : lane + 1]
        q[:, dc * PART : (dc + 1) * PART] = rotated(value, cos, sin)
        column = bias[dc][0, :, 0:1].astype(F32)
        value = rows[base + HD : base + IN] * scale + column
        kv[c if dc == 0 else 1 - c] = value.astype(BF)


def reduced_in_body(layer, where, keep, *refs):
    came, (columns, bias, other_bias, cosine, sine, q, kv) = refs[:-7], refs[-7:]
    rows = keep[...]
    sums, ss = rows[: 2 * IN], rows[2 * IN : 2 * IN + 1]
    for ref in came:
        sums = sums + ref[0 : 2 * IN, :].astype(F32)
        ss = ss + unpack_ss(ref[2 * IN :, :])
    scale = lax.rsqrt(ss / D + 1e-06)
    finish(where, sums, scale, columns, layer, (bias, other_bias), cosine, sine, q, kv)


def attend_body(
    where, length, q, own, other, cosine, sine, keep, send, raw, keys, vals, tall
):
    y, c = where[2], where[3]
    for ref, half in ((own, half_lanes(c)), (other, half_lanes(1 - c))):
        for i in range(4):
            rows = slice(i * QUARTER, (i + 1) * QUARTER)
            slot = (i - y) & 3
            raw[rows, half] = ref[slot, 0]
            vals[rows, half] = ref[slot, 1]
    keys[...] = rotated(raw[...].astype(F32), cosine[...], sine[...])
    scores = lax.dot_general(
        keys[...], q[...], (((0,), (0,)), ((), ())), preferred_element_type=F32
    ) / jnp.sqrt(jnp.float32(HD))
    s_at = lax.broadcasted_iota(jnp.int32, (TOK, TOK), 0)
    t_at = (lax.broadcasted_iota(jnp.int32, (TOK, TOK), 1) & (PART - 1)) + c * PART
    allowed = (s_at <= t_at) & (s_at < length[0])
    scores = jnp.where(allowed, scores, -1e30)
    weights = jnp.exp(scores - jnp.max(scores, axis=0, keepdims=True))
    probs = (weights / jnp.sum(weights, axis=0, keepdims=True)).astype(BF)
    attended = jnp.dot(vals[...], probs, preferred_element_type=F32).astype(BF)
    for dc in range(2):
        part = attended[:, dc * PART : (dc + 1) * PART]
        tall[dc] = part.reshape(GRP, QUARTER, PART)
    share(where, tall, keep, send)


def multiply_out(where, blocks, parts, weight, placed, total):
    place(where, blocks, placed)
    out = jnp.zeros((ROWS, 2 * PART), F32)
    for qi in range(2):
        for dc in range(2):
            weight[qi, dc * HD : (dc + 1) * HD, :] = parts[2 * dc + qi][...]
        out = out + jnp.dot(weight[qi], placed[qi], preferred_element_type=F32)
    total[...] = out


def partial_out_body(where, *refs):
    blocks, parts = refs[0:8], refs[8:12]
    keep, send, weight, placed, total = refs[12:]
    g = where[4]
    multiply_out(where, blocks, parts, weight, placed, total)
    for prompt in range(2):
        lanes = slice(prompt * PART, (prompt + 1) * PART)
        for dc in range(2):
            for qi in range(2):
                here = pl.multiple_of(dc * HD + (g ^ (2 * qi)) * QUARTER, QUARTER)
                there = pl.multiple_of(dc * HD + ((g ^ 1) ^ (2 * qi)) * QUARTER, QUARTER)
                keep[rows_at(prompt, dc, qi), :] = total[pl.ds(here, QUARTER), lanes]
                sent = total[pl.ds(there, QUARTER), lanes].astype(BF)
                send[rows_at(1 - prompt, dc, qi), :] = sent


def advance_body(layer, where, x, keep, came, columns, new, block):
    value = x[...].astype(F32) + (keep[...] + came[...].astype(F32))
    new[...] = value.astype(BF)
    emit_block(layer, where, new[...].astype(F32), columns, block)


def last_out_body(where, *refs):
    blocks, parts, x = refs[0:8], refs[8:12], refs[12]
    keep, send, weight, placed, total = refs[13:]
    multiply_out(where, blocks, parts, weight, placed, total)
    keep[...] = total[:, :PART]
    send[:ROWS, :] = total[:, PART:].astype(BF)
    send[ROWS:, :] = x[ROWS // 2 :, :]


def total_body(where, x, keep, came, mine, theirs, tall):
    g = where[4]
    for dc in range(2):
        for qi in range(2):
            tall[dc, g ^ (2 * qi)] = x[rows_at(0, dc, qi), :]
            at = rows_at(0, dc, qi)
            tall[dc, (g ^ 1) ^ (2 * qi)] = came[ROWS + at.start : ROWS + at.stop, :]
    for dc, out in enumerate((mine, theirs)):
        rows = slice(dc * HD, (dc + 1) * HD)
        mixed = keep[rows, :] + came[rows, :].astype(F32)
        out[...] = (tall[dc].reshape(HD, PART).astype(F32) + mixed).astype(BF)


def final_body(where, mine, theirs, out):
    c = where[3]
    out[0, half_lanes(c), :] = mine[...].astype(F32).T.astype(BF)
    out[0, half_lanes(1 - c), :] = theirs[...].astype(F32).T.astype(BF)


def local(hidden, lengths, norm_gain, q_weight, q_bias, kv_weight, kv_bias, out_weight):
    tp = lax.axis_index("tp").astype(jnp.int32)
    g = lax.axis_index("grp").astype(jnp.int32)
    where = jnp.stack([tp // 16, (tp // 8) % 2, (tp // 2) % 4, tp % 2, g, g, g, g])

    tile = shape((HD, PART))
    quarters = pltpu.VMEM((2, GRP, QUARTER, PART), BF)
    x_own, theirs = call(init_body, [tile, tile], where, hidden, specs=[SM, VM])
    x_other = lax.ppermute(theirs, "tp", CORE_SWAP)
    lines = jnp.concatenate([norm_gain, q_bias.astype(F32)])
    columns = jnp.concatenate([lines, lax.ppermute(lines, "tp", CORE_SWAP)]).T
    part = shape((2 * QUARTER, PART))
    keep, *sends = call(
        spread_body,
        [tile, tile, part, part],
        where,
        x_own,
        x_other,
        specs=[SM, VM, VM],
        scratch=[quarters],
    )
    x, block = call(
        join_body,
        [shape((ROWS, PART)), shape((ROWS + 16, PART))],
        where,
        keep,
        *(lax.ppermute(sends[k - 1], "grp", G_XOR[k]) for k in (1, 2, 3)),
        columns,
        specs=[SM] + [VM] * 5,
    )

    kv_turned = call(
        turn_kv_body, shape((LAYERS, QUARTER, DEPTH + HD)), kv_weight, kv_bias.T
    )
    kv_own = lax.ppermute(kv_turned, "tp", KV_MOVE)
    q_turned = turn(q_weight)
    out_turned = turn(out_weight)

    inv = 1.0 / 1000000.0 ** (jnp.arange(HD // 2, dtype=F32) * 2.0 / HD)
    angle = inv[:, None] * jnp.arange(TOK, dtype=F32)[None, :]
    cosine, sine = jnp.cos(angle), jnp.sin(angle)

    for layer in range(LAYERS):
        if layer == 0:
            blocks, _, _, kv_own = gather(block, kv_own)
            bias = kv_own[:, :, DEPTH:]
            biases = (bias, lax.ppermute(bias, "tp", CORE_SWAP))
            bundles = [bundle(i, q_turned[i], kv_own) for i in range(LAYERS)]
            keep, *sends = call(
                first_in_body,
                [shape((2 * IN + 8, PART), F32)] + [shape((2 * IN + 16, PART))] * 3,
                where,
                *blocks,
                *with_other(bundles[0]),
                specs=[SM] + [VM] * 10,
                scratch=[pltpu.VMEM((2 * IN, DEPTH), BF), pltpu.VMEM((DEPTH, WIDE), BF)],
            )
        else:
            blocks, both, late, _ = gather(block)
            wide = both_quarters(bundles[layer], both, late)
            keep, *sends = call(
                partial_in_body,
                [shape((2 * IN + 8, PART), F32), shape((2 * IN + 16, PART))],
                where,
                *blocks,
                *wide,
                specs=[SM] + [VM] * 12,
                scratch=[
                    pltpu.VMEM((2, 2 * IN, DEPTH), BF),
                    pltpu.VMEM((2, DEPTH, 2 * PART), BF),
                ],
            )
        came = [lax.ppermute(send, "grp", G_XOR[k]) for k, send in enumerate(sends, start=1)]
        bias = of_layer(layer, QUARTER, HD)
        q, kv = call(
            functools.partial(reduced_in_body, layer),
            [shape((HD, 2 * PART)), shape((2, QUARTER, PART))],
            where,
            keep,
            *came,
            columns,
            *biases,
            cosine,
            sine,
            specs=[SM] + [VM] * (2 + len(came)) + [bias, bias, VM, VM],
        )
        kvs = jnp.stack([kv] + [lax.ppermute(kv, "tp", Y_SLOT[s]) for s in (1, 2, 3)])
        keep, send = call(
            attend_body,
            [tile, tile],
            where,
            lengths,
            q,
            kvs,
            lax.ppermute(kvs, "tp", CORE_SWAP),
            cosine,
            sine,
            specs=[SM, SM] + [VM] * 5,
            scratch=[pltpu.VMEM((HD, TOK), BF)] * 3 + [quarters],
        )
        block = jnp.concatenate([keep, lax.ppermute(send, "grp", WORK_SWAP)])
        blocks, both, late, _ = gather(block)
        wide = both_quarters(out_turned[layer], both, late)
        scratch = [
            pltpu.VMEM((2, ROWS, DEPTH), BF),
            pltpu.VMEM((2, DEPTH, 2 * PART), BF),
            pltpu.VMEM((ROWS, 2 * PART), F32),
        ]
        if layer < LAYERS - 1:
            keep, send = call(
                partial_out_body,
                [shape((ROWS, PART), F32), shape((ROWS, PART))],
                where,
                *blocks,
                *wide,
                specs=[SM] + [VM] * 12,
                scratch=scratch,
            )
            x, block = call(
                functools.partial(advance_body, layer + 1),
                [shape((ROWS, PART)), shape((ROWS + 16, PART))],
                where,
                x,
                keep,
                lax.ppermute(send, "grp", WORK_SWAP),
                columns,
                specs=[SM] + [VM] * 4,
            )
    keep, send = call(
        last_out_body,
        [shape((ROWS, PART), F32), shape((ROWS + HD, PART))],
        where,
        *blocks,
        *wide,
        x,
        specs=[SM] + [VM] * 13,
        scratch=scratch,
    )
    mine, theirs = call(
        total_body,
        [tile, tile],
        where,
        x,
        keep,
        lax.ppermute(send, "grp", WORK_SWAP),
        specs=[SM] + [VM] * 3,
        scratch=[quarters],
    )
    theirs = lax.ppermute(theirs, "tp", CORE_SWAP)
    return call(final_body, shape((1, TOK, HD)), where, mine, theirs, specs=[SM, VM, VM])


def solution(mesh):
    placed = (
        P("grp", None, "tp"),
        P("grp"),
        P(None, "tp"),
        P(None, None, "grp", "tp"),
        P(None, "tp"),
        P(None, None, "grp", "tp"),
        P(None, "tp"),
        P(None, None, "grp", "tp"),
    )
    return jax.shard_map(
        local, mesh=mesh, in_specs=placed, out_specs=P("grp", None, "tp"), check_vma=False
    )
```

```python
import functools

import jax
import jax.numpy as jnp
from jax import lax
from jax.experimental import pallas as pl
from jax.experimental.pallas import tpu as pltpu
from jax.sharding import PartitionSpec as P

D = 8192
HD = 128
LAYERS = 2
TOK = 256
GRP = 4
QUARTER = HD // GRP
PART = TOK // 2
WIDE = GRP * PART
DEPTH = 64 * QUARTER
IN = HD + QUARTER
ROWS = 2 * HD
BF = jnp.bfloat16
F32 = jnp.float32

VM = pl.BlockSpec(memory_space=pltpu.VMEM)
SM = pl.BlockSpec(memory_space=pltpu.SMEM)
ANY = pl.BlockSpec(memory_space=pl.ANY)
PARAMS = pltpu.CompilerParams(vmem_limit_bytes=40 * 1024 * 1024)


def tp_index(x, z, y, c):
    return ((x * 2 + z) * 4 + y) * 2 + c


COORDS = [
    (x, z, y, c) for x in range(4) for z in range(2) for y in range(4) for c in range(2)
]


def tp_perm(move):
    return [(tp_index(*at), tp_index(*move(*at))) for at in COORDS]


def along(x_first, s):
    def move(x, z, y, c):
        if (c == 0) == x_first:
            return ((x - s) % 4, z, y, c)
        return (x, z, (y - s) % 4, c)

    return tp_perm(move)


CORE_SWAP = tp_perm(lambda x, z, y, c: (x, z, y, 1 - c))
Z_SWAP = tp_perm(lambda x, z, y, c: (x, 1 - z, y, c))
FIRST = [along(True, s) for s in range(4)]
SECOND = [along(False, s) for s in range(4)]
Y_SLOT = [tp_perm(lambda x, z, y, c, s=s: (x, z, (y - s) % 4, c)) for s in range(4)]
G_XOR = [[(g, g ^ k) for g in range(GRP)] for k in range(GRP)]
WORK_SWAP, WEIGHT_SWAP = G_XOR[1], G_XOR[2]
KV_MOVE = [(m, 8 * ((m % 32) // 4) + 2 * (m % 4) + m // 32) for m in range(64)]


def split3(value):
    high = value.astype(BF)
    rest = value - high.astype(F32)
    middle = rest.astype(BF)
    low = (rest - middle.astype(F32)).astype(BF)
    return high, middle, low


def call(body, outs, *args, specs=None, scratch=()):
    return pl.pallas_call(
        body,
        grid=(1,),
        out_shape=outs,
        in_specs=specs or [VM] * len(args),
        out_specs=jax.tree.map(lambda _: VM, outs),
        scratch_shapes=list(scratch),
        compiler_params=PARAMS,
        cost_estimate=pl.CostEstimate(flops=0, bytes_accessed=1 << 10, transcendentals=0),
    )(*args)


def shape(dims, dtype=BF):
    return jax.ShapeDtypeStruct(dims, dtype)


def half_lanes(index):
    return pl.ds(pl.multiple_of(index * PART, PART), PART)


def pack_ss(ss):
    parts = [p.astype(F32) for p in split3(jnp.broadcast_to(ss, (16, ss.shape[1])))]
    row = lax.broadcasted_iota(jnp.int32, parts[0].shape, 0)
    out = jnp.zeros(parts[0].shape, F32)
    for i, part in enumerate(parts):
        out = jnp.where(row == i, part, out)
    return out.astype(BF)


def unpack_ss(rows):
    rows = rows.astype(F32)
    return rows[0:1] + rows[1:2] + rows[2:3]


def rotated(value, cosine, sine):
    first, second = value[:64], value[64:]
    return jnp.concatenate(
        [first * cosine - second * sine, second * cosine + first * sine], axis=0
    ).astype(BF)


def turn_body(weight, first, second):
    for layer, out in enumerate((first, second)):
        out[...] = weight[layer].reshape(DEPTH, HD).T


def turn(weight):
    return call(turn_body, [shape((HD, DEPTH))] * 2, weight)


def turn_kv_body(weight, bias, out):
    for layer in range(LAYERS):
        out[layer, :, :DEPTH] = weight[layer].reshape(DEPTH, QUARTER).T
        out[layer, :, DEPTH:] = jnp.broadcast_to(bias[:, layer : layer + 1], (QUARTER, HD))


def of_layer(layer, rows, depth, at=0):
    return pl.BlockSpec((1, rows, depth), lambda i: (layer, 0, at))


def bundle_body(wide, narrow, out):
    out[:HD, :] = wide[...]
    out[HD:, :] = narrow[0, :, :DEPTH]


def bundle(layer, wide, narrow):
    return call(
        bundle_body,
        shape((IN, DEPTH)),
        wide,
        narrow,
        specs=[VM, of_layer(layer, QUARTER, DEPTH + HD)],
    )


def with_other(*quarters):
    return [*quarters, *(lax.ppermute(w, "tp", CORE_SWAP) for w in quarters)]


def both_quarters(own, after, late):
    held, _ = lax.optimization_barrier((own, after))
    partner = lax.ppermute(held, "grp", WEIGHT_SWAP)
    here, *_ = lax.optimization_barrier((partner, *late))
    return [
        own,
        partner,
        lax.ppermute(own, "tp", CORE_SWAP),
        lax.ppermute(here, "tp", CORE_SWAP),
    ]


def rows_at(prompt, dc, qi):
    start = ((prompt * 2 + dc) * 2 + qi) * QUARTER
    return slice(start, start + QUARTER)


def share(where, tall, keep, send):
    g = where[4]
    for dc in range(2):
        for qi in range(2):
            keep[rows_at(0, dc, qi), :] = tall[dc, g ^ (2 * qi)]
            send[rows_at(0, dc, qi), :] = tall[dc, (g ^ 1) ^ (2 * qi)]


def init_body(where, hidden, mine, theirs):
    c = where[3]
    mine[...] = hidden[0, half_lanes(c), :].astype(F32).T.astype(BF)
    theirs[...] = hidden[0, half_lanes(1 - c), :].astype(F32).T.astype(BF)


def spread_body(where, own, other, keep, send, third, fourth, tall):
    g = where[4]
    tall[0] = own[...].reshape(GRP, QUARTER, PART)
    tall[1] = other[...].reshape(GRP, QUARTER, PART)
    share(where, tall, keep, send)
    for dc in range(2):
        third[dc * QUARTER : (dc + 1) * QUARTER, :] = tall[dc, g ^ 2]
        fourth[dc * QUARTER : (dc + 1) * QUARTER, :] = tall[dc, g ^ 3]


def emit_block(layer, where, values, columns, block):
    g = where[4]
    sums = []
    for prompt in range(2):
        squares = jnp.zeros((QUARTER, PART), F32)
        for dc in range(2):
            for qi in range(2):
                rows = rows_at(prompt, dc, qi)
                start = pl.multiple_of((g ^ (2 * qi)) * QUARTER, QUARTER)
                lane = 4 * dc + layer
                gain = columns[pl.ds(start, QUARTER), lane : lane + 1]
                value = values[rows]
                block[rows, :] = (value * gain).astype(BF)
                squares = squares + value * value
        ss = jnp.sum(squares, axis=0, keepdims=True)
        sums += [p.astype(F32) for p in split3(jnp.broadcast_to(ss, (8, PART)))]
    tile = jnp.concatenate([p[0:1] for p in sums] + [jnp.zeros((10, PART), F32)], axis=0)
    block[ROWS:, :] = tile.astype(BF)


def join_body(where, keep, came, third, fourth, columns, x, block):
    x[: ROWS // 2, :] = keep[...]
    x[ROWS // 2 :, :] = came[...]
    sums = []
    for prompt in range(GRP):
        squares = jnp.zeros((QUARTER, PART), F32)
        for dc in range(2):
            start = pl.multiple_of(where[4] * QUARTER, QUARTER)
            gain = columns[pl.ds(start, QUARTER), 4 * dc : 4 * dc + 1]
            if prompt < 2:
                value = x[rows_at(prompt, dc, 0), :].astype(F32)
            else:
                rows = slice(dc * QUARTER, (dc + 1) * QUARTER)
                value = (third, fourth)[prompt - 2][rows, :].astype(F32)
            at = (2 * prompt + dc) * QUARTER
            block[at : at + QUARTER, :] = (value * gain).astype(BF)
            squares = squares + value * value
        ss = jnp.sum(squares, axis=0, keepdims=True)
        sums += [p.astype(F32) for p in split3(jnp.broadcast_to(ss, (8, PART)))]
    tile = jnp.concatenate([p[0:1] for p in sums] + [jnp.zeros((4, PART), F32)], axis=0)
    block[ROWS:, :] = tile.astype(BF)


def gather(block, early=None):
    other = lax.ppermute(block, "tp", Z_SWAP)
    if early is not None:
        other, early = lax.optimization_barrier((other, early))
    both = jnp.stack([block, other])
    up = lax.ppermute(both, "tp", FIRST[1])
    across = lax.ppermute(both, "tp", FIRST[2])
    down = lax.ppermute(both, "tp", FIRST[3])
    low, high = jnp.stack([both, up]), jnp.stack([across, down])
    low_up = lax.ppermute(low, "tp", SECOND[1])
    high_down = lax.ppermute(high, "tp", SECOND[3])
    high_up = lax.ppermute(high, "tp", SECOND[1])
    low_down = lax.ppermute(low, "tp", SECOND[3])
    low_across = lax.ppermute(low_up, "tp", SECOND[1])
    high_across = lax.ppermute(high_down, "tp", SECOND[3])
    blocks = (low, high, low_up, high_up, low_across, high_across, low_down, high_down)
    return blocks, both, blocks[2:], early


def arrivals(where, refs):
    x, z, y, c = where[0], where[1], where[2], where[3]
    for second in range(4):
        for first in range(4):
            ref, at = refs[2 * second + first // 2], first % 2
            col = (x + jnp.where(c == 0, first, second)) & 3
            row = (y + jnp.where(c == 0, second, first)) & 3
            for dz in range(2):
                yield (col * 2 + (z ^ dz)) * 4 + row, ref, at, dz


def block_rows(where, pair, dc):
    start = (2 * pair + (where[3] ^ dc)) * QUARTER
    return pl.ds(pl.multiple_of(start, QUARTER), QUARTER)


def place(where, blocks, placed):
    ss = [jnp.zeros((1, PART), F32) for _ in range(2)]
    for pair, ref, at, dz in arrivals(where, blocks):
        for prompt in range(2):
            lanes = slice(prompt * PART, (prompt + 1) * PART)
            for dc in range(2):
                for qi in range(2):
                    placed[qi, block_rows(where, pair, dc), lanes] = ref[
                        at, dz, rows_at(prompt, dc, qi), :
                    ]
        if ref.shape[2] > ROWS:
            sums = ref[at, dz, ROWS : ROWS + 16, :].astype(F32)
            for i in range(6):
                ss[i // 3] = ss[i // 3] + sums[i : i + 1]
    return ss


def pack_ss(ss):
    parts = [p.astype(F32) for p in split3(jnp.broadcast_to(ss, (16, ss.shape[1])))]
    row = lax.broadcasted_iota(jnp.int32, parts[0].shape, 0)
    out = jnp.zeros(parts[0].shape, F32)
    for i, part in enumerate(parts):
        out = jnp.where(row == i, part, out)
    return out.astype(BF)


def unpack_ss(rows):
    rows = rows.astype(F32)
    return rows[0:1] + rows[1:2] + rows[2:3]


def rotated(value, cosine, sine):
    first, second = value[:64], value[64:]
    return jnp.concatenate(
        [first * cosine - second * sine, second * cosine + first * sine], axis=0
    ).astype(BF)


def partial_in_body(where, *refs):
    blocks, parts = refs[0:8], refs[8:12]
    keep, send, weight, placed = refs[12:]
    ss = place(where, blocks, placed)
    out = jnp.zeros((2 * IN, 2 * PART), F32)
    for qi in range(2):
        for dc in range(2):
            weight[qi, dc * IN : (dc + 1) * IN, :] = parts[2 * dc + qi][...]
        out = out + jnp.dot(weight[qi], placed[qi], preferred_element_type=F32)
    keep[0 : 2 * IN, :] = out[:, :PART]
    keep[2 * IN :, :] = jnp.broadcast_to(ss[0], (8, PART))
    send[0 : 2 * IN, :] = out[:, PART:].astype(BF)
    send[2 * IN :, :] = pack_ss(ss[1])


def first_in_body(where, *refs):
    blocks, own, other = refs[0:8], refs[8], refs[9]
    keep, sends, (weight, placed) = refs[10], refs[11:14], refs[14:]
    weight[:IN, :] = own[...]
    weight[IN:, :] = other[...]
    ss = [jnp.zeros((1, PART), F32) for _ in range(GRP)]
    for pair, ref, at, dz in arrivals(where, blocks):
        sums = ref[at, dz, ROWS : ROWS + 16, :].astype(F32)
        for prompt in range(GRP):
            lanes = slice(prompt * PART, (prompt + 1) * PART)
            for dc in range(2):
                start = (2 * prompt + dc) * QUARTER
                placed[block_rows(where, pair, dc), lanes] = ref[
                    at, dz, start : start + QUARTER, :
                ]
            for i in range(3):
                ss[prompt] = ss[prompt] + sums[3 * prompt + i : 3 * prompt + i + 1]
    out = jnp.dot(weight[...], placed[...], preferred_element_type=F32)
    keep[0 : 2 * IN, :] = out[:, :PART]
    keep[2 * IN :, :] = jnp.broadcast_to(ss[0], (8, PART))
    for k, send in enumerate(sends, start=1):
        send[0 : 2 * IN, :] = out[:, k * PART : (k + 1) * PART].astype(BF)
        send[2 * IN :, :] = pack_ss(ss[k])


def finish(where, rows, scale, columns, layer, bias, cosine, sine, q, kv):
    c = where[3]
    half = half_lanes(c)
    cos, sin = cosine[:, half], sine[:, half]
    for dc in range(2):
        base = dc * IN
        lane = 4 * dc + 2 + layer
        value = rows[base : base + HD] * scale + columns[:, lane : lane + 1]
        q[:, dc * PART : (dc + 1) * PART] = rotated(value, cos, sin)
        column = bias[dc][0, :, 0:1].astype(F32)
        value = rows[base + HD : base + IN] * scale + column
        kv[c if dc == 0 else 1 - c] = value.astype(BF)


def reduced_in_body(layer, where, keep, *refs):
    came, (columns, bias, other_bias, cosine, sine, q, kv) = refs[:-7], refs[-7:]
    rows = keep[...]
    sums, ss = rows[: 2 * IN], rows[2 * IN : 2 * IN + 1]
    for ref in came:
        sums = sums + ref[0 : 2 * IN, :].astype(F32)
        ss = ss + unpack_ss(ref[2 * IN :, :])
    scale = lax.rsqrt(ss / D + 1e-06)
    finish(where, sums, scale, columns, layer, (bias, other_bias), cosine, sine, q, kv)


def attend_body(
    where, length, q, own, other, cosine, sine, keep, send, raw, keys, vals, tall
):
    y, c = where[2], where[3]
    for ref, half in ((own, half_lanes(c)), (other, half_lanes(1 - c))):
        for i in range(4):
            rows = slice(i * QUARTER, (i + 1) * QUARTER)
            slot = (i - y) & 3
            raw[rows, half] = ref[slot, 0]
            vals[rows, half] = ref[slot, 1]
    keys[...] = rotated(raw[...].astype(F32), cosine[...], sine[...])
    scores = lax.dot_general(
        keys[...], q[...], (((0,), (0,)), ((), ())), preferred_element_type=F32
    ) / jnp.sqrt(jnp.float32(HD))
    s_at = lax.broadcasted_iota(jnp.int32, (TOK, TOK), 0)
    t_at = (lax.broadcasted_iota(jnp.int32, (TOK, TOK), 1) & (PART - 1)) + c * PART
    allowed = (s_at <= t_at) & (s_at < length[0])
    scores = jnp.where(allowed, scores, -1e30)
    weights = jnp.exp(scores - jnp.max(scores, axis=0, keepdims=True))
    probs = (weights / jnp.sum(weights, axis=0, keepdims=True)).astype(BF)
    attended = jnp.dot(vals[...], probs, preferred_element_type=F32).astype(BF)
    for dc in range(2):
        part = attended[:, dc * PART : (dc + 1) * PART]
        tall[dc] = part.reshape(GRP, QUARTER, PART)
    share(where, tall, keep, send)


def multiply_out(where, blocks, parts, weight, placed, total):
    place(where, blocks, placed)
    out = jnp.zeros((ROWS, 2 * PART), F32)
    for qi in range(2):
        for dc in range(2):
            weight[qi, dc * HD : (dc + 1) * HD, :] = parts[2 * dc + qi][...]
        out = out + jnp.dot(weight[qi], placed[qi], preferred_element_type=F32)
    total[...] = out


def partial_out_body(where, *refs):
    blocks, parts = refs[0:8], refs[8:12]
    keep, send, weight, placed, total = refs[12:]
    g = where[4]
    multiply_out(where, blocks, parts, weight, placed, total)
    for prompt in range(2):
        lanes = slice(prompt * PART, (prompt + 1) * PART)
        for dc in range(2):
            for qi in range(2):
                here = pl.multiple_of(dc * HD + (g ^ (2 * qi)) * QUARTER, QUARTER)
                there = pl.multiple_of(dc * HD + ((g ^ 1) ^ (2 * qi)) * QUARTER, QUARTER)
                keep[rows_at(prompt, dc, qi), :] = total[pl.ds(here, QUARTER), lanes]
                sent = total[pl.ds(there, QUARTER), lanes].astype(BF)
                send[rows_at(1 - prompt, dc, qi), :] = sent


def advance_body(layer, where, x, keep, came, columns, new, block):
    value = x[...].astype(F32) + (keep[...] + came[...].astype(F32))
    new[...] = value.astype(BF)
    emit_block(layer, where, new[...].astype(F32), columns, block)


def last_out_body(where, *refs):
    blocks, parts, x = refs[0:8], refs[8:12], refs[12]
    keep, send, weight, placed, total = refs[13:]
    multiply_out(where, blocks, parts, weight, placed, total)
    keep[...] = total[:, :PART]
    send[:ROWS, :] = total[:, PART:].astype(BF)
    send[ROWS:, :] = x[ROWS // 2 :, :]


def total_body(where, x, keep, came, mine, theirs, tall):
    g = where[4]
    for dc in range(2):
        for qi in range(2):
            tall[dc, g ^ (2 * qi)] = x[rows_at(0, dc, qi), :]
            at = rows_at(0, dc, qi)
            tall[dc, (g ^ 1) ^ (2 * qi)] = came[ROWS + at.start : ROWS + at.stop, :]
    for dc, out in enumerate((mine, theirs)):
        rows = slice(dc * HD, (dc + 1) * HD)
        mixed = keep[rows, :] + came[rows, :].astype(F32)
        out[...] = (tall[dc].reshape(HD, PART).astype(F32) + mixed).astype(BF)


def final_body(where, mine, theirs, out):
    c = where[3]
    out[0, half_lanes(c), :] = mine[...].astype(F32).T.astype(BF)
    out[0, half_lanes(1 - c), :] = theirs[...].astype(F32).T.astype(BF)


def local(hidden, lengths, norm_gain, q_weight, q_bias, kv_weight, kv_bias, out_weight):
    tp = lax.axis_index("tp").astype(jnp.int32)
    g = lax.axis_index("grp").astype(jnp.int32)
    where = jnp.stack([tp // 16, (tp // 8) % 2, (tp // 2) % 4, tp % 2, g, g, g, g])

    tile = shape((HD, PART))
    quarters = pltpu.VMEM((2, GRP, QUARTER, PART), BF)
    x_own, theirs = call(init_body, [tile, tile], where, hidden, specs=[SM, VM])
    x_other = lax.ppermute(theirs, "tp", CORE_SWAP)
    lines = jnp.concatenate([norm_gain, q_bias.astype(F32)])
    columns = jnp.concatenate([lines, lax.ppermute(lines, "tp", CORE_SWAP)]).T
    part = shape((2 * QUARTER, PART))
    keep, *sends = call(
        spread_body,
        [tile, tile, part, part],
        where,
        x_own,
        x_other,
        specs=[SM, VM, VM],
        scratch=[quarters],
    )
    spread = [lax.ppermute(sends[k - 1], "grp", G_XOR[k]) for k in (1, 2, 3)]
    x, block = call(
        join_body,
        [shape((ROWS, PART)), shape((ROWS + 16, PART))],
        where,
        keep,
        *spread,
        columns,
        specs=[SM] + [VM] * 5,
    )

    kv_held, _ = lax.optimization_barrier((kv_weight, spread[1]))
    kv_turned = call(
        turn_kv_body, shape((LAYERS, QUARTER, DEPTH + HD)), kv_held, kv_bias.T
    )
    kv_own = lax.ppermute(kv_turned, "tp", KV_MOVE)
    q_turned = turn(q_weight)
    out_turned = turn(out_weight)

    inv = 1.0 / 1000000.0 ** (jnp.arange(HD // 2, dtype=F32) * 2.0 / HD)
    angle = inv[:, None] * jnp.arange(TOK, dtype=F32)[None, :]
    cosine, sine = jnp.cos(angle), jnp.sin(angle)

    for layer in range(LAYERS):
        if layer == 0:
            blocks, _, _, _ = gather(block)
            bias = kv_own[:, :, DEPTH:]
            biases = (bias, lax.ppermute(bias, "tp", CORE_SWAP))
            bundles = [bundle(i, q_turned[i], kv_own) for i in range(LAYERS)]
            keep, *sends = call(
                first_in_body,
                [shape((2 * IN + 8, PART), F32)] + [shape((2 * IN + 16, PART))] * 3,
                where,
                *blocks,
                *with_other(bundles[0]),
                specs=[SM] + [VM] * 10,
                scratch=[pltpu.VMEM((2 * IN, DEPTH), BF), pltpu.VMEM((DEPTH, WIDE), BF)],
            )
        else:
            blocks, both, late, _ = gather(block)
            wide = both_quarters(bundles[layer], both, late)
            keep, *sends = call(
                partial_in_body,
                [shape((2 * IN + 8, PART), F32), shape((2 * IN + 16, PART))],
                where,
                *blocks,
                *wide,
                specs=[SM] + [VM] * 12,
                scratch=[
                    pltpu.VMEM((2, 2 * IN, DEPTH), BF),
                    pltpu.VMEM((2, DEPTH, 2 * PART), BF),
                ],
            )
        came = [lax.ppermute(send, "grp", G_XOR[k]) for k, send in enumerate(sends, start=1)]
        bias = of_layer(layer, QUARTER, HD)
        q, kv = call(
            functools.partial(reduced_in_body, layer),
            [shape((HD, 2 * PART)), shape((2, QUARTER, PART))],
            where,
            keep,
            *came,
            columns,
            *biases,
            cosine,
            sine,
            specs=[SM] + [VM] * (2 + len(came)) + [bias, bias, VM, VM],
        )
        kvs = jnp.stack([kv] + [lax.ppermute(kv, "tp", Y_SLOT[s]) for s in (1, 2, 3)])
        keep, send = call(
            attend_body,
            [tile, tile],
            where,
            lengths,
            q,
            kvs,
            lax.ppermute(kvs, "tp", CORE_SWAP),
            cosine,
            sine,
            specs=[SM, SM] + [VM] * 5,
            scratch=[pltpu.VMEM((HD, TOK), BF)] * 3 + [quarters],
        )
        block = jnp.concatenate([keep, lax.ppermute(send, "grp", WORK_SWAP)])
        blocks, both, late, _ = gather(block)
        wide = both_quarters(out_turned[layer], both, late)
        scratch = [
            pltpu.VMEM((2, ROWS, DEPTH), BF),
            pltpu.VMEM((2, DEPTH, 2 * PART), BF),
            pltpu.VMEM((ROWS, 2 * PART), F32),
        ]
        if layer < LAYERS - 1:
            keep, send = call(
                partial_out_body,
                [shape((ROWS, PART), F32), shape((ROWS, PART))],
                where,
                *blocks,
                *wide,
                specs=[SM] + [VM] * 12,
                scratch=scratch,
            )
            x, block = call(
                functools.partial(advance_body, layer + 1),
                [shape((ROWS, PART)), shape((ROWS + 16, PART))],
                where,
                x,
                keep,
                lax.ppermute(send, "grp", WORK_SWAP),
                columns,
                specs=[SM] + [VM] * 4,
            )
    keep, send = call(
        last_out_body,
        [shape((ROWS, PART), F32), shape((ROWS + HD, PART))],
        where,
        *blocks,
        *wide,
        x,
        specs=[SM] + [VM] * 13,
        scratch=scratch,
    )
    mine, theirs = call(
        total_body,
        [tile, tile],
        where,
        x,
        keep,
        lax.ppermute(send, "grp", WORK_SWAP),
        specs=[SM] + [VM] * 3,
        scratch=[quarters],
    )
    theirs = lax.ppermute(theirs, "tp", CORE_SWAP)
    return call(final_body, shape((1, TOK, HD)), where, mine, theirs, specs=[SM, VM, VM])


def solution(mesh):
    placed = (
        P("grp", None, "tp"),
        P("grp"),
        P(None, "tp"),
        P(None, None, "grp", "tp"),
        P(None, "tp"),
        P(None, None, "grp", "tp"),
        P(None, "tp"),
        P(None, None, "grp", "tp"),
    )
    return jax.shard_map(
        local, mesh=mesh, in_specs=placed, out_specs=P("grp", None, "tp"), check_vma=False
    )
```
